128 devices in a mesh: inline: 8 (over z_hi, x), xline: 16 (over y, z_lo, core).
Axes of the slice: x: 4, y: 4, z: 4 (z_hi: 2, z_lo: 2; z = z_hi * 2 + z_lo), core: 2. Of those that a mesh axis runs over, the one named last changes fastest.
Arguments:
- base_volume: float32 [128, 256, 256], P('inline', 'xline'), may hold values from -6 to 6
- vintage_traces: float32 [131072, 256], P(('inline', 'xline')), may hold values from -6 to 6
- dest_device: int32 [131072, 1], P(('inline', 'xline')), may hold values from 0 to 127; in each aligned block of 1024 rows (0 to 1023, 1024 to 2047, ...) at most 16 rows name the same one
- dest_slot: int32 [131072], P(('inline', 'xline')), may hold values from 0 to 255
- vintage_id: int32 [131072], P(('inline', 'xline')), may hold values from 0 to 3
- vintage_gains: float32 [4], replicated, may hold values from 0.5 to 2
- dictionary: bfloat16 [512, 512], replicated, may hold values from -0.09375 to 0.09375
Outputs:
- codes: float32 [32, 64, 64, 512], P('inline', 'xline')
- residual: float32 [128, 256, 256], P('inline', 'xline')
The draws below stay inside these ranges and needn't reach their ends.
Inputs may be any that keep to these rules, and one draw needn't show every extreme that they name: `dest_device`: among the traces of one device, no tile is named more than 16 times, a bound that some block reaches.
All inputs are finite; a program needn't handle non-finite values.
Results may differ from the reference program's by a relative error of at most 0.0022.
Values may be sent and summed in bfloat16 or wider, within the bound.
No kernel may reach another device: no remote copies, remote signals or barrier semaphores. Data moves between devices by JAX's collectives and lax.ppermute only.
A program may use at most 64 MiB of HBM per device.

```python
import math
import jax
import jax.numpy as jnp
import numpy as np
from jax import lax

SIDE = 16
NT = 256
ATOMS = 512
PATCH = 8
VT = 1024
NV = 4
CAP = 16
TRACES = 131072
ROWS = 128
COLS = 256
N_INLINE = 8
N_XLINE = 16
DEVICES = 128


def place_ends(array, stream_key, low, largest):
    longest = array.shape.index(max(array.shape))
    spots = []
    for shift in (0, 1):
        where = [jax.random.randint(jax.random.fold_in(stream_key, axis), (), 0, length) for axis, length in enumerate(array.shape)]
        where[longest] = (where[longest] + shift) % array.shape[longest]
        spots.append(tuple(where))
    return array.at[spots[0]].set(low).at[spots[1]].set(largest)


def levels(stream_key, dims, pieces, smallest, largest):
    level = 1.0
    for dim, shards_of in pieces:
        draws = jax.random.uniform(jax.random.fold_in(jax.random.fold_in(stream_key, 6), dim), (shards_of,), jnp.float32, smallest / len(pieces), largest / len(pieces))
        level = level * jnp.repeat(jnp.exp(draws), dims[dim] // shards_of).reshape((-1,) + (1,) * (len(dims) - 1 - dim))
    return level


def assign_block(key, own, number, rows, number_of, top, most, slope):
    order = jax.random.permutation(key, number_of)
    crowded, usual = shares(number_of, rows * top, most, slope, True), shares(number_of, rows * top, most, slope, False)
    places = jnp.arange(number_of)

    def named(lengths, turn):
        used = int((lengths > 0).sum())
        fixed = max(1, used // 4)
        moved = fixed + (places - fixed + turn * (used - fixed)) % max(1, number_of - fixed)
        return jnp.zeros((number_of,), jnp.int32).at[order[jnp.where(places < fixed, places, moved)]].set(jnp.asarray(lengths, jnp.int32))

    lengths = jnp.where(number % 4 == 0, named(crowded, number // 4), named(usual, number - number // 4 - 1))
    mixed = jax.random.permutation(jax.random.fold_in(own, 3), number_of)
    giver, receiver = mixed[0:number_of // 2 * 2:2], mixed[1:number_of // 2 * 2:2]
    margin = jnp.minimum(lengths[giver] - 1, most - lengths[receiver]) // 2
    margin = jnp.where((giver == order[0]) | (receiver == order[0]) | (lengths[receiver] == 0), 0, jnp.maximum(margin, 0))
    moved = jax.random.randint(jax.random.fold_in(own, 4), (number_of // 2,), 0, 1 << 20) % (margin + 1)
    lengths = lengths.at[giver].add(-moved).at[receiver].add(moved)
    members = jnp.searchsorted(jnp.cumsum(lengths), jnp.arange(rows * top), side="right").astype(jnp.int32)
    grid = members.reshape(top, rows).T
    grid = grid[jax.random.permutation(jax.random.fold_in(own, 1), rows)]
    turn = jax.random.randint(jax.random.fold_in(own, 2), (rows, 1), 0, top)
    return jnp.take_along_axis(grid, (jnp.arange(top)[None, :] + turn) % top, axis=1)


def shares(amount, total, bound, slope, full):
    weights = [(1 << 20) // math.isqrt(grade ** slope) + 1 for grade in range(1, amount + 1)]
    largest = bound if full else min(bound, max(-(-total // amount), total * weights[0] // sum(weights)))
    least = 1 if total - largest >= amount - 1 else 0
    counts, rest = [largest] + [least] * (amount - 1), total - largest - least * (amount - 1)
    while rest > 0:
        candidates = [i for i in range(1, amount) if counts[i] < largest] or [i for i in range(1, amount) if counts[i] < bound]
        whole, budget = sum([weights[i] for i in candidates]), rest
        for i in candidates:
            addition = min(bound - counts[i], max(1, budget * weights[i] // whole), rest)
            counts[i] = counts[i] + addition
            rest = rest - addition
    return np.array(counts)


def scatter_about(rng, shape, width, reach, split=(), kind=jnp.bfloat16):
    gain = levels(rng, shape, split, -0.22, 0.18) if split else 1.0
    values = jax.random.normal(rng, shape, jnp.float32) * width * gain
    return jnp.minimum(jnp.maximum(values, -reach), reach).astype(kind)


def setup_inputs(seed: int = 0) -> dict:
    splits = jax.random.split(jax.random.key(seed), 8)
    base_volume = scatter_about(splits[0], (ROWS, COLS, NT), 1.0, 6.0, ((0, 8), (1, 16)), jnp.float32)
    vintage_traces = scatter_about(splits[1], (TRACES, NT), 1.0, 6.0, ((0, 128),), jnp.float32)
    dest_device_keys = jax.random.split(jax.random.fold_in(splits[2], 1), TRACES // VT)
    dest_device_turns = jax.random.permutation(jax.random.fold_in(splits[2], 3), TRACES // VT)
    dest_device = jax.vmap(lambda own, number: assign_block(jax.random.fold_in(splits[2], 2), own, number, VT, DEVICES, 1, CAP, 2))(dest_device_keys, dest_device_turns).reshape((TRACES, 1))
    dest_slot = place_ends(jax.random.randint(splits[3], (TRACES,), 0, SIDE * SIDE), jax.random.fold_in(splits[3], 1), 0, (SIDE * SIDE) - 1).astype(jnp.int32)
    vintage_id = place_ends(jax.random.randint(splits[4], (TRACES,), 0, NV), jax.random.fold_in(splits[4], 1), 0, NV - 1).astype(jnp.int32)
    vintage_gains = jnp.clip(jnp.exp(jax.random.uniform(splits[5], (NV,), jnp.float32, math.log(0.5), math.log(2.0))), 0.5, 2.0)
    dictionary = scatter_about(splits[6], (PATCH * PATCH * PATCH, ATOMS), 4096 ** -0.5, 0.09375)
    return dict(base_volume=base_volume, vintage_traces=vintage_traces, dest_device=dest_device, dest_slot=dest_slot, vintage_id=vintage_id, vintage_gains=vintage_gains, dictionary=dictionary)


step_size = 0.25
threshold = 0.02


def shrink_codes(values):
    return values - jnp.clip(values, -threshold, threshold)


def correlate(field_half, dict_blocks):
    row_count, col_count, time_count = field_half.shape
    patch_i, patch_j, patch_k = row_count // 4, col_count // 4, time_count // 4
    padded = jnp.pad(field_half.astype(jnp.float32), ((0, 4), (0, 4), (0, 4)))
    padded = padded.reshape(patch_i + 1, 4, patch_j + 1, 4, patch_k + 1, 4)
    atom_count = dict_blocks.shape[-1]

    def one_row(row_index):
        row_slab = lax.dynamic_slice_in_dim(padded, row_index, 2, 0)
        running = jnp.zeros((patch_j, patch_k, atom_count), jnp.float32)
        for shift_a in (0, 1):
            for shift_b in (0, 1):
                for shift_c in (0, 1):
                    block_piece = row_slab[shift_a][:, shift_b:shift_b + patch_j, :, shift_c:shift_c + patch_k, :]
                    running = running + jnp.einsum('ajbkc,abcn->jkn', block_piece, dict_blocks[shift_a, :, shift_b, :, shift_c, :, :])
        return running

    return lax.map(one_row, jnp.arange(patch_i, dtype=jnp.int32))


def place_part(contrib, shift_a, patch_j, patch_k):
    output = jnp.zeros((4, patch_j, 4, patch_k, 4), jnp.float32)
    for shift_b in (0, 1):
        for shift_c in (0, 1):
            block_piece = contrib[:, :, shift_a, :, shift_b, :, shift_c, :].transpose(2, 0, 3, 1, 4)
            moved = jnp.pad(block_piece, ((0, 0), (shift_b, 0), (0, 0), (shift_c, 0), (0, 0)))
            output = output + moved[:, :patch_j, :, :patch_k, :]
    return output


def reconstruct(codes_half, dict_float):
    patch_i, patch_j, patch_k, atom_count = codes_half.shape

    def advance(carried, code_row):
        contrib = jnp.einsum('jkn,en->jke', code_row.astype(jnp.float32), dict_float)
        contrib = contrib.reshape(patch_j, patch_k, 2, 4, 2, 4, 2, 4)
        current = place_part(contrib, 0, patch_j, patch_k) + carried
        return place_part(contrib, 1, patch_j, patch_k), current

    start = jnp.zeros((4, patch_j, 4, patch_k, 4), jnp.float32)
    unused, rows_out = lax.scan(advance, start, codes_half)
    return rows_out.reshape(patch_i * 4, patch_j * 4, patch_k * 4)


def reference(base_volume, vintage_traces, dest_device, dest_slot, vintage_id, vintage_gains, dictionary):
    tile_side = base_volume.shape[0] // N_INLINE
    weighted = vintage_gains[vintage_id][:, None] * vintage_traces
    target = dest_device[:, 0]
    row_at = (target // N_XLINE) * tile_side + dest_slot // tile_side
    col_at = (target % N_XLINE) * tile_side + dest_slot % tile_side
    stack = jnp.zeros(base_volume.shape, jnp.float32).at[row_at, col_at].add(weighted)
    fold = jnp.zeros(base_volume.shape[:2], jnp.float32).at[row_at, col_at].add(jnp.float32(1.0))
    merged = (base_volume + stack) / (1.0 + fold)[:, :, None]
    dict_float = dictionary.astype(jnp.float32)
    dict_blocks = dict_float.reshape(2, 4, 2, 4, 2, 4, dict_float.shape[1])
    first = shrink_codes(step_size * correlate(merged.astype(jnp.bfloat16), dict_blocks))
    recon = reconstruct(first.astype(jnp.bfloat16), dict_float)
    residual = merged - recon
    codes = shrink_codes(first + step_size * correlate(residual.astype(jnp.bfloat16), dict_blocks))
    return codes, residual
```

```python
import math

import jax
import jax.numpy as jnp
from jax import lax
from jax.experimental import pallas as pl
from jax.experimental.pallas import tpu as pltpu
from jax.sharding import PartitionSpec as P

step_size = 0.25
threshold = 0.02
octaves = 40.0
code_top = 32767.0
log_top = math.log2(12.0)
vmem_bytes = 48 * 1024 * 1024


def shrink_codes(values):
    return values - jnp.clip(values, -threshold, threshold)


def call_kernel(kernel, out_shape, scratch, smem_inputs, inputs):
    vmem = pl.BlockSpec(memory_space=pltpu.VMEM)
    smem = pl.BlockSpec(memory_space=pltpu.SMEM)
    return pl.pallas_call(
        kernel,
        out_shape=out_shape,
        in_specs=[smem] * len(smem_inputs) + [vmem] * len(inputs),
        out_specs=jax.tree.map(lambda _: vmem, out_shape),
        scratch_shapes=scratch,
        compiler_params=pltpu.CompilerParams(vmem_limit_bytes=vmem_bytes),
    )(*smem_inputs, *inputs)


def encode(values):
    size = jnp.log2(jnp.maximum(jnp.abs(values), 1e-30))
    code = (size + (octaves - log_top)) * (code_top / octaves)
    code = jnp.clip(jnp.round(code), 0.0, code_top).astype(jnp.int32)
    return jnp.where(values < 0, -code, code)


def decode(code):
    code = code.astype(jnp.float32)
    size = jnp.exp2(jnp.abs(code) * (octaves / code_top) + (log_top - octaves))
    return size * jnp.clip(code, -1.0, 1.0)


def pack_kernel(gains, traces, dest, slot, vid, out):
    trace_count = traces.shape[0]
    device_count = out.shape[0]
    chunks = trace_count // 128
    source = lax.rem(lax.axis_index("xline"), 8)
    survey = vid[...]
    gain = jnp.zeros(survey.shape, jnp.float32)
    for number in range(gains.shape[0]):
        gain = jnp.where(survey == number, gains[number], gain)
    gain = jnp.transpose(jnp.broadcast_to(gain, (128, trace_count)))
    high, low = [], []
    for half in range(2):
        code = encode(traces[:, half * 128 : half * 128 + 128] * gain)
        high.append((code >> 8).astype(jnp.float32).astype(jnp.bfloat16))
        low.append((code & 255).astype(jnp.float32).astype(jnp.bfloat16))
    halves = jnp.concatenate(high + low, axis=1)

    row = lax.broadcasted_iota(jnp.int32, (128, 128), 0)
    lane = lax.broadcasted_iota(jnp.int32, (128, 128), 1)
    before = jnp.where(row < lane, 1.0, 0.0).astype(jnp.bfloat16)
    carry = jnp.zeros((device_count, 1), jnp.float32)
    places, owners, listed = [], [], []
    for chunk in range(chunks):
        target = dest[:, chunk * 128 : chunk * 128 + 128]
        hit = jnp.where(row == target, 1.0, 0.0)
        hit_half = hit.astype(jnp.bfloat16)
        earlier = jnp.dot(hit_half, before, preferred_element_type=jnp.float32)
        rank = jnp.sum(hit * (earlier + carry), axis=0, keepdims=True)
        carry = carry + jnp.sum(hit, axis=1, keepdims=True)
        rank = rank.astype(jnp.int32)
        places.append(target * 16 + rank)
        owners.append(hit_half)
        wanted = (slot[:, chunk * 128 : chunk * 128 + 128] + 1).astype(jnp.float32)
        listed.append(jnp.where(row == rank + 16 * source, wanted, 0.0).astype(jnp.bfloat16))
    place = jnp.concatenate(places, axis=1)
    owner = jnp.concatenate(owners, axis=1)
    listing = jnp.concatenate(listed, axis=1)
    slots = lax.dot_general(
        owner, listing, (((1,), (1,)), ((), ())), preferred_element_type=jnp.float32
    )
    slots = slots.astype(jnp.int32)
    out[:, 32:40, :] = jnp.broadcast_to(slots[:, None, :], (device_count, 8, 128)).astype(jnp.int16)
    rows = 256
    index = lax.broadcasted_iota(jnp.int32, (rows, trace_count), 0)
    for block in range(device_count * 16 // rows):
        pick = jnp.where(index == place - block * rows, 1.0, 0.0).astype(jnp.bfloat16)
        moved = jnp.dot(pick, halves, preferred_element_type=jnp.float32)
        code = (moved[:, :256] * 256.0 + moved[:, 256:]).astype(jnp.int32).astype(jnp.int16)
        spot = pl.ds(block * (rows // 16), rows // 16)
        out[spot, 0:16, :] = code[:, :128].reshape(rows // 16, 16, 128)
        out[spot, 16:32, :] = code[:, 128:].reshape(rows // 16, 16, 128)


def merge_kernel(got, base, whole, half, upper, lower, pick, parts, turned):
    groups = got.shape[0] // 8
    bin_row = lax.broadcasted_iota(jnp.int32, (256, 128), 0)
    bin_slot = (
        (bin_row // 64) * 64 + ((bin_row // 4) % 4) * 16 + ((bin_row // 16) % 4) * 4 + bin_row % 4
    )
    wanted = bin_slot + 1
    fold = jnp.zeros((256, 128), jnp.float32)
    for group in range(groups):
        spot = pl.ds(group * 8, 8)
        listed = jnp.sum(got[spot, 32:40, :].astype(jnp.int32), axis=0)
        listed = jnp.broadcast_to(listed[None], (32, 8, 128)).reshape(256, 128)
        hit = jnp.where(listed == wanted, 1.0, 0.0)
        fold = fold + hit
        pick[:, group * 128 : group * 128 + 128] = hit.astype(jnp.bfloat16)
        for side in range(2):
            code = got[spot, side * 16 : side * 16 + 16, :].reshape(128, 128).astype(jnp.int32)
            value = decode(code)
            high = value.astype(jnp.bfloat16)
            low = (value - high.astype(jnp.float32)).astype(jnp.bfloat16)
            parts[group * 128 : group * 128 + 128, side * 128 : side * 128 + 128] = high
            parts[group * 128 : group * 128 + 128, 256 + side * 128 : 384 + side * 128] = low
    stack = jnp.dot(pick[...], parts[...], preferred_element_type=jnp.float32)
    fold = jnp.sum(fold, axis=1, keepdims=True)
    merged = (base[...] + (stack[:, :256] + stack[:, 256:])) / (1.0 + fold)
    turned[0] = jnp.transpose(merged[:128])
    turned[1] = jnp.transpose(merged[128:])
    lane = lax.broadcasted_iota(jnp.int32, (64, 128), 1) // 16
    for tile in range(2):
        slabs = [turned[tile, pl.ds(phase, 64, stride=4), :] for phase in range(4)]
        for part in range(2):
            for pair in range(2):
                made = None
                for odd in range(2):
                    for phase in range(4):
                        shift = (48 * odd + 16 * phase - 64 * part - 32 * pair) % 128
                        piece = slabs[phase] if shift == 0 else pltpu.roll(slabs[phase], shift, 1)
                        made = (
                            piece if made is None else jnp.where(lane == 4 * odd + phase, piece, made)
                        )
                block_row = 2 * tile + part
                whole[block_row, pair] = made
                made = made.astype(jnp.bfloat16)
                half[pair, block_row] = made
                if block_row < 2:
                    upper[pair, block_row] = made
                if block_row == 3:
                    lower[pair, 0] = made


def time_rolled(values, distance):
    row = lax.broadcasted_iota(jnp.int32, values.shape, 0)
    if distance < 0:
        return jnp.where(row == values.shape[0] - 1, 0.0, pltpu.roll(values, values.shape[0] - 1, 0))
    return jnp.where(row == 0, 0.0, pltpu.roll(values, 1, 0))


def widened(both):
    left = lax.broadcasted_iota(jnp.int32, both.shape, 1) < 64
    later = time_rolled(both, -1)
    even = jnp.where(left, both, pltpu.roll(later, 64, 1))
    odd = jnp.where(left, pltpu.roll(both, 64, 1), later)
    return even.astype(jnp.bfloat16), odd.astype(jnp.bfloat16)


def sparse_kernel(
    whole, own, before, after, words, words_back, codes, residual, field, first, recon, tail, turned, binned
):
    inline_at, xline_at = lax.axis_index("inline"), lax.axis_index("xline")
    inline_last = inline_at == lax.axis_size("inline") - 1
    xline_last = xline_at == lax.axis_size("xline") - 1
    not_top = jnp.where(inline_at == 0, 0.0, 1.0)
    not_left = jnp.where(xline_at == 0, 0.0, 1.0)
    not_bottom = jnp.where(inline_last, 0.0, 1.0)
    not_right = jnp.where(xline_last, 0.0, 1.0)

    sources = [before.at[0], own.at[0], own.at[1], after.at[0]]
    for block_row in range(7):
        for pair in range(4):
            even, odd = widened(sources[pair][block_row].astype(jnp.float32))
            if pair > 0:
                field[block_row, 2 * pair - 1] = even
            if pair < 4:
                field[block_row, 2 * pair] = odd

    def correlated(source, patch_row, count):
        lhs = [
            source[patch_row + shift_a, shift_b : shift_b + count].reshape(count * 64, 128)
            for shift_a in (0, 1)
            for shift_b in (0, 1)
        ]
        return jnp.dot(
            jnp.concatenate(lhs, axis=1), words[...], preferred_element_type=jnp.float32
        )

    for patch_row in range(6):
        found = shrink_codes(step_size * correlated(field, patch_row, 6))
        if 1 <= patch_row <= 4:
            first[patch_row - 1] = found[64:320]
        if patch_row == 0:
            found = found * not_top
        found = jnp.concatenate([found[:64] * not_left, found[64:]], axis=0).astype(jnp.bfloat16)
        given = jnp.dot(found, words_back[...], preferred_element_type=jnp.float32)
        given = given.reshape(6, 64, 512)
        if patch_row > 0:
            upper = given[0:5, :, 128:256] + given[1:6, :, 0:128]
            if patch_row == 1:
                recon[0] = tail[...] + upper
            elif patch_row < 6:
                recon[patch_row - 1] = tail[...] + upper
        if patch_row < 5:
            tail[...] = given[0:5, :, 384:512] + given[1:6, :, 256:384]

    left = lax.broadcasted_iota(jnp.int32, (64, 128), 1) < 64
    for block_row in range(5):
        for pair in range(3):
            even = recon[block_row, 2 * pair]
            odd = recon[block_row, 2 * pair + 1] if pair < 2 else even
            near = jnp.where(left, even, pltpu.roll(odd, 64, 1))
            far = jnp.where(left, pltpu.roll(even, 64, 1), odd)
            rebuilt = near + time_rolled(far, 1)
            if block_row < 4 and pair < 2:
                rest = whole[block_row, pair] - rebuilt
                whole_rest = rest
                binned[block_row, pair] = whole_rest
            elif pair < 2:
                rest = (own[pair, 5].astype(jnp.float32) - rebuilt) * not_bottom
            else:
                rest = (after[0, block_row + 1].astype(jnp.float32) - rebuilt) * not_right
                if block_row == 4:
                    rest = rest * not_bottom
            even, odd = widened(rest)
            field[block_row, 2 * pair] = even
            if pair < 2:
                field[block_row, 2 * pair + 1] = odd

    for patch_row in range(4):
        found = first[patch_row] + step_size * correlated(field, patch_row, 4)
        codes[patch_row] = shrink_codes(found).reshape(4, 64, 512)

    lane = lax.broadcasted_iota(jnp.int32, (64, 128), 1) // 16
    for tile in range(2):
        for phase in range(4):
            made = None
            for part in range(2):
                for pair in range(2):
                    for odd in range(2):
                        shift = (64 * part + 32 * pair - 48 * odd - 16 * phase) % 128
                        piece = binned[2 * tile + part, pair]
                        piece = piece if shift == 0 else pltpu.roll(piece, shift, 1)
                        made = (
                            piece
                            if made is None
                            else jnp.where(lane == 4 * part + 2 * pair + odd, piece, made)
                        )
            turned[tile, pl.ds(phase, 64, stride=4), :] = made
    for tile in range(2):
        flat = jnp.transpose(turned[tile])
        for part in range(2):
            for block_col in range(4):
                for row in range(4):
                    at = part * 64 + block_col * 16 + row * 4
                    to = (2 * tile + part) * 64 + row * 16 + block_col * 4
                    residual[to : to + 4, :] = flat[at : at + 4, :]


def body(
    base_volume, vintage_traces, dest_device, dest_slot, vintage_id, vintage_gains, dictionary
):
    trace_count, time_len = vintage_traces.shape
    device_count = lax.axis_size("inline") * lax.axis_size("xline")
    sent = call_kernel(
        pack_kernel,
        jax.ShapeDtypeStruct((device_count, 40, 128), jnp.int16),
        [],
        [vintage_gains],
        [
            vintage_traces,
            dest_device.reshape(1, trace_count),
            dest_slot.reshape(1, trace_count),
            vintage_id.reshape(1, trace_count),
        ],
    )
    got = lax.all_to_all(sent, ("inline", "xline"), split_axis=0, concat_axis=0, tiled=True)
    words = dictionary.reshape(2, 4, 2, 4, 2, 4, 512).transpose(0, 2, 4, 5, 1, 3, 6).reshape(512, 512)
    words_back = words.T
    base = (
        base_volume.reshape(4, 4, 4, 4, time_len).transpose(0, 2, 1, 3, 4).reshape(256, time_len)
    )
    pair_shape = lambda *lead: jax.ShapeDtypeStruct(lead + (64, 128), jnp.bfloat16)
    whole, half, upper, lower = call_kernel(
        merge_kernel,
        (
            jax.ShapeDtypeStruct((4, 2, 64, 128), jnp.float32),
            pair_shape(2, 4),
            pair_shape(2, 2),
            pair_shape(2, 1),
        ),
        [
            pltpu.VMEM((256, device_count * 16), jnp.bfloat16),
            pltpu.VMEM((device_count * 16, 512), jnp.bfloat16),
            pltpu.VMEM((2, 256, 128), jnp.float32),
        ],
        [],
        [got, base],
    )

    def along(block, axis, distance):
        devices = range(lax.axis_size(axis))
        route = [(i - distance, i) for i in devices if i - distance in devices]
        return lax.ppermute(block, axis, route)

    from_below = along(upper, "inline", -1)
    from_above = along(lower, "inline", 1)
    own = jnp.concatenate([from_above, half, from_below], axis=1)
    after = along(own[0:1], "xline", -1)
    before = along(own[1:2], "xline", 1)
    codes, residual = call_kernel(
        sparse_kernel,
        (
            jax.ShapeDtypeStruct((4, 4, 64, 512), jnp.float32),
            jax.ShapeDtypeStruct((256, time_len), jnp.float32),
        ),
        [
            pltpu.VMEM((7, 7, 64, 128), jnp.bfloat16),
            pltpu.VMEM((4, 256, 512), jnp.float32),
            pltpu.VMEM((5, 5, 64, 128), jnp.float32),
            pltpu.VMEM((5, 64, 128), jnp.float32),
            pltpu.VMEM((2, 256, 128), jnp.float32),
            pltpu.VMEM((4, 2, 64, 128), jnp.float32),
        ],
        [],
        [whole, own, before, after, words, words_back],
    )
    return codes, residual.reshape(16, 16, time_len)


def solution(mesh):
    in_specs = (
        P("inline", "xline", None),
        P(("inline", "xline"), None),
        P(("inline", "xline"), None),
        P(("inline", "xline")),
        P(("inline", "xline")),
        P(),
        P(),
    )
    out_specs = (P("inline", "xline", None, None), P("inline", "xline", None))
    return jax.shard_map(body, mesh=mesh, in_specs=in_specs, out_specs=out_specs, check_vma=False)
```

```python
import math

import jax
import jax.numpy as jnp
from jax import lax
from jax.experimental import pallas as pl
from jax.experimental.pallas import tpu as pltpu
from jax.sharding import PartitionSpec as P

step_size = 0.25
threshold = 0.02
octaves = 40.0
code_top = 32767.0
log_top = math.log2(12.0)
vmem_bytes = 48 * 1024 * 1024


def shrink_codes(values):
    return values - jnp.clip(values, -threshold, threshold)


def call_kernel(kernel, out_shape, out_spaces, scratch, in_space, inputs):
    return pl.pallas_call(
        kernel,
        out_shape=out_shape,
        in_specs=[pl.BlockSpec(memory_space=in_space)] * len(inputs),
        out_specs=jax.tree.map(lambda space: pl.BlockSpec(memory_space=space), out_spaces),
        scratch_shapes=scratch,
        compiler_params=pltpu.CompilerParams(vmem_limit_bytes=vmem_bytes),
    )(*inputs)


def encode(values):
    size = jnp.log2(jnp.maximum(jnp.abs(values), 1e-30))
    code = (size + (octaves - log_top)) * (code_top / octaves)
    code = jnp.clip(jnp.round(code), 0.0, code_top).astype(jnp.int32)
    return jnp.where(values < 0, -code, code)


def decode(code):
    code = code.astype(jnp.float32)
    size = jnp.exp2(jnp.abs(code) * (octaves / code_top) + (log_top - octaves))
    return size * jnp.clip(code, -1.0, 1.0)


def pack_kernel(gains_in, traces_in, dest_in, slot_in, vid_in, out, gains, traces, dest, slot, vid, built, arrive, leave):
    loads = [
        pltpu.make_async_copy(source, target, arrive.at[number])
        for number, (source, target) in enumerate(
            ((dest_in, dest), (slot_in, slot), (gains_in, gains), (vid_in, vid), (traces_in, traces))
        )
    ]
    for load in loads:
        load.start()
    trace_count = traces.shape[0]
    device_count = out.shape[0] // 17
    chunks = trace_count // 128
    me = lax.axis_index("inline") * lax.axis_size("xline") + lax.axis_index("xline")
    loads[0].wait()
    loads[1].wait()
    row = lax.broadcasted_iota(jnp.int32, (128, 128), 0)
    lane = lax.broadcasted_iota(jnp.int32, (128, 128), 1)
    before = jnp.where(row < lane, 1.0, 0.0).astype(jnp.bfloat16)
    carry = jnp.zeros((device_count, 1), jnp.float32)
    places, owners, listed = [], [], []
    for chunk in range(chunks):
        target = dest[:, chunk * 128 : chunk * 128 + 128]
        hit = jnp.where(row == target, 1.0, 0.0)
        hit_half = hit.astype(jnp.bfloat16)
        earlier = jnp.dot(hit_half, before, preferred_element_type=jnp.float32)
        rank = jnp.sum(hit * (earlier + carry), axis=0, keepdims=True)
        carry = carry + jnp.sum(hit, axis=1, keepdims=True)
        rank = rank.astype(jnp.int32)
        places.append(target * 17 + rank)
        owners.append(hit_half)
        wanted = (slot[:, chunk * 128 : chunk * 128 + 128] + 1).astype(jnp.float32)
        spot = lax.rem(17 * me + rank, 128)
        listed.append(jnp.where(row == spot, wanted, 0.0).astype(jnp.bfloat16))
    place = jnp.concatenate(places, axis=1)
    owner = jnp.concatenate(owners, axis=1)
    listing = jnp.concatenate(listed, axis=1)
    slots = lax.dot_general(
        owner, listing, (((1,), (1,)), ((), ())), preferred_element_type=jnp.float32
    ).astype(jnp.int32)

    loads[2].wait()
    loads[3].wait()
    survey = vid[...]
    gain = jnp.zeros(survey.shape, jnp.float32)
    for number in range(gains.shape[0]):
        gain = jnp.where(survey == number, gains[number], gain)
    gain = jnp.transpose(jnp.broadcast_to(gain, (128, trace_count)))
    loads[4].wait()
    high, low = [], []
    for half in range(2):
        code = encode(traces[:, half * 128 : half * 128 + 128] * gain)
        high.append((code >> 8).astype(jnp.float32).astype(jnp.bfloat16))
        low.append((code & 255).astype(jnp.float32).astype(jnp.bfloat16))
    halves = jnp.concatenate(high + low, axis=1)

    owners_each = 16
    rows = owners_each * 17
    index = lax.broadcasted_iota(jnp.int32, (rows, trace_count), 0)
    stores = []
    for block in range(device_count // owners_each):
        pick = jnp.where(index == place - block * rows, 1.0, 0.0).astype(jnp.bfloat16)
        moved = jnp.dot(pick, halves, preferred_element_type=jnp.float32)
        code = (moved[:, :256] * 256.0 + moved[:, 256:]).astype(jnp.int32)
        built[block * rows : block * rows + rows, :] = (code[:, :128] << 16) | (
            code[:, 128:] & 65535
        )
        built[pl.ds(block * rows + 16, owners_each, stride=17), :] = slots[
            block * owners_each : block * owners_each + owners_each
        ]
        spot = pl.ds(block * rows, rows)
        stores.append(pltpu.make_async_copy(built.at[spot], out.at[spot], leave.at[block]))
        stores[-1].start()
    for store in stores:
        store.wait()


def merge_kernel(got, base, whole, half, upper, lower, pick, parts, turned):
    tiles = got.shape[0] // 128
    bin_row = lax.broadcasted_iota(jnp.int32, (256, 128), 0)
    bin_slot = (
        (bin_row // 64) * 64 + ((bin_row // 4) % 4) * 16 + ((bin_row // 16) % 4) * 4 + bin_row % 4
    )
    wanted = bin_slot + 1
    listed = got[pl.ds(16, 128, stride=17), :]
    begin = 17 * lax.broadcasted_iota(jnp.int32, (128, 128), 0)
    lane = lax.broadcasted_iota(jnp.int32, (128, 128), 1)
    tile_of = begin // 128 + jnp.where(lane < begin % 128, 1, 0)
    fold = jnp.zeros((256, 128), jnp.float32)
    for tile in range(tiles):
        low_group, high_group = (128 * tile) // 136, min((128 * tile + 127) // 136, 15)
        spot = slice(8 * low_group, 8 * high_group + 8)
        slots = jnp.sum(jnp.where(tile_of[spot] == tile, listed[spot], 0), axis=0, keepdims=True)
        hit = jnp.where(wanted == slots, 1.0, 0.0)
        fold = fold + hit
        spot = slice(128 * tile, 128 * tile + 128)
        pick[:, spot] = hit.astype(jnp.bfloat16)
        word = got[spot, :]
        for side, code in enumerate((word >> 16, (word << 16) >> 16)):
            value = decode(code)
            high = value.astype(jnp.bfloat16)
            low = (value - high.astype(jnp.float32)).astype(jnp.bfloat16)
            parts[spot, side * 128 : side * 128 + 128] = high
            parts[spot, 256 + side * 128 : 384 + side * 128] = low
    stack = jnp.dot(pick[...], parts[...], preferred_element_type=jnp.float32)
    fold = jnp.sum(fold, axis=1, keepdims=True)
    merged = (base[...] + (stack[:, :256] + stack[:, 256:])) / (1.0 + fold)
    turned[0] = jnp.transpose(merged[:128])
    turned[1] = jnp.transpose(merged[128:])
    lane = lax.broadcasted_iota(jnp.int32, (64, 128), 1) // 16
    for tile in range(2):
        slabs = [turned[tile, pl.ds(phase, 64, stride=4), :] for phase in range(4)]
        for part in range(2):
            for pair in range(2):
                made = None
                for odd in range(2):
                    for phase in range(4):
                        shift = (48 * odd + 16 * phase - 64 * part - 32 * pair) % 128
                        piece = slabs[phase] if shift == 0 else pltpu.roll(slabs[phase], shift, 1)
                        made = (
                            piece if made is None else jnp.where(lane == 4 * odd + phase, piece, made)
                        )
                block_row = 2 * tile + part
                whole[block_row, pair] = made
                made = made.astype(jnp.bfloat16)
                half[pair, block_row] = made
                if block_row < 2:
                    upper[pair, block_row] = made
                if block_row == 3:
                    lower[pair, 0] = made


def time_rolled(values, distance):
    row = lax.broadcasted_iota(jnp.int32, values.shape, 0)
    if distance < 0:
        return jnp.where(row == values.shape[0] - 1, 0.0, pltpu.roll(values, values.shape[0] - 1, 0))
    return jnp.where(row == 0, 0.0, pltpu.roll(values, 1, 0))


def widened(both):
    left = lax.broadcasted_iota(jnp.int32, both.shape, 1) < 64
    later = time_rolled(both, -1)
    even = jnp.where(left, both, pltpu.roll(later, 64, 1))
    odd = jnp.where(left, pltpu.roll(both, 64, 1), later)
    return even.astype(jnp.bfloat16), odd.astype(jnp.bfloat16)


def sparse_kernel(
    whole, own, before, after, words, words_back, codes, residual, field, first, recon, tail, turned, binned, leave
):
    inline_at, xline_at = lax.axis_index("inline"), lax.axis_index("xline")
    inline_last = inline_at == lax.axis_size("inline") - 1
    xline_last = xline_at == lax.axis_size("xline") - 1
    not_top = jnp.where(inline_at == 0, 0.0, 1.0)
    not_left = jnp.where(xline_at == 0, 0.0, 1.0)
    not_bottom = jnp.where(inline_last, 0.0, 1.0)
    not_right = jnp.where(xline_last, 0.0, 1.0)

    sources = [before.at[0], own.at[0], own.at[1], after.at[0]]
    for block_row in range(7):
        for pair in range(4):
            even, odd = widened(sources[pair][block_row].astype(jnp.float32))
            if pair > 0:
                field[block_row, 2 * pair - 1] = even
            if pair < 4:
                field[block_row, 2 * pair] = odd

    def correlated(source, patch_row, count):
        lhs = [
            source[patch_row + shift_a, shift_b : shift_b + count].reshape(count * 64, 128)
            for shift_a in (0, 1)
            for shift_b in (0, 1)
        ]
        return jnp.dot(
            jnp.concatenate(lhs, axis=1), words[...], preferred_element_type=jnp.float32
        )

    for patch_row in range(6):
        found = shrink_codes(step_size * correlated(field, patch_row, 6))
        if 1 <= patch_row <= 4:
            first[patch_row - 1] = found[64:320]
        if patch_row == 0:
            found = found * not_top
        found = jnp.concatenate([found[:64] * not_left, found[64:]], axis=0).astype(jnp.bfloat16)
        given = jnp.dot(found, words_back[...], preferred_element_type=jnp.float32)
        given = given.reshape(6, 64, 512)
        if patch_row > 0:
            upper = given[0:5, :, 128:256] + given[1:6, :, 0:128]
            if patch_row == 1:
                recon[0] = tail[...] + upper
            elif patch_row < 6:
                recon[patch_row - 1] = tail[...] + upper
        if patch_row < 5:
            tail[...] = given[0:5, :, 384:512] + given[1:6, :, 256:384]

    left = lax.broadcasted_iota(jnp.int32, (64, 128), 1) < 64
    for block_row in range(5):
        for pair in range(3):
            even = recon[block_row, 2 * pair]
            odd = recon[block_row, 2 * pair + 1] if pair < 2 else even
            near = jnp.where(left, even, pltpu.roll(odd, 64, 1))
            far = jnp.where(left, pltpu.roll(even, 64, 1), odd)
            rebuilt = near + time_rolled(far, 1)
            if block_row < 4 and pair < 2:
                rest = whole[block_row, pair] - rebuilt
                whole_rest = rest
                binned[block_row, pair] = whole_rest
            elif pair < 2:
                rest = (own[pair, 5].astype(jnp.float32) - rebuilt) * not_bottom
            else:
                rest = (after[0, block_row + 1].astype(jnp.float32) - rebuilt) * not_right
                if block_row == 4:
                    rest = rest * not_bottom
            even, odd = widened(rest)
            field[block_row, 2 * pair] = even
            if pair < 2:
                field[block_row, 2 * pair + 1] = odd

    stores = []
    for patch_row in range(4):
        found = first[patch_row] + step_size * correlated(field, patch_row, 4)
        first[patch_row] = shrink_codes(found)
        stores.append(
            pltpu.make_async_copy(first.at[patch_row], codes.at[patch_row], leave.at[patch_row])
        )
        stores[-1].start()

    lane = lax.broadcasted_iota(jnp.int32, (64, 128), 1) // 16
    for tile in range(2):
        for phase in range(4):
            made = None
            for part in range(2):
                for pair in range(2):
                    for odd in range(2):
                        shift = (64 * part + 32 * pair - 48 * odd - 16 * phase) % 128
                        piece = binned[2 * tile + part, pair]
                        piece = piece if shift == 0 else pltpu.roll(piece, shift, 1)
                        made = (
                            piece
                            if made is None
                            else jnp.where(lane == 4 * part + 2 * pair + odd, piece, made)
                        )
            turned[tile, pl.ds(phase, 64, stride=4), :] = made
    for tile in range(2):
        flat = jnp.transpose(turned[tile])
        for part in range(2):
            for block_col in range(4):
                for row in range(4):
                    at = part * 64 + block_col * 16 + row * 4
                    to = (2 * tile + part) * 64 + row * 16 + block_col * 4
                    residual[to : to + 4, :] = flat[at : at + 4, :]
    for store in stores:
        store.wait()


def body(
    base_volume, vintage_traces, dest_device, dest_slot, vintage_id, vintage_gains, dictionary
):
    trace_count, time_len = vintage_traces.shape
    device_count = lax.axis_size("inline") * lax.axis_size("xline")
    send_rows = device_count * 17
    sent = call_kernel(
        pack_kernel,
        jax.ShapeDtypeStruct((send_rows, 128), jnp.int32),
        pltpu.HBM,
        [
            pltpu.SMEM(vintage_gains.shape, jnp.float32),
            pltpu.VMEM(vintage_traces.shape, jnp.float32),
            pltpu.VMEM((1, trace_count), jnp.int32),
            pltpu.VMEM((1, trace_count), jnp.int32),
            pltpu.VMEM((1, trace_count), jnp.int32),
            pltpu.VMEM((send_rows, 128), jnp.int32),
            pltpu.SemaphoreType.DMA((5,)),
            pltpu.SemaphoreType.DMA((device_count // 16,)),
        ],
        pltpu.HBM,
        [
            vintage_gains,
            vintage_traces,
            dest_device.reshape(1, trace_count),
            dest_slot.reshape(1, trace_count),
            vintage_id.reshape(1, trace_count),
        ],
    )
    got = lax.all_to_all(
        sent.reshape(send_rows, 1, 128), ("inline", "xline"), split_axis=0, concat_axis=0, tiled=True
    ).reshape(send_rows, 128)
    words = dictionary.reshape(2, 4, 2, 4, 2, 4, 512).transpose(0, 2, 4, 5, 1, 3, 6).reshape(512, 512)
    words_back = words.T
    base = (
        base_volume.reshape(4, 4, 4, 4, time_len).transpose(0, 2, 1, 3, 4).reshape(256, time_len)
    )
    pair_shape = lambda *lead: jax.ShapeDtypeStruct(lead + (64, 128), jnp.bfloat16)
    whole, half, upper, lower = call_kernel(
        merge_kernel,
        (
            jax.ShapeDtypeStruct((4, 2, 64, 128), jnp.float32),
            pair_shape(2, 4),
            pair_shape(2, 2),
            pair_shape(2, 1),
        ),
        (pltpu.VMEM,) * 4,
        [
            pltpu.VMEM((256, send_rows), jnp.bfloat16),
            pltpu.VMEM((send_rows, 512), jnp.bfloat16),
            pltpu.VMEM((2, 256, 128), jnp.float32),
        ],
        pltpu.VMEM,
        [got, base],
    )

    def along(block, axis, distance):
        devices = range(lax.axis_size(axis))
        route = [(i - distance, i) for i in devices if i - distance in devices]
        return lax.ppermute(block, axis, route)

    from_below = along(upper, "inline", -1)
    from_above = along(lower, "inline", 1)
    own = jnp.concatenate([from_above, half, from_below], axis=1)
    after = along(own[0:1], "xline", -1)
    before = along(own[1:2], "xline", 1)
    codes, residual = call_kernel(
        sparse_kernel,
        (
            jax.ShapeDtypeStruct((4, 256, 512), jnp.float32),
            jax.ShapeDtypeStruct((256, time_len), jnp.float32),
        ),
        (pltpu.HBM, pltpu.VMEM),
        [
            pltpu.VMEM((7, 7, 64, 128), jnp.bfloat16),
            pltpu.VMEM((4, 256, 512), jnp.float32),
            pltpu.VMEM((5, 5, 64, 128), jnp.float32),
            pltpu.VMEM((5, 64, 128), jnp.float32),
            pltpu.VMEM((2, 256, 128), jnp.float32),
            pltpu.VMEM((4, 2, 64, 128), jnp.float32),
            pltpu.SemaphoreType.DMA((4,)),
        ],
        pltpu.VMEM,
        [whole, own, before, after, words, words_back],
    )
    return codes.reshape(4, 4, 64, 512), residual.reshape(16, 16, time_len)


def solution(mesh):
    in_specs = (
        P("inline", "xline", None),
        P(("inline", "xline"), None),
        P(("inline", "xline"), None),
        P(("inline", "xline")),
        P(("inline", "xline")),
        P(),
        P(),
    )
    out_specs = (P("inline", "xline", None, None), P("inline", "xline", None))
    return jax.shard_map(body, mesh=mesh, in_specs=in_specs, out_specs=out_specs, check_vma=False)
```

```python
import math

import jax
import jax.numpy as jnp
from jax import lax
from jax.experimental import pallas as pl
from jax.experimental.pallas import tpu as pltpu
from jax.sharding import PartitionSpec as P

step_size = 0.25
threshold = 0.02
octaves = 40.0
code_top = 32767.0
log_top = math.log2(12.0)
vmem_bytes = 48 * 1024 * 1024
all_vmem_bytes = 64 * 1024 * 1024


def shrink_codes(values):
    return values - jnp.clip(values, -threshold, threshold)


def call_kernel(kernel, out_shape, out_spaces, scratch, in_space, inputs, vmem_limit=vmem_bytes):
    return pl.pallas_call(
        kernel,
        out_shape=out_shape,
        in_specs=[pl.BlockSpec(memory_space=in_space)] * len(inputs),
        out_specs=jax.tree.map(lambda space: pl.BlockSpec(memory_space=space), out_spaces),
        scratch_shapes=scratch,
        compiler_params=pltpu.CompilerParams(vmem_limit_bytes=vmem_limit),
    )(*inputs)


def encode(values):
    size = jnp.log2(jnp.maximum(jnp.abs(values), 1e-30))
    code = (size + (octaves - log_top)) * (code_top / octaves)
    code = jnp.clip(jnp.round(code), 0.0, code_top).astype(jnp.int32)
    return jnp.where(values < 0, -code, code)


def decode(code):
    code = code.astype(jnp.float32)
    size = jnp.exp2(jnp.abs(code) * (octaves / code_top) + (log_top - octaves))
    return size * jnp.clip(code, -1.0, 1.0)


def pack_kernel(gains_in, traces_in, dest_in, slot_in, vid_in, out, gains, traces, dest, slot, vid, built, arrive, leave):
    loads = [
        pltpu.make_async_copy(source, target, arrive.at[number])
        for number, (source, target) in enumerate(
            ((dest_in, dest), (slot_in, slot), (gains_in, gains), (vid_in, vid), (traces_in, traces))
        )
    ]
    for load in loads:
        load.start()
    trace_count = traces.shape[0]
    device_count = out.shape[0] // 17
    chunks = trace_count // 128
    me = lax.axis_index("inline") * lax.axis_size("xline") + lax.axis_index("xline")
    loads[0].wait()
    loads[1].wait()
    row = lax.broadcasted_iota(jnp.int32, (128, 128), 0)
    lane = lax.broadcasted_iota(jnp.int32, (128, 128), 1)
    before = jnp.where(row < lane, 1.0, 0.0).astype(jnp.bfloat16)
    carry = jnp.zeros((device_count, 1), jnp.float32)
    places, owners, listed = [], [], []
    for chunk in range(chunks):
        target = dest[:, chunk * 128 : chunk * 128 + 128]
        hit = jnp.where(row == target, 1.0, 0.0)
        hit_half = hit.astype(jnp.bfloat16)
        earlier = jnp.dot(hit_half, before, preferred_element_type=jnp.float32)
        rank = jnp.sum(hit * (earlier + carry), axis=0, keepdims=True)
        carry = carry + jnp.sum(hit, axis=1, keepdims=True)
        rank = rank.astype(jnp.int32)
        places.append(target * 17 + rank)
        owners.append(hit_half)
        wanted = (slot[:, chunk * 128 : chunk * 128 + 128] + 1).astype(jnp.float32)
        spot = lax.rem(17 * me + rank, 128)
        listed.append(jnp.where(row == spot, wanted, 0.0).astype(jnp.bfloat16))
    place = jnp.concatenate(places, axis=1)
    owner = jnp.concatenate(owners, axis=1)
    listing = jnp.concatenate(listed, axis=1)
    slots = lax.dot_general(
        owner, listing, (((1,), (1,)), ((), ())), preferred_element_type=jnp.float32
    ).astype(jnp.int32)

    loads[2].wait()
    loads[3].wait()
    survey = vid[...]
    gain = jnp.zeros(survey.shape, jnp.float32)
    for number in range(gains.shape[0]):
        gain = jnp.where(survey == number, gains[number], gain)
    gain = jnp.transpose(jnp.broadcast_to(gain, (128, trace_count)))
    loads[4].wait()
    high, low = [], []
    for half in range(2):
        code = encode(traces[:, half * 128 : half * 128 + 128] * gain)
        high.append((code >> 8).astype(jnp.float32).astype(jnp.bfloat16))
        low.append((code & 255).astype(jnp.float32).astype(jnp.bfloat16))
    halves = jnp.concatenate(high + low, axis=1)

    owners_each = 16
    rows = owners_each * 17
    index = lax.broadcasted_iota(jnp.int32, (rows, trace_count), 0)
    stores = []
    for block in range(device_count // owners_each):
        pick = jnp.where(index == place - block * rows, 1.0, 0.0).astype(jnp.bfloat16)
        moved = jnp.dot(pick, halves, preferred_element_type=jnp.float32)
        code = (moved[:, :256] * 256.0 + moved[:, 256:]).astype(jnp.int32)
        built[block * rows : block * rows + rows, :] = (code[:, :128] << 16) | (
            code[:, 128:] & 65535
        )
        built[pl.ds(block * rows + 16, owners_each, stride=17), :] = slots[
            block * owners_each : block * owners_each + owners_each
        ]
        spot = pl.ds(block * rows, rows)
        stores.append(pltpu.make_async_copy(built.at[spot], out.at[spot], leave.at[block]))
        stores[-1].start()
    for store in stores:
        store.wait()


def merge_kernel(got, base, whole, half, to_even, to_odd, pick, parts, turned):
    tiles = got.shape[0] // 128
    bin_row = lax.broadcasted_iota(jnp.int32, (256, 128), 0)
    bin_slot = (
        (bin_row // 64) * 64 + ((bin_row // 4) % 4) * 16 + ((bin_row // 16) % 4) * 4 + bin_row % 4
    )
    wanted = bin_slot + 1
    listed = got[pl.ds(16, 128, stride=17), :]
    begin = 17 * lax.broadcasted_iota(jnp.int32, (128, 128), 0)
    lane = lax.broadcasted_iota(jnp.int32, (128, 128), 1)
    tile_of = begin // 128 + jnp.where(lane < begin % 128, 1, 0)
    fold = jnp.zeros((256, 128), jnp.float32)
    for tile in range(tiles):
        low_group, high_group = (128 * tile) // 136, min((128 * tile + 127) // 136, 15)
        spot = slice(8 * low_group, 8 * high_group + 8)
        slots = jnp.sum(jnp.where(tile_of[spot] == tile, listed[spot], 0), axis=0, keepdims=True)
        hit = jnp.where(wanted == slots, 1.0, 0.0)
        fold = fold + hit
        spot = slice(128 * tile, 128 * tile + 128)
        pick[:, spot] = hit.astype(jnp.bfloat16)
        word = got[spot, :]
        for side, code in enumerate((word >> 16, (word << 16) >> 16)):
            value = decode(code)
            high = value.astype(jnp.bfloat16)
            low = (value - high.astype(jnp.float32)).astype(jnp.bfloat16)
            parts[spot, side * 128 : side * 128 + 128] = high
            parts[spot, 256 + side * 128 : 384 + side * 128] = low
    stack = jnp.dot(pick[...], parts[...], preferred_element_type=jnp.float32)
    fold = jnp.sum(fold, axis=1, keepdims=True)
    merged = (base[...] + (stack[:, :256] + stack[:, 256:])) / (1.0 + fold)
    turned[0] = jnp.transpose(merged[:128])
    turned[1] = jnp.transpose(merged[128:])
    lane = lax.broadcasted_iota(jnp.int32, (64, 128), 1) // 16
    for tile in range(2):
        slabs = [turned[tile, pl.ds(phase, 64, stride=4), :] for phase in range(4)]
        for part in range(2):
            for pair in range(2):
                made = None
                for odd in range(2):
                    for phase in range(4):
                        shift = (48 * odd + 16 * phase - 64 * part - 32 * pair) % 128
                        piece = slabs[phase] if shift == 0 else pltpu.roll(slabs[phase], shift, 1)
                        made = (
                            piece if made is None else jnp.where(lane == 4 * odd + phase, piece, made)
                        )
                block_row = 2 * tile + part
                whole[block_row, pair] = made
                made = made.astype(jnp.bfloat16)
                half[pair, block_row] = made
    odd_device = lax.rem(lax.axis_index("inline"), 2)
    to_even[...] = half[:, pl.ds(2 - 2 * odd_device, 2)]
    to_odd[...] = half[:, pl.ds(2 * odd_device, 2)]


def assemble_kernel(half, from_even, from_odd, to_even, to_odd):
    inline_at = lax.axis_index("inline")
    odd_row = lax.rem(inline_at, 2) == 1
    odd_col = lax.rem(lax.axis_index("xline"), 2)
    for target, pair in ((to_even, 1 - odd_col), (to_odd, odd_col)):
        above = jnp.where(odd_row, from_even[pair, 1], from_odd[pair, 1])
        target[0] = jnp.where(inline_at == 0, jnp.zeros_like(above), above)
        target[1:5] = half[pair]
        below = jnp.where(odd_row, from_odd[pair], from_even[pair])
        last = inline_at == lax.axis_size("inline") - 1
        target[5:7] = jnp.where(last, jnp.zeros_like(below), below)


def time_rolled(values, distance):
    row = lax.broadcasted_iota(jnp.int32, values.shape, 0)
    if distance < 0:
        return jnp.where(row == values.shape[0] - 1, 0.0, pltpu.roll(values, values.shape[0] - 1, 0))
    return jnp.where(row == 0, 0.0, pltpu.roll(values, 1, 0))


def widened(both):
    left = lax.broadcasted_iota(jnp.int32, both.shape, 1) < 64
    later = time_rolled(both, -1)
    even = jnp.where(left, both, pltpu.roll(later, 64, 1))
    odd = jnp.where(left, pltpu.roll(both, 64, 1), later)
    return even.astype(jnp.bfloat16), odd.astype(jnp.bfloat16)


def sparse_kernel(
    whole, own_even, own_odd, from_even, from_odd, words, words_back, codes, residual, field, first, recon, tail, turned, binned, leave
):
    inline_at, xline_at = lax.axis_index("inline"), lax.axis_index("xline")
    inline_last = inline_at == lax.axis_size("inline") - 1
    xline_last = xline_at == lax.axis_size("xline") - 1
    not_top = jnp.where(inline_at == 0, 0.0, 1.0)
    not_left = jnp.where(xline_at == 0, 0.0, 1.0)
    not_bottom = jnp.where(inline_last, 0.0, 1.0)
    not_right = jnp.where(xline_last, 0.0, 1.0)

    odd_device = lax.rem(xline_at, 2) == 1
    sources = ((from_odd, from_even), (own_odd, own_even), (own_even, own_odd), (from_even, from_odd))
    edges = (not_left, None, None, not_right)

    def loaded(pair, block_row):
        if_even, if_odd = sources[pair]
        both = jnp.where(odd_device, if_odd[block_row], if_even[block_row]).astype(jnp.float32)
        return both if edges[pair] is None else both * edges[pair]

    for block_row in range(7):
        for pair in range(4):
            even, odd = widened(loaded(pair, block_row))
            if pair > 0:
                field[block_row, 2 * pair - 1] = even
            if pair < 4:
                field[block_row, 2 * pair] = odd

    def correlated(source, patch_row, count):
        lhs = [
            source[patch_row + shift_a, shift_b : shift_b + count].reshape(count * 64, 128)
            for shift_a in (0, 1)
            for shift_b in (0, 1)
        ]
        return jnp.dot(
            jnp.concatenate(lhs, axis=1), words[...], preferred_element_type=jnp.float32
        )

    for patch_row in range(6):
        found = shrink_codes(step_size * correlated(field, patch_row, 6))
        if 1 <= patch_row <= 4:
            first[patch_row - 1] = found[64:320]
        if patch_row == 0:
            found = found * not_top
        found = jnp.concatenate([found[:64] * not_left, found[64:]], axis=0).astype(jnp.bfloat16)
        given = jnp.dot(found, words_back[...], preferred_element_type=jnp.float32)
        given = given.reshape(6, 64, 512)
        if patch_row > 0:
            upper = given[0:5, :, 128:256] + given[1:6, :, 0:128]
            if patch_row == 1:
                recon[0] = tail[...] + upper
            elif patch_row < 6:
                recon[patch_row - 1] = tail[...] + upper
        if patch_row < 5:
            tail[...] = given[0:5, :, 384:512] + given[1:6, :, 256:384]

    left = lax.broadcasted_iota(jnp.int32, (64, 128), 1) < 64
    for block_row in range(5):
        for pair in range(3):
            even = recon[block_row, 2 * pair]
            odd = recon[block_row, 2 * pair + 1] if pair < 2 else even
            near = jnp.where(left, even, pltpu.roll(odd, 64, 1))
            far = jnp.where(left, pltpu.roll(even, 64, 1), odd)
            rebuilt = near + time_rolled(far, 1)
            if block_row < 4 and pair < 2:
                rest = whole[block_row, pair] - rebuilt
                whole_rest = rest
                binned[block_row, pair] = whole_rest
            elif pair < 2:
                rest = (loaded(pair + 1, 5) - rebuilt) * not_bottom
            else:
                rest = (loaded(3, block_row + 1) - rebuilt) * not_right
                if block_row == 4:
                    rest = rest * not_bottom
            even, odd = widened(rest)
            field[block_row, 2 * pair] = even
            if pair < 2:
                field[block_row, 2 * pair + 1] = odd

    stores = []
    for patch_row in range(4):
        found = first[patch_row] + step_size * correlated(field, patch_row, 4)
        first[patch_row] = shrink_codes(found)
        stores.append(
            pltpu.make_async_copy(first.at[patch_row], codes.at[patch_row], leave.at[patch_row])
        )
        stores[-1].start()

    lane = lax.broadcasted_iota(jnp.int32, (64, 128), 1) // 16
    for tile in range(2):
        for phase in range(4):
            made = None
            for part in range(2):
                for pair in range(2):
                    for odd in range(2):
                        shift = (64 * part + 32 * pair - 48 * odd - 16 * phase) % 128
                        piece = binned[2 * tile + part, pair]
                        piece = piece if shift == 0 else pltpu.roll(piece, shift, 1)
                        made = (
                            piece
                            if made is None
                            else jnp.where(lane == 4 * part + 2 * pair + odd, piece, made)
                        )
            turned[tile, pl.ds(phase, 64, stride=4), :] = made
    for tile in range(2):
        flat = jnp.transpose(turned[tile])
        for part in range(2):
            for block_col in range(4):
                for row in range(4):
                    at = part * 64 + block_col * 16 + row * 4
                    to = (2 * tile + part) * 64 + row * 16 + block_col * 4
                    residual[to : to + 4, :] = flat[at : at + 4, :]
    for store in stores:
        store.wait()


def body(
    base_volume, vintage_traces, dest_device, dest_slot, vintage_id, vintage_gains, dictionary
):
    trace_count, time_len = vintage_traces.shape
    device_count = lax.axis_size("inline") * lax.axis_size("xline")
    send_rows = device_count * 17
    sent = call_kernel(
        pack_kernel,
        jax.ShapeDtypeStruct((send_rows, 128), jnp.int32),
        pltpu.HBM,
        [
            pltpu.SMEM(vintage_gains.shape, jnp.float32),
            pltpu.VMEM(vintage_traces.shape, jnp.float32),
            pltpu.VMEM((1, trace_count), jnp.int32),
            pltpu.VMEM((1, trace_count), jnp.int32),
            pltpu.VMEM((1, trace_count), jnp.int32),
            pltpu.VMEM((send_rows, 128), jnp.int32),
            pltpu.SemaphoreType.DMA((5,)),
            pltpu.SemaphoreType.DMA((device_count // 16,)),
        ],
        pltpu.HBM,
        [
            vintage_gains,
            vintage_traces,
            dest_device.reshape(1, trace_count),
            dest_slot.reshape(1, trace_count),
            vintage_id.reshape(1, trace_count),
        ],
        all_vmem_bytes,
    )
    got = lax.all_to_all(
        sent.reshape(send_rows, 1, 128), ("inline", "xline"), split_axis=0, concat_axis=0, tiled=True
    ).reshape(send_rows, 128)
    words = dictionary.reshape(2, 4, 2, 4, 2, 4, 512).transpose(0, 2, 4, 5, 1, 3, 6).reshape(512, 512)
    words_back = words.T
    base = (
        base_volume.reshape(4, 4, 4, 4, time_len).transpose(0, 2, 1, 3, 4).reshape(256, time_len)
    )
    pair_shape = lambda *lead: jax.ShapeDtypeStruct(lead + (64, 128), jnp.bfloat16)
    whole, half, to_even, to_odd = call_kernel(
        merge_kernel,
        (
            jax.ShapeDtypeStruct((4, 2, 64, 128), jnp.float32),
            pair_shape(2, 4),
            pair_shape(2, 2),
            pair_shape(2, 2),
        ),
        (pltpu.VMEM,) * 4,
        [
            pltpu.VMEM((256, send_rows), jnp.bfloat16),
            pltpu.VMEM((send_rows, 512), jnp.bfloat16),
            pltpu.VMEM((2, 256, 128), jnp.float32),
        ],
        pltpu.VMEM,
        [got, base],
    )

    def swapped(block, axis, odd_pairs):
        count = lax.axis_size(axis)
        partner = [(i + 1 if i % 2 == odd_pairs else i - 1) % count for i in range(count)]
        return lax.ppermute(block, axis, list(enumerate(partner)))

    from_even, from_odd = swapped(to_even, "inline", 0), swapped(to_odd, "inline", 1)
    own_even, own_odd = call_kernel(
        assemble_kernel,
        (pair_shape(7), pair_shape(7)),
        (pltpu.VMEM,) * 2,
        [],
        pltpu.VMEM,
        [half, from_even, from_odd],
    )
    from_even, from_odd = swapped(own_even, "xline", 0), swapped(own_odd, "xline", 1)
    codes, residual = call_kernel(
        sparse_kernel,
        (
            jax.ShapeDtypeStruct((4, 256, 512), jnp.float32),
            jax.ShapeDtypeStruct((256, time_len), jnp.float32),
        ),
        (pltpu.HBM, pltpu.VMEM),
        [
            pltpu.VMEM((7, 7, 64, 128), jnp.bfloat16),
            pltpu.VMEM((4, 256, 512), jnp.float32),
            pltpu.VMEM((5, 5, 64, 128), jnp.float32),
            pltpu.VMEM((5, 64, 128), jnp.float32),
            pltpu.VMEM((2, 256, 128), jnp.float32),
            pltpu.VMEM((4, 2, 64, 128), jnp.float32),
            pltpu.SemaphoreType.DMA((4,)),
        ],
        pltpu.VMEM,
        [whole, own_even, own_odd, from_even, from_odd, words, words_back],
    )
    return codes.reshape(4, 4, 64, 512), residual.reshape(16, 16, time_len)


def solution(mesh):
    in_specs = (
        P("inline", "xline", None),
        P(("inline", "xline"), None),
        P(("inline", "xline"), None),
        P(("inline", "xline")),
        P(("inline", "xline")),
        P(),
        P(),
    )
    out_specs = (P("inline", "xline", None, None), P("inline", "xline", None))
    return jax.shard_map(body, mesh=mesh, in_specs=in_specs, out_specs=out_specs, check_vma=False)
```

```python
import math

import jax
import jax.numpy as jnp
from jax import lax
from jax.experimental import pallas as pl
from jax.experimental.pallas import tpu as pltpu
from jax.sharding import PartitionSpec as P

step_size = 0.25
threshold = 0.02
octaves = 40.0
code_top = 32767.0
log_top = math.log2(12.0)
vmem_bytes = 48 * 1024 * 1024
all_vmem_bytes = 64 * 1024 * 1024


def shrink_codes(values):
    return values - jnp.clip(values, -threshold, threshold)


def call_kernel(kernel, out_shape, out_spaces, scratch, in_space, inputs, vmem_limit=vmem_bytes, cost=None):
    return pl.pallas_call(
        kernel,
        out_shape=out_shape,
        in_specs=[pl.BlockSpec(memory_space=in_space)] * len(inputs),
        out_specs=jax.tree.map(lambda space: pl.BlockSpec(memory_space=space), out_spaces),
        scratch_shapes=scratch,
        cost_estimate=cost,
        compiler_params=pltpu.CompilerParams(vmem_limit_bytes=vmem_limit),
    )(*inputs)


def encode(values):
    size = jnp.log2(jnp.maximum(jnp.abs(values), 1e-30))
    code = (size + (octaves - log_top)) * (code_top / octaves)
    code = jnp.clip(jnp.round(code), 0.0, code_top).astype(jnp.int32)
    return jnp.where(values < 0, -code, code)


def decode(code):
    code = code.astype(jnp.float32)
    size = jnp.exp2(jnp.abs(code) * (octaves / code_top) + (log_top - octaves))
    return size * jnp.clip(code, -1.0, 1.0)


def pack_kernel(gains_in, traces_in, dest_in, slot_in, vid_in, out, gains, traces, dest, slot, vid, built, arrive, leave):
    loads = [
        pltpu.make_async_copy(source, target, arrive.at[number])
        for number, (source, target) in enumerate(
            ((dest_in, dest), (slot_in, slot), (gains_in, gains), (vid_in, vid), (traces_in, traces))
        )
    ]
    for load in loads:
        load.start()
    trace_count = traces.shape[0]
    device_count = out.shape[0] // 17
    chunks = trace_count // 128
    me = lax.axis_index("inline") * lax.axis_size("xline") + lax.axis_index("xline")
    loads[0].wait()
    loads[1].wait()
    row = lax.broadcasted_iota(jnp.int32, (128, 128), 0)
    lane = lax.broadcasted_iota(jnp.int32, (128, 128), 1)
    before = jnp.where(row < lane, 1.0, 0.0).astype(jnp.bfloat16)
    carry = jnp.zeros((device_count, 1), jnp.float32)
    places, owners, listed = [], [], []
    for chunk in range(chunks):
        target = dest[:, chunk * 128 : chunk * 128 + 128]
        hit = jnp.where(row == target, 1.0, 0.0)
        hit_half = hit.astype(jnp.bfloat16)
        earlier = jnp.dot(hit_half, before, preferred_element_type=jnp.float32)
        rank = jnp.sum(hit * (earlier + carry), axis=0, keepdims=True)
        carry = carry + jnp.sum(hit, axis=1, keepdims=True)
        rank = rank.astype(jnp.int32)
        places.append(target * 17 + rank)
        owners.append(hit_half)
        wanted = (slot[:, chunk * 128 : chunk * 128 + 128] + 1).astype(jnp.float32)
        spot = lax.rem(17 * me + rank, 128)
        listed.append(jnp.where(row == spot, wanted, 0.0).astype(jnp.bfloat16))
    place = jnp.concatenate(places, axis=1)
    owner = jnp.concatenate(owners, axis=1)
    listing = jnp.concatenate(listed, axis=1)
    slots = lax.dot_general(
        owner, listing, (((1,), (1,)), ((), ())), preferred_element_type=jnp.float32
    ).astype(jnp.int32)

    loads[2].wait()
    loads[3].wait()
    survey = vid[...]
    gain = jnp.zeros(survey.shape, jnp.float32)
    for number in range(gains.shape[0]):
        gain = jnp.where(survey == number, gains[number], gain)
    gain = jnp.transpose(jnp.broadcast_to(gain, (128, trace_count)))
    loads[4].wait()
    high, low = [], []
    for half in range(2):
        code = encode(traces[:, half * 128 : half * 128 + 128] * gain)
        high.append((code >> 8).astype(jnp.float32).astype(jnp.bfloat16))
        low.append((code & 255).astype(jnp.float32).astype(jnp.bfloat16))
    halves = jnp.concatenate(high + low, axis=1)

    owners_each = 16
    rows = owners_each * 17
    index = lax.broadcasted_iota(jnp.int32, (rows, trace_count), 0)
    stores = []
    for block in range(device_count // owners_each):
        pick = jnp.where(index == place - block * rows, 1.0, 0.0).astype(jnp.bfloat16)
        moved = jnp.dot(pick, halves, preferred_element_type=jnp.float32)
        code = (moved[:, :256] * 256.0 + moved[:, 256:]).astype(jnp.int32)
        built[block * rows : block * rows + rows, :] = (code[:, :128] << 16) | (
            code[:, 128:] & 65535
        )
        built[pl.ds(block * rows + 16, owners_each, stride=17), :] = slots[
            block * owners_each : block * owners_each + owners_each
        ]
        spot = pl.ds(block * rows, rows)
        stores.append(pltpu.make_async_copy(built.at[spot], out.at[spot], leave.at[block]))
        stores[-1].start()
    for store in stores:
        store.wait()


def merge_kernel(got, base, whole, half, to_even, to_odd, pick, parts, turned):
    tiles = got.shape[0] // 128
    bin_row = lax.broadcasted_iota(jnp.int32, (256, 128), 0)
    bin_slot = (
        (bin_row // 64) * 64 + ((bin_row // 4) % 4) * 16 + ((bin_row // 16) % 4) * 4 + bin_row % 4
    )
    wanted = bin_slot + 1
    listed = got[pl.ds(16, 128, stride=17), :]
    begin = 17 * lax.broadcasted_iota(jnp.int32, (128, 128), 0)
    lane = lax.broadcasted_iota(jnp.int32, (128, 128), 1)
    tile_of = begin // 128 + jnp.where(lane < begin % 128, 1, 0)
    fold = jnp.zeros((256, 128), jnp.float32)
    for tile in range(tiles):
        low_group, high_group = (128 * tile) // 136, min((128 * tile + 127) // 136, 15)
        spot = slice(8 * low_group, 8 * high_group + 8)
        slots = jnp.sum(jnp.where(tile_of[spot] == tile, listed[spot], 0), axis=0, keepdims=True)
        hit = jnp.where(wanted == slots, 1.0, 0.0)
        fold = fold + hit
        spot = slice(128 * tile, 128 * tile + 128)
        pick[:, spot] = hit.astype(jnp.bfloat16)
        word = got[spot, :]
        for side, code in enumerate((word >> 16, (word << 16) >> 16)):
            value = decode(code)
            high = value.astype(jnp.bfloat16)
            low = (value - high.astype(jnp.float32)).astype(jnp.bfloat16)
            parts[spot, side * 128 : side * 128 + 128] = high
            parts[spot, 256 + side * 128 : 384 + side * 128] = low
    stack = jnp.dot(pick[...], parts[...], preferred_element_type=jnp.float32)
    fold = jnp.sum(fold, axis=1, keepdims=True)
    merged = (base[...] + (stack[:, :256] + stack[:, 256:])) / (1.0 + fold)
    turned[0] = jnp.transpose(merged[:128])
    turned[1] = jnp.transpose(merged[128:])
    lane = lax.broadcasted_iota(jnp.int32, (64, 128), 1) // 16
    for tile in range(2):
        slabs = [turned[tile, pl.ds(phase, 64, stride=4), :] for phase in range(4)]
        for part in range(2):
            for pair in range(2):
                made = None
                for odd in range(2):
                    for phase in range(4):
                        shift = (48 * odd + 16 * phase - 64 * part - 32 * pair) % 128
                        piece = slabs[phase] if shift == 0 else pltpu.roll(slabs[phase], shift, 1)
                        made = (
                            piece if made is None else jnp.where(lane == 4 * odd + phase, piece, made)
                        )
                block_row = 2 * tile + part
                whole[block_row, pair] = made
                made = made.astype(jnp.bfloat16)
                half[pair, block_row] = made
    odd_device = lax.rem(lax.axis_index("inline"), 2)
    to_even[...] = half[:, pl.ds(2 - 2 * odd_device, 2)]
    to_odd[...] = half[:, pl.ds(2 * odd_device, 2)]


def assemble_kernel(half, from_even, from_odd, to_even, to_odd):
    inline_at = lax.axis_index("inline")
    odd_row = lax.rem(inline_at, 2) == 1
    odd_col = lax.rem(lax.axis_index("xline"), 2)
    for target, pair in ((to_even, 1 - odd_col), (to_odd, odd_col)):
        above = jnp.where(odd_row, from_even[pair, 1], from_odd[pair, 1])
        target[0] = jnp.where(inline_at == 0, jnp.zeros_like(above), above)
        target[1:5] = half[pair]
        below = jnp.where(odd_row, from_odd[pair], from_even[pair])
        last = inline_at == lax.axis_size("inline") - 1
        target[5:7] = jnp.where(last, jnp.zeros_like(below), below)


def time_rolled(values, distance):
    row = lax.broadcasted_iota(jnp.int32, values.shape, 0)
    if distance < 0:
        return jnp.where(row == values.shape[0] - 1, 0.0, pltpu.roll(values, values.shape[0] - 1, 0))
    return jnp.where(row == 0, 0.0, pltpu.roll(values, 1, 0))


def widened(both):
    left = lax.broadcasted_iota(jnp.int32, both.shape, 1) < 64
    later = time_rolled(both, -1)
    even = jnp.where(left, both, pltpu.roll(later, 64, 1))
    odd = jnp.where(left, pltpu.roll(both, 64, 1), later)
    return even.astype(jnp.bfloat16), odd.astype(jnp.bfloat16)


def correlated(near, far, words, first_row, count):
    lhs = [
        source[first_row + shift : first_row + shift + count].reshape(count * 64, 128)
        for shift in (0, 1)
        for source in (near, far)
    ]
    return jnp.dot(jnp.concatenate(lhs, axis=1), words[...], preferred_element_type=jnp.float32)


def given_back(found, words_back, sides):
    given = {}
    for side in sides:
        for shift in (0, 1):
            at = 256 * shift + 128 * side
            given[shift, side] = at
    columns = {}
    if len(sides) == 2:
        full = jnp.dot(found, words_back[...], preferred_element_type=jnp.float32)
        for key, at in given.items():
            columns[key] = full[:, at : at + 128].reshape(6, 64, 128)
    else:
        picked = jnp.concatenate([words_back[:, at : at + 128] for at in given.values()], axis=1)
        full = jnp.dot(found, picked, preferred_element_type=jnp.float32)
        for number, key in enumerate(given):
            columns[key] = full[:, 128 * number : 128 * number + 128].reshape(6, 64, 128)
    return [columns[0, side][1:6] + columns[1, side][0:5] for side in sides]


def rebuilt_half(given, odd):
    moved = pltpu.roll(given, 64, 1)
    return moved + time_rolled(given, 1) if odd else given + time_rolled(moved, 1)


def widened_half(block, odd):
    left = lax.broadcasted_iota(jnp.int32, block.shape, 1) < 64
    later = time_rolled(block, -1)
    if odd:
        return jnp.where(left, pltpu.roll(block, 64, 1), later).astype(jnp.bfloat16)
    return jnp.where(left, block, pltpu.roll(later, 64, 1)).astype(jnp.bfloat16)


def first_codes(near, far, words, not_top):
    found = shrink_codes(step_size * correlated(near, far, words, 0, 6))
    return found[64:320], jnp.concatenate([found[:64] * not_top, found[64:]], axis=0)


def last_codes(before, near, far, words):
    found = before + step_size * correlated(near, far, words, 0, 4)
    return shrink_codes(found).reshape(4, 64, 512)


def inner_kernel(whole, own_even, own_odd, words, words_back, field, first, recon, rests, later, made_codes):
    inline_at = lax.axis_index("inline")
    not_top = jnp.where(inline_at == 0, 0.0, 1.0)
    not_bottom = jnp.where(inline_at == lax.axis_size("inline") - 1, 0.0, 1.0)
    odd_device = lax.rem(lax.axis_index("xline"), 2) == 1

    def loaded(pair, block_row):
        if_even, if_odd = ((own_odd, own_even), (own_even, own_odd))[pair]
        return jnp.where(odd_device, if_odd[block_row], if_even[block_row]).astype(jnp.float32)

    for pair in range(2):
        for block_row in range(7):
            even, odd = widened(loaded(pair, block_row))
            field[2 * pair, block_row] = even
            field[2 * pair + 1, block_row] = odd
    kept, found = zip(
        *(first_codes(field.at[at], field.at[at + 1], words, not_top) for at in range(3))
    )
    given = [given_back(part.astype(jnp.bfloat16), words_back, (0, 1)) for part in found]
    recon[0] = given[0][0]
    recon[1] = given[2][1]
    for column in (1, 2):
        pair, odd = column // 2, column % 2
        for block_row in range(5):
            rebuilt = rebuilt_half(given[column][0][block_row] + given[column - 1][1][block_row], odd)
            if block_row < 4:
                rest = whole[block_row, pair] - rebuilt
                rests[column - 1, block_row] = rest
            else:
                rest = (loaded(pair, 5) - rebuilt) * not_bottom
            later[column - 1, block_row] = widened_half(rest, odd)
    first[0] = kept[0]
    first[1] = kept[2]
    made_codes[...] = last_codes(kept[1], later.at[0], later.at[1], words)


def sparse_kernel(
    whole, own_even, own_odd, from_even, from_odd, inner, first_inner, recon_inner, rests, later_inner,
    codes_inner, words, words_back, codes, residual, outer, later, turned, binned, made_codes, flat_rest, leave
):
    stores = [pltpu.make_async_copy(codes_inner, codes.at[:, 1], leave.at[0])]
    stores[0].start()
    inline_at, xline_at = lax.axis_index("inline"), lax.axis_index("xline")
    inline_last = inline_at == lax.axis_size("inline") - 1
    xline_last = xline_at == lax.axis_size("xline") - 1
    not_top = jnp.where(inline_at == 0, 0.0, 1.0)
    not_left = jnp.where(xline_at == 0, 0.0, 1.0)
    not_bottom = jnp.where(inline_last, 0.0, 1.0)
    not_right = jnp.where(xline_last, 0.0, 1.0)

    odd_device = lax.rem(xline_at, 2) == 1
    sources = ((from_odd, from_even), (own_odd, own_even), (own_even, own_odd), (from_even, from_odd))
    edges = (not_left, None, None, not_right)

    def loaded(pair, block_row):
        if_even, if_odd = sources[pair]
        both = jnp.where(odd_device, if_odd[block_row], if_even[block_row]).astype(jnp.float32)
        return both if edges[pair] is None else both * edges[pair]

    def leaving(column, made):
        made_codes[len(stores) - 1] = made
        for part in range(2 if column == 3 else 1):
            rows = pl.ds(2 * part, 2) if column == 3 else pl.ds(0, 4)
            stores.append(
                pltpu.make_async_copy(
                    made_codes.at[len(stores) - 1 - part, rows],
                    codes.at[rows, column],
                    leave.at[len(stores)],
                )
            )
            stores[-1].start()

    def rest_of(column, given, spot):
        pair, odd = column // 2, column % 2
        for block_row in range(5):
            rebuilt = rebuilt_half(given[block_row], odd)
            if column == 4:
                rest = (loaded(3, block_row + 1) - rebuilt) * not_right
            elif block_row < 4:
                rest = whole[block_row, pair] - rebuilt
                binned[pair, block_row] = rest
            else:
                rest = loaded(pair + 1, 5) - rebuilt
            if block_row == 4:
                rest = rest * not_bottom
            later[spot, block_row] = widened_half(rest, odd)

    for block_row in range(7):
        outer[0, block_row] = widened(loaded(0, block_row))[1]
        even, odd = widened(loaded(3, block_row))
        outer[1, block_row] = even
        outer[2, block_row] = odd
    unused, left_found = first_codes(outer.at[0], inner.at[0], words, not_top)
    kept, middle = first_codes(inner.at[3], outer.at[1], words, not_top)
    unused, right_found = first_codes(outer.at[1], outer.at[2], words, not_top)
    (left_far,) = given_back((left_found * not_left).astype(jnp.bfloat16), words_back, (1,))
    near, far = given_back(middle.astype(jnp.bfloat16), words_back, (0, 1))
    (right_near,) = given_back(right_found.astype(jnp.bfloat16), words_back, (0,))
    rest_of(0, recon_inner[0] + left_far, 0)
    rest_of(3, recon_inner[1] + near, 1)
    rest_of(4, far + right_near, 2)
    leaving(0, last_codes(first_inner[0], later.at[0], later_inner.at[0], words))
    leaving(2, last_codes(first_inner[1], later_inner.at[1], later.at[1], words))
    leaving(3, last_codes(kept, later.at[1], later.at[2], words))
    left = lax.broadcasted_iota(jnp.int32, (64, 128), 1) < 64
    for block_row in range(4):
        binned[0, block_row] = jnp.where(left, binned[0, block_row], rests[0, block_row])
        binned[1, block_row] = jnp.where(left, rests[1, block_row], binned[1, block_row])
    lane = lax.broadcasted_iota(jnp.int32, (64, 128), 1) // 16
    for tile in range(2):
        for phase in range(4):
            made = None
            for part in range(2):
                for pair in range(2):
                    for odd in range(2):
                        shift = (64 * part + 32 * pair - 48 * odd - 16 * phase) % 128
                        piece = binned[pair, 2 * tile + part]
                        piece = piece if shift == 0 else pltpu.roll(piece, shift, 1)
                        made = (
                            piece
                            if made is None
                            else jnp.where(lane == 4 * part + 2 * pair + odd, piece, made)
                        )
            turned[tile, pl.ds(phase, 64, stride=4), :] = made
    for tile in range(2):
        flat = jnp.transpose(turned[tile])
        for part in range(2):
            for block_col in range(4):
                for row in range(4):
                    at = part * 64 + block_col * 16 + row * 4
                    to = (2 * tile + part) * 64 + row * 16 + block_col * 4
                    flat_rest[to : to + 4, :] = flat[at : at + 4, :]
    stores.append(pltpu.make_async_copy(flat_rest, residual, leave.at[5]))
    stores[-1].start()
    for store in stores:
        store.wait()


def body(
    base_volume, vintage_traces, dest_device, dest_slot, vintage_id, vintage_gains, dictionary
):
    trace_count, time_len = vintage_traces.shape
    device_count = lax.axis_size("inline") * lax.axis_size("xline")
    send_rows = device_count * 17
    sent = call_kernel(
        pack_kernel,
        jax.ShapeDtypeStruct((send_rows, 128), jnp.int32),
        pltpu.HBM,
        [
            pltpu.SMEM(vintage_gains.shape, jnp.float32),
            pltpu.VMEM(vintage_traces.shape, jnp.float32),
            pltpu.VMEM((1, trace_count), jnp.int32),
            pltpu.VMEM((1, trace_count), jnp.int32),
            pltpu.VMEM((1, trace_count), jnp.int32),
            pltpu.VMEM((send_rows, 128), jnp.int32),
            pltpu.SemaphoreType.DMA((5,)),
            pltpu.SemaphoreType.DMA((device_count // 16,)),
        ],
        pltpu.HBM,
        [
            vintage_gains,
            vintage_traces,
            dest_device.reshape(1, trace_count),
            dest_slot.reshape(1, trace_count),
            vintage_id.reshape(1, trace_count),
        ],
        all_vmem_bytes,
    )
    got = lax.all_to_all(
        sent.reshape(send_rows, 1, 128), ("inline", "xline"), split_axis=0, concat_axis=0, tiled=True
    ).reshape(send_rows, 128)
    words = dictionary.reshape(2, 4, 2, 4, 2, 4, 512).transpose(0, 2, 4, 5, 1, 3, 6).reshape(512, 512)
    words_back = words.T
    base = (
        base_volume.reshape(4, 4, 4, 4, time_len).transpose(0, 2, 1, 3, 4).reshape(256, time_len)
    )
    pair_shape = lambda *lead: jax.ShapeDtypeStruct(lead + (64, 128), jnp.bfloat16)
    whole, half, to_even, to_odd = call_kernel(
        merge_kernel,
        (
            jax.ShapeDtypeStruct((4, 2, 64, 128), jnp.float32),
            pair_shape(2, 4),
            pair_shape(2, 2),
            pair_shape(2, 2),
        ),
        (pltpu.VMEM,) * 4,
        [
            pltpu.VMEM((256, send_rows), jnp.bfloat16),
            pltpu.VMEM((send_rows, 512), jnp.bfloat16),
            pltpu.VMEM((2, 256, 128), jnp.float32),
        ],
        pltpu.VMEM,
        [got, base],
    )

    def swapped(block, axis, odd_pairs):
        count = lax.axis_size(axis)
        partner = [(i + 1 if i % 2 == odd_pairs else i - 1) % count for i in range(count)]
        return lax.ppermute(block, axis, list(enumerate(partner)))

    from_even, from_odd = swapped(to_even, "inline", 0), swapped(to_odd, "inline", 1)
    own_even, own_odd = call_kernel(
        assemble_kernel,
        (pair_shape(7), pair_shape(7)),
        (pltpu.VMEM,) * 2,
        [],
        pltpu.VMEM,
        [half, from_even, from_odd],
    )
    from_even, from_odd = swapped(own_even, "xline", 0), swapped(own_odd, "xline", 1)
    full_shape = lambda *shape: jax.ShapeDtypeStruct(shape, jnp.float32)
    inner, first, recon, rests, later, codes_inner = call_kernel(
        inner_kernel,
        (
            pair_shape(4, 7),
            full_shape(2, 256, 512),
            full_shape(2, 5, 64, 128),
            full_shape(2, 4, 64, 128),
            pair_shape(2, 5),
            full_shape(4, 64, 512),
        ),
        (pltpu.VMEM,) * 6,
        [],
        pltpu.VMEM,
        [whole, own_even, own_odd, words, words_back],
        cost=pl.CostEstimate(flops=1_400_000_000, bytes_accessed=4_000_000, transcendentals=0),
    )
    codes, residual = call_kernel(
        sparse_kernel,
        (full_shape(4, 4, 64, 512), full_shape(256, time_len)),
        (pltpu.HBM, pltpu.HBM),
        [
            pltpu.VMEM((3, 7, 64, 128), jnp.bfloat16),
            pltpu.VMEM((3, 5, 64, 128), jnp.bfloat16),
            pltpu.VMEM((2, 256, 128), jnp.float32),
            pltpu.VMEM((2, 4, 64, 128), jnp.float32),
            pltpu.VMEM((3, 4, 64, 512), jnp.float32),
            pltpu.VMEM((256, time_len), jnp.float32),
            pltpu.SemaphoreType.DMA((6,)),
        ],
        pltpu.VMEM,
        [
            whole, own_even, own_odd, from_even, from_odd, inner, first, recon, rests, later,
            codes_inner, words, words_back,
        ],
    )
    return codes, residual.reshape(16, 16, time_len)


def solution(mesh):
    in_specs = (
        P("inline", "xline", None),
        P(("inline", "xline"), None),
        P(("inline", "xline"), None),
        P(("inline", "xline")),
        P(("inline", "xline")),
        P(),
        P(),
    )
    out_specs = (P("inline", "xline", None, None), P("inline", "xline", None))
    return jax.shard_map(body, mesh=mesh, in_specs=in_specs, out_specs=out_specs, check_vma=False)
```

```python
import math

import jax
import jax.numpy as jnp
from jax import lax
from jax.experimental import pallas as pl
from jax.experimental.pallas import tpu as pltpu
from jax.sharding import PartitionSpec as P

step_size = 0.25
threshold = 0.02
octaves = 40.0
code_top = 32767.0
log_top = math.log2(12.0)
vmem_bytes = 48 * 1024 * 1024
all_vmem_bytes = 64 * 1024 * 1024


def shrink_codes(values):
    return values - jnp.clip(values, -threshold, threshold)


def call_kernel(kernel, out_shape, out_spaces, scratch, in_space, inputs, vmem_limit=vmem_bytes, cost=None):
    return pl.pallas_call(
        kernel,
        out_shape=out_shape,
        in_specs=[pl.BlockSpec(memory_space=in_space)] * len(inputs),
        out_specs=jax.tree.map(lambda space: pl.BlockSpec(memory_space=space), out_spaces),
        scratch_shapes=scratch,
        cost_estimate=cost,
        compiler_params=pltpu.CompilerParams(vmem_limit_bytes=vmem_limit),
    )(*inputs)


def encode(values):
    size = jnp.log2(jnp.maximum(jnp.abs(values), 1e-30))
    code = (size + (octaves - log_top)) * (code_top / octaves)
    code = jnp.clip(jnp.round(code), 0.0, code_top).astype(jnp.int32)
    return jnp.where(values < 0, -code, code)


def decode(code):
    code = code.astype(jnp.float32)
    size = jnp.exp2(jnp.abs(code) * (octaves / code_top) + (log_top - octaves))
    return size * jnp.clip(code, -1.0, 1.0)


def pack_kernel(gains_in, traces_in, dest_in, slot_in, vid_in, out, gains, traces, dest, slot, vid, built, arrive, leave):
    loads = [
        pltpu.make_async_copy(source, target, arrive.at[number])
        for number, (source, target) in enumerate(
            ((dest_in, dest), (slot_in, slot), (gains_in, gains), (vid_in, vid), (traces_in, traces))
        )
    ]
    for load in loads:
        load.start()
    trace_count = traces.shape[0]
    device_count = out.shape[0] // 17
    chunks = trace_count // 128
    me = lax.axis_index("inline") * lax.axis_size("xline") + lax.axis_index("xline")
    loads[0].wait()
    loads[1].wait()
    row = lax.broadcasted_iota(jnp.int32, (128, 128), 0)
    lane = lax.broadcasted_iota(jnp.int32, (128, 128), 1)
    before = jnp.where(row < lane, 1.0, 0.0).astype(jnp.bfloat16)
    carry = jnp.zeros((device_count, 1), jnp.float32)
    places, owners, listed = [], [], []
    for chunk in range(chunks):
        target = dest[:, chunk * 128 : chunk * 128 + 128]
        hit = jnp.where(row == target, 1.0, 0.0)
        hit_half = hit.astype(jnp.bfloat16)
        earlier = jnp.dot(hit_half, before, preferred_element_type=jnp.float32)
        rank = jnp.sum(hit * (earlier + carry), axis=0, keepdims=True)
        carry = carry + jnp.sum(hit, axis=1, keepdims=True)
        rank = rank.astype(jnp.int32)
        places.append(target * 17 + rank)
        owners.append(hit_half)
        wanted = (slot[:, chunk * 128 : chunk * 128 + 128] + 1).astype(jnp.float32)
        spot = lax.rem(17 * me + rank, 128)
        listed.append(jnp.where(row == spot, wanted, 0.0).astype(jnp.bfloat16))
    place = jnp.concatenate(places, axis=1)
    owner = jnp.concatenate(owners, axis=1)
    listing = jnp.concatenate(listed, axis=1)
    slots = lax.dot_general(
        owner, listing, (((1,), (1,)), ((), ())), preferred_element_type=jnp.float32
    ).astype(jnp.int32)

    loads[2].wait()
    loads[3].wait()
    survey = vid[...]
    gain = jnp.zeros(survey.shape, jnp.float32)
    for number in range(gains.shape[0]):
        gain = jnp.where(survey == number, gains[number], gain)
    gain = jnp.transpose(jnp.broadcast_to(gain, (128, trace_count)))
    loads[4].wait()
    high, low = [], []
    for half in range(2):
        code = encode(traces[:, half * 128 : half * 128 + 128] * gain)
        high.append((code >> 8).astype(jnp.float32).astype(jnp.bfloat16))
        low.append((code & 255).astype(jnp.float32).astype(jnp.bfloat16))
    halves = jnp.concatenate(high + low, axis=1)

    owners_each = 16
    rows = owners_each * 17
    index = lax.broadcasted_iota(jnp.int32, (rows, trace_count), 0)
    stores = []
    for block in range(device_count // owners_each):
        pick = jnp.where(index == place - block * rows, 1.0, 0.0).astype(jnp.bfloat16)
        moved = jnp.dot(pick, halves, preferred_element_type=jnp.float32)
        code = (moved[:, :256] * 256.0 + moved[:, 256:]).astype(jnp.int32)
        built[block * rows : block * rows + rows, :] = (code[:, :128] << 16) | (
            code[:, 128:] & 65535
        )
        built[pl.ds(block * rows + 16, owners_each, stride=17), :] = slots[
            block * owners_each : block * owners_each + owners_each
        ]
        spot = pl.ds(block * rows, rows)
        stores.append(pltpu.make_async_copy(built.at[spot], out.at[spot], leave.at[block]))
        stores[-1].start()
    for store in stores:
        store.wait()


def exchanged(four):
    lane = lax.broadcasted_iota(jnp.int32, four[0].shape, 1)

    def crossed(lower, upper, distance):
        keep = (lane // distance) % 2 == 0
        return (
            jnp.where(keep, lower, pltpu.roll(upper, distance, 1)),
            jnp.where(keep, pltpu.roll(lower, 128 - distance, 1), upper),
        )

    (zero, two), (one, three) = crossed(four[0], four[2], 32), crossed(four[1], four[3], 32)
    (zero, one), (two, three) = crossed(zero, one, 16), crossed(two, three, 16)
    return zero, one, two, three


def merge_kernel(got, base, whole, half, to_even, to_odd, turned):
    tiles = got.shape[0] // 128
    bin_row = lax.broadcasted_iota(jnp.int32, (256, 128), 0)
    tile, part, pair, odd = bin_row // 128, (bin_row // 32) % 2, (bin_row // 16) % 2, (bin_row // 64) % 2
    block_row, block_col = 2 * tile + part, 2 * pair + odd
    bin_slot = block_row * 64 + ((bin_row // 4) % 4) * 16 + block_col * 4 + bin_row % 4
    wanted = bin_slot + 1
    listed = got[pl.ds(16, 128, stride=17), :]
    begin = 17 * lax.broadcasted_iota(jnp.int32, (128, 128), 0)
    lane = lax.broadcasted_iota(jnp.int32, (128, 128), 1)
    tile_of = begin // 128 + jnp.where(lane < begin % 128, 1, 0)
    tiles_each = 4
    fold = jnp.zeros((256, 128), jnp.float32)
    stack = jnp.zeros((256, 512), jnp.float32)
    for at in range(0, tiles, tiles_each):
        hits, rows = [], []
        for tile in range(at, min(at + tiles_each, tiles)):
            low_group, high_group = (128 * tile) // 136, min((128 * tile + 127) // 136, 15)
            spot = slice(8 * low_group, 8 * high_group + 8)
            slots = jnp.sum(jnp.where(tile_of[spot] == tile, listed[spot], 0), axis=0, keepdims=True)
            hit = jnp.where(wanted == slots, 1.0, 0.0)
            fold = fold + hit
            hits.append(hit.astype(jnp.bfloat16))
            word = got[128 * tile : 128 * tile + 128, :]
            values = [decode(code) for code in (word >> 16, (word << 16) >> 16)]
            high = [value.astype(jnp.bfloat16) for value in values]
            low = [
                (value - part.astype(jnp.float32)).astype(jnp.bfloat16)
                for value, part in zip(values, high)
            ]
            rows.append(jnp.concatenate(high + low, axis=1))
        stack = stack + jnp.dot(
            jnp.concatenate(hits, axis=1),
            jnp.concatenate(rows, axis=0),
            preferred_element_type=jnp.float32,
        )
    fold = jnp.sum(fold, axis=1, keepdims=True)
    merged = (base[...] + (stack[:, :256] + stack[:, 256:])) / (1.0 + fold)
    turned[0] = jnp.transpose(merged[:128])
    turned[1] = jnp.transpose(merged[128:])
    for tile in range(2):
        slabs = [turned[tile, pl.ds(phase, 64, stride=4), :] for phase in range(4)]
        for number, made in enumerate(exchanged(slabs)):
            part, pair = number // 2, number % 2
            whole[2 * tile + part, pair] = made
            half[pair, 2 * tile + part] = made.astype(jnp.bfloat16)
    odd_device = lax.rem(lax.axis_index("inline"), 2)
    to_even[...] = half[:, pl.ds(2 - 2 * odd_device, 2)]
    to_odd[...] = half[:, pl.ds(2 * odd_device, 2)]


def assemble_kernel(half, from_even, from_odd, to_even, to_odd):
    inline_at = lax.axis_index("inline")
    odd_row = lax.rem(inline_at, 2) == 1
    odd_col = lax.rem(lax.axis_index("xline"), 2)
    for target, pair in ((to_even, 1 - odd_col), (to_odd, odd_col)):
        above = jnp.where(odd_row, from_even[pair, 1], from_odd[pair, 1])
        target[0] = jnp.where(inline_at == 0, jnp.zeros_like(above), above)
        target[1:5] = half[pair]
        below = jnp.where(odd_row, from_odd[pair], from_even[pair])
        last = inline_at == lax.axis_size("inline") - 1
        target[5:7] = jnp.where(last, jnp.zeros_like(below), below)


def time_rolled(values, distance):
    row = lax.broadcasted_iota(jnp.int32, values.shape, 0)
    if distance < 0:
        return jnp.where(row == values.shape[0] - 1, 0.0, pltpu.roll(values, values.shape[0] - 1, 0))
    return jnp.where(row == 0, 0.0, pltpu.roll(values, 1, 0))


def widened(both):
    left = lax.broadcasted_iota(jnp.int32, both.shape, 1) < 64
    later = time_rolled(both, -1)
    even = jnp.where(left, both, pltpu.roll(later, 64, 1))
    odd = jnp.where(left, pltpu.roll(both, 64, 1), later)
    return even.astype(jnp.bfloat16), odd.astype(jnp.bfloat16)


def correlated(near, far, words, first_row, count):
    lhs = [
        source[first_row + shift : first_row + shift + count].reshape(count * 64, 128)
        for shift in (0, 1)
        for source in (near, far)
    ]
    return jnp.dot(jnp.concatenate(lhs, axis=1), words[...], preferred_element_type=jnp.float32)


def given_back(found, words_back, sides):
    given = {}
    for side in sides:
        for shift in (0, 1):
            at = 256 * shift + 128 * side
            given[shift, side] = at
    columns = {}
    if len(sides) == 2:
        full = jnp.dot(found, words_back[...], preferred_element_type=jnp.float32)
        for key, at in given.items():
            columns[key] = full[:, at : at + 128].reshape(6, 64, 128)
    else:
        picked = jnp.concatenate([words_back[:, at : at + 128] for at in given.values()], axis=1)
        full = jnp.dot(found, picked, preferred_element_type=jnp.float32)
        for number, key in enumerate(given):
            columns[key] = full[:, 128 * number : 128 * number + 128].reshape(6, 64, 128)
    return [columns[0, side][1:6] + columns[1, side][0:5] for side in sides]


def rebuilt_half(given, odd):
    moved = pltpu.roll(given, 64, 1)
    return moved + time_rolled(given, 1) if odd else given + time_rolled(moved, 1)


def widened_half(block, odd):
    left = lax.broadcasted_iota(jnp.int32, block.shape, 1) < 64
    later = time_rolled(block, -1)
    if odd:
        return jnp.where(left, pltpu.roll(block, 64, 1), later).astype(jnp.bfloat16)
    return jnp.where(left, block, pltpu.roll(later, 64, 1)).astype(jnp.bfloat16)


def first_codes(near, far, words, not_top):
    found = shrink_codes(step_size * correlated(near, far, words, 0, 6))
    return found[64:320], jnp.concatenate([found[:64] * not_top, found[64:]], axis=0)


def last_codes(before, near, far, words):
    found = before + step_size * correlated(near, far, words, 0, 4)
    return shrink_codes(found).reshape(4, 64, 512)


def inner_kernel(whole, own_even, own_odd, words, words_back, field, first, recon, rests, later, made_codes):
    inline_at = lax.axis_index("inline")
    not_top = jnp.where(inline_at == 0, 0.0, 1.0)
    not_bottom = jnp.where(inline_at == lax.axis_size("inline") - 1, 0.0, 1.0)
    odd_device = lax.rem(lax.axis_index("xline"), 2) == 1

    def loaded(pair, block_row):
        if_even, if_odd = ((own_odd, own_even), (own_even, own_odd))[pair]
        return jnp.where(odd_device, if_odd[block_row], if_even[block_row]).astype(jnp.float32)

    for pair in range(2):
        for block_row in range(7):
            even, odd = widened(loaded(pair, block_row))
            field[2 * pair, block_row] = even
            field[2 * pair + 1, block_row] = odd
    kept, found = zip(
        *(first_codes(field.at[at], field.at[at + 1], words, not_top) for at in range(3))
    )
    given = [given_back(part.astype(jnp.bfloat16), words_back, (0, 1)) for part in found]
    recon[0] = given[0][0]
    recon[1] = given[2][1]
    for column in (1, 2):
        pair, odd = column // 2, column % 2
        for block_row in range(5):
            rebuilt = rebuilt_half(given[column][0][block_row] + given[column - 1][1][block_row], odd)
            if block_row < 4:
                rest = whole[block_row, pair] - rebuilt
                rests[column - 1, block_row] = rest
            else:
                rest = (loaded(pair, 5) - rebuilt) * not_bottom
            later[column - 1, block_row] = widened_half(rest, odd)
    first[0] = kept[0]
    first[1] = kept[2]
    made_codes[...] = last_codes(kept[1], later.at[0], later.at[1], words)


def sparse_kernel(
    whole, own_even, own_odd, from_even, from_odd, inner, first_inner, recon_inner, rests, later_inner,
    codes_inner, words, words_back, codes, residual, outer, later, turned, binned, made_codes, flat_rest, leave
):
    stores = [pltpu.make_async_copy(codes_inner, codes.at[:, 1], leave.at[0])]
    stores[0].start()
    inline_at, xline_at = lax.axis_index("inline"), lax.axis_index("xline")
    inline_last = inline_at == lax.axis_size("inline") - 1
    xline_last = xline_at == lax.axis_size("xline") - 1
    not_top = jnp.where(inline_at == 0, 0.0, 1.0)
    not_left = jnp.where(xline_at == 0, 0.0, 1.0)
    not_bottom = jnp.where(inline_last, 0.0, 1.0)
    not_right = jnp.where(xline_last, 0.0, 1.0)

    odd_device = lax.rem(xline_at, 2) == 1
    sources = ((from_odd, from_even), (own_odd, own_even), (own_even, own_odd), (from_even, from_odd))
    edges = (not_left, None, None, not_right)

    def loaded(pair, block_row):
        if_even, if_odd = sources[pair]
        both = jnp.where(odd_device, if_odd[block_row], if_even[block_row]).astype(jnp.float32)
        return both if edges[pair] is None else both * edges[pair]

    def leaving(column, made):
        made_codes[len(stores) - 1] = made
        for part in range(2 if column == 3 else 1):
            rows = pl.ds(2 * part, 2) if column == 3 else pl.ds(0, 4)
            stores.append(
                pltpu.make_async_copy(
                    made_codes.at[len(stores) - 1 - part, rows],
                    codes.at[rows, column],
                    leave.at[len(stores)],
                )
            )
            stores[-1].start()

    def rest_of(column, given, spot):
        pair, odd = column // 2, column % 2
        for block_row in range(5):
            rebuilt = rebuilt_half(given[block_row], odd)
            if column == 4:
                rest = (loaded(3, block_row + 1) - rebuilt) * not_right
            elif block_row < 4:
                rest = whole[block_row, pair] - rebuilt
                binned[pair, block_row] = rest
            else:
                rest = loaded(pair + 1, 5) - rebuilt
            if block_row == 4:
                rest = rest * not_bottom
            later[spot, block_row] = widened_half(rest, odd)

    for block_row in range(7):
        outer[0, block_row] = widened(loaded(0, block_row))[1]
        even, odd = widened(loaded(3, block_row))
        outer[1, block_row] = even
        outer[2, block_row] = odd
    unused, left_found = first_codes(outer.at[0], inner.at[0], words, not_top)
    kept, middle = first_codes(inner.at[3], outer.at[1], words, not_top)
    unused, right_found = first_codes(outer.at[1], outer.at[2], words, not_top)
    (left_far,) = given_back((left_found * not_left).astype(jnp.bfloat16), words_back, (1,))
    near, far = given_back(middle.astype(jnp.bfloat16), words_back, (0, 1))
    (right_near,) = given_back(right_found.astype(jnp.bfloat16), words_back, (0,))
    rest_of(0, recon_inner[0] + left_far, 0)
    rest_of(3, recon_inner[1] + near, 1)
    rest_of(4, far + right_near, 2)
    leaving(0, last_codes(first_inner[0], later.at[0], later_inner.at[0], words))
    leaving(2, last_codes(first_inner[1], later_inner.at[1], later.at[1], words))
    leaving(3, last_codes(kept, later.at[1], later.at[2], words))
    left = lax.broadcasted_iota(jnp.int32, (64, 128), 1) < 64
    for block_row in range(4):
        binned[0, block_row] = jnp.where(left, binned[0, block_row], rests[0, block_row])
        binned[1, block_row] = jnp.where(left, rests[1, block_row], binned[1, block_row])
    for tile in range(2):
        blocks = [binned[pair, 2 * tile + part] for part in range(2) for pair in range(2)]
        for phase, made in enumerate(exchanged(blocks)):
            turned[tile, pl.ds(phase, 64, stride=4), :] = made
    for tile in range(2):
        flat = jnp.transpose(turned[tile])
        for number in range(8):
            odd, part, pair = number // 4, (number // 2) % 2, number % 2
            for row in range(4):
                at = number * 16 + row * 4
                to = (2 * tile + part) * 64 + row * 16 + (2 * pair + odd) * 4
                flat_rest[to : to + 4, :] = flat[at : at + 4, :]
    stores.append(pltpu.make_async_copy(flat_rest, residual, leave.at[5]))
    stores[-1].start()
    for store in stores:
        store.wait()


def body(
    base_volume, vintage_traces, dest_device, dest_slot, vintage_id, vintage_gains, dictionary
):
    trace_count, time_len = vintage_traces.shape
    device_count = lax.axis_size("inline") * lax.axis_size("xline")
    send_rows = device_count * 17
    sent = call_kernel(
        pack_kernel,
        jax.ShapeDtypeStruct((send_rows, 128), jnp.int32),
        pltpu.HBM,
        [
            pltpu.SMEM(vintage_gains.shape, jnp.float32),
            pltpu.VMEM(vintage_traces.shape, jnp.float32),
            pltpu.VMEM((1, trace_count), jnp.int32),
            pltpu.VMEM((1, trace_count), jnp.int32),
            pltpu.VMEM((1, trace_count), jnp.int32),
            pltpu.VMEM((send_rows, 128), jnp.int32),
            pltpu.SemaphoreType.DMA((5,)),
            pltpu.SemaphoreType.DMA((device_count // 16,)),
        ],
        pltpu.HBM,
        [
            vintage_gains,
            vintage_traces,
            dest_device.reshape(1, trace_count),
            dest_slot.reshape(1, trace_count),
            vintage_id.reshape(1, trace_count),
        ],
        all_vmem_bytes,
    )
    got = lax.all_to_all(
        sent.reshape(send_rows, 1, 128), ("inline", "xline"), split_axis=0, concat_axis=0, tiled=True
    ).reshape(send_rows, 128)
    words = dictionary.reshape(2, 4, 2, 4, 2, 4, 512).transpose(0, 2, 4, 5, 1, 3, 6).reshape(512, 512)
    words_back = words.T
    base = (
        base_volume.reshape(2, 2, 4, 2, 2, 4, time_len)
        .transpose(0, 4, 1, 3, 2, 5, 6)
        .reshape(256, time_len)
    )
    pair_shape = lambda *lead: jax.ShapeDtypeStruct(lead + (64, 128), jnp.bfloat16)
    whole, half, to_even, to_odd = call_kernel(
        merge_kernel,
        (
            jax.ShapeDtypeStruct((4, 2, 64, 128), jnp.float32),
            pair_shape(2, 4),
            pair_shape(2, 2),
            pair_shape(2, 2),
        ),
        (pltpu.VMEM,) * 4,
        [
            pltpu.VMEM((2, 256, 128), jnp.float32),
        ],
        pltpu.VMEM,
        [got, base],
    )

    rows, columns = lax.axis_size("inline"), lax.axis_size("xline")

    def swapped(block, along_rows, odd_pairs):
        route = []
        for row in range(rows):
            for column in range(columns):
                at, count = (row, rows) if along_rows else (column, columns)
                to = at + 1 if at % 2 == odd_pairs else at - 1
                if not 0 <= to < count:
                    partner = (row, column ^ 1) if along_rows else (row ^ 1, column)
                else:
                    partner = (to, column) if along_rows else (row, to)
                route.append((row * columns + column, partner[0] * columns + partner[1]))
        return lax.ppermute(block, ("inline", "xline"), route)

    from_odd = swapped(to_odd, True, 1)
    from_even = swapped(to_even, True, 0)
    own_even, own_odd = call_kernel(
        assemble_kernel,
        (pair_shape(7), pair_shape(7)),
        (pltpu.VMEM,) * 2,
        [],
        pltpu.VMEM,
        [half, from_even, from_odd],
    )
    from_odd = swapped(own_odd, False, 1)
    from_even = swapped(own_even, False, 0)
    full_shape = lambda *shape: jax.ShapeDtypeStruct(shape, jnp.float32)
    inner, first, recon, rests, later, codes_inner = call_kernel(
        inner_kernel,
        (
            pair_shape(4, 7),
            full_shape(2, 256, 512),
            full_shape(2, 5, 64, 128),
            full_shape(2, 4, 64, 128),
            pair_shape(2, 5),
            full_shape(4, 64, 512),
        ),
        (pltpu.VMEM,) * 6,
        [],
        pltpu.VMEM,
        [whole, own_even, own_odd, words, words_back],
        cost=pl.CostEstimate(flops=1_400_000_000, bytes_accessed=4_000_000, transcendentals=0),
    )
    codes, residual = call_kernel(
        sparse_kernel,
        (full_shape(4, 4, 64, 512), full_shape(256, time_len)),
        (pltpu.HBM, pltpu.HBM),
        [
            pltpu.VMEM((3, 7, 64, 128), jnp.bfloat16),
            pltpu.VMEM((3, 5, 64, 128), jnp.bfloat16),
            pltpu.VMEM((2, 256, 128), jnp.float32),
            pltpu.VMEM((2, 4, 64, 128), jnp.float32),
            pltpu.VMEM((3, 4, 64, 512), jnp.float32),
            pltpu.VMEM((256, time_len), jnp.float32),
            pltpu.SemaphoreType.DMA((6,)),
        ],
        pltpu.VMEM,
        [
            whole, own_even, own_odd, from_even, from_odd, inner, first, recon, rests, later,
            codes_inner, words, words_back,
        ],
    )
    return codes, residual.reshape(16, 16, time_len)


def solution(mesh):
    in_specs = (
        P("inline", "xline", None),
        P(("inline", "xline"), None),
        P(("inline", "xline"), None),
        P(("inline", "xline")),
        P(("inline", "xline")),
        P(),
        P(),
    )
    out_specs = (P("inline", "xline", None, None), P("inline", "xline", None))
    return jax.shard_map(body, mesh=mesh, in_specs=in_specs, out_specs=out_specs, check_vma=False)
```

```python
import math

import jax
import jax.numpy as jnp
from jax import lax
from jax.experimental import pallas as pl
from jax.experimental.pallas import tpu as pltpu
from jax.sharding import PartitionSpec as P

step_size = 0.25
threshold = 0.02
octaves = 40.0
code_top = 32767.0
log_top = math.log2(12.0)
vmem_bytes = 48 * 1024 * 1024
all_vmem_bytes = 64 * 1024 * 1024


def shrink_codes(values):
    return values - jnp.clip(values, -threshold, threshold)


def call_kernel(kernel, out_shape, out_spaces, scratch, in_space, inputs, vmem_limit=vmem_bytes, cost=None):
    return pl.pallas_call(
        kernel,
        out_shape=out_shape,
        in_specs=[pl.BlockSpec(memory_space=in_space)] * len(inputs),
        out_specs=jax.tree.map(lambda space: pl.BlockSpec(memory_space=space), out_spaces),
        scratch_shapes=scratch,
        cost_estimate=cost,
        compiler_params=pltpu.CompilerParams(vmem_limit_bytes=vmem_limit),
    )(*inputs)


def encode(values):
    size = jnp.log2(jnp.maximum(jnp.abs(values), 1e-30))
    code = (size + (octaves - log_top)) * (code_top / octaves)
    code = jnp.clip(jnp.round(code), 0.0, code_top).astype(jnp.int32)
    return jnp.where(values < 0, -code, code)


def decode(code):
    code = code.astype(jnp.float32)
    size = jnp.exp2(jnp.abs(code) * (octaves / code_top) + (log_top - octaves))
    return size * jnp.clip(code, -1.0, 1.0)


def pack_kernel(gains_in, traces_in, dest_in, slot_in, vid_in, out, gains, traces, dest, slot, vid, built, words, place, place_at, arrive, leave):
    loads = [
        pltpu.make_async_copy(source, target, arrive.at[number])
        for number, (source, target) in enumerate(
            ((dest_in, dest), (slot_in, slot), (gains_in, gains), (vid_in, vid), (traces_in, traces))
        )
    ]
    for load in loads:
        load.start()
    trace_count = traces.shape[0]
    device_count = out.shape[0] // 17
    built[...] = jnp.zeros_like(built)
    chunks = trace_count // 128
    me = lax.axis_index("inline") * lax.axis_size("xline") + lax.axis_index("xline")
    loads[0].wait()
    loads[1].wait()
    row = lax.broadcasted_iota(jnp.int32, (128, 128), 0)
    lane = lax.broadcasted_iota(jnp.int32, (128, 128), 1)
    before = jnp.where(row < lane, 1.0, 0.0).astype(jnp.bfloat16)
    carry = jnp.zeros((device_count, 1), jnp.float32)
    places, owners, listed = [], [], []
    for chunk in range(chunks):
        target = dest[:, chunk * 128 : chunk * 128 + 128]
        hit = jnp.where(row == target, 1.0, 0.0)
        hit_half = hit.astype(jnp.bfloat16)
        earlier = jnp.dot(hit_half, before, preferred_element_type=jnp.float32)
        rank = jnp.sum(hit * (earlier + carry), axis=0, keepdims=True)
        carry = carry + jnp.sum(hit, axis=1, keepdims=True)
        rank = rank.astype(jnp.int32)
        places.append(target * 17 + rank)
        owners.append(hit_half)
        wanted = (slot[:, chunk * 128 : chunk * 128 + 128] + 1).astype(jnp.float32)
        spot = lax.rem(17 * me + rank, 128)
        listed.append(jnp.where(row == spot, wanted, 0.0).astype(jnp.bfloat16))
    place[...] = jnp.concatenate(places, axis=1)
    put = pltpu.make_async_copy(place, place_at, arrive.at[5])
    put.start()
    owner = jnp.concatenate(owners, axis=1)
    listing = jnp.concatenate(listed, axis=1)
    slots = lax.dot_general(
        owner, listing, (((1,), (1,)), ((), ())), preferred_element_type=jnp.float32
    ).astype(jnp.int32)

    loads[2].wait()
    loads[3].wait()
    survey = vid[...]
    gain = jnp.zeros(survey.shape, jnp.float32)
    for number in range(gains.shape[0]):
        gain = jnp.where(survey == number, gains[number], gain)
    gain = jnp.transpose(jnp.broadcast_to(gain, (128, trace_count)))
    loads[4].wait()
    code = [encode(traces[:, half * 128 : half * 128 + 128] * gain) for half in range(2)]
    words[...] = (code[0] << 16) | (code[1] & 65535)
    built[pl.ds(16, device_count, stride=17), :] = slots
    put.wait()
    for trace in range(trace_count):
        built[pl.ds(place_at[0, trace], 1), :] = words[trace : trace + 1, :]
    send = pltpu.make_async_copy(built, out, leave)
    send.start()
    send.wait()


def exchanged(four):
    lane = lax.broadcasted_iota(jnp.int32, four[0].shape, 1)

    def crossed(lower, upper, distance):
        keep = (lane // distance) % 2 == 0
        return (
            jnp.where(keep, lower, pltpu.roll(upper, distance, 1)),
            jnp.where(keep, pltpu.roll(lower, 128 - distance, 1), upper),
        )

    (zero, two), (one, three) = crossed(four[0], four[2], 32), crossed(four[1], four[3], 32)
    (zero, one), (two, three) = crossed(zero, one, 16), crossed(two, three, 16)
    return zero, one, two, three


def merge_kernel(got, base, whole, half, to_even, to_odd, turned):
    tiles = got.shape[0] // 128
    bin_row = lax.broadcasted_iota(jnp.int32, (256, 128), 0)
    tile, part, pair, odd = bin_row // 128, (bin_row // 32) % 2, (bin_row // 16) % 2, (bin_row // 64) % 2
    block_row, block_col = 2 * tile + part, 2 * pair + odd
    bin_slot = block_row * 64 + ((bin_row // 4) % 4) * 16 + block_col * 4 + bin_row % 4
    wanted = bin_slot + 1
    listed = got[pl.ds(16, 128, stride=17), :]
    begin = 17 * lax.broadcasted_iota(jnp.int32, (128, 128), 0)
    lane = lax.broadcasted_iota(jnp.int32, (128, 128), 1)
    tile_of = begin // 128 + jnp.where(lane < begin % 128, 1, 0)
    tiles_each = 4
    fold = jnp.zeros((256, 128), jnp.float32)
    stack = jnp.zeros((256, 512), jnp.float32)
    for at in range(0, tiles, tiles_each):
        hits, rows = [], []
        for tile in range(at, min(at + tiles_each, tiles)):
            low_group, high_group = (128 * tile) // 136, min((128 * tile + 127) // 136, 15)
            spot = slice(8 * low_group, 8 * high_group + 8)
            slots = jnp.sum(jnp.where(tile_of[spot] == tile, listed[spot], 0), axis=0, keepdims=True)
            hit = jnp.where(wanted == slots, 1.0, 0.0)
            fold = fold + hit
            hits.append(hit.astype(jnp.bfloat16))
            word = got[128 * tile : 128 * tile + 128, :]
            values = [decode(code) for code in (word >> 16, (word << 16) >> 16)]
            high = [value.astype(jnp.bfloat16) for value in values]
            low = [
                (value - part.astype(jnp.float32)).astype(jnp.bfloat16)
                for value, part in zip(values, high)
            ]
            rows.append(jnp.concatenate(high + low, axis=1))
        stack = stack + jnp.dot(
            jnp.concatenate(hits, axis=1),
            jnp.concatenate(rows, axis=0),
            preferred_element_type=jnp.float32,
        )
    fold = jnp.sum(fold, axis=1, keepdims=True)
    merged = (base[...] + (stack[:, :256] + stack[:, 256:])) / (1.0 + fold)
    turned[0] = jnp.transpose(merged[:128])
    turned[1] = jnp.transpose(merged[128:])
    for tile in range(2):
        slabs = [turned[tile, pl.ds(phase, 64, stride=4), :] for phase in range(4)]
        for number, made in enumerate(exchanged(slabs)):
            part, pair = number // 2, number % 2
            whole[2 * tile + part, pair] = made
            half[pair, 2 * tile + part] = made.astype(jnp.bfloat16)
    odd_device = lax.rem(lax.axis_index("inline"), 2)
    to_even[...] = half[:, pl.ds(2 - 2 * odd_device, 2)]
    to_odd[...] = half[:, pl.ds(2 * odd_device, 2)]


def assemble_kernel(half, from_even, from_odd, to_even, to_odd):
    inline_at = lax.axis_index("inline")
    odd_row = lax.rem(inline_at, 2) == 1
    odd_col = lax.rem(lax.axis_index("xline"), 2)
    for target, pair in ((to_even, 1 - odd_col), (to_odd, odd_col)):
        above = jnp.where(odd_row, from_even[pair, 1], from_odd[pair, 1])
        target[0] = jnp.where(inline_at == 0, jnp.zeros_like(above), above)
        target[1:5] = half[pair]
        below = jnp.where(odd_row, from_odd[pair], from_even[pair])
        last = inline_at == lax.axis_size("inline") - 1
        target[5:7] = jnp.where(last, jnp.zeros_like(below), below)


def time_rolled(values, distance):
    row = lax.broadcasted_iota(jnp.int32, values.shape, 0)
    if distance < 0:
        return jnp.where(row == values.shape[0] - 1, 0.0, pltpu.roll(values, values.shape[0] - 1, 0))
    return jnp.where(row == 0, 0.0, pltpu.roll(values, 1, 0))


def widened(both):
    left = lax.broadcasted_iota(jnp.int32, both.shape, 1) < 64
    later = time_rolled(both, -1)
    even = jnp.where(left, both, pltpu.roll(later, 64, 1))
    odd = jnp.where(left, pltpu.roll(both, 64, 1), later)
    return even.astype(jnp.bfloat16), odd.astype(jnp.bfloat16)


def correlated(near, far, words, first_row, count):
    lhs = [
        source[first_row + shift : first_row + shift + count].reshape(count * 64, 128)
        for shift in (0, 1)
        for source in (near, far)
    ]
    return jnp.dot(jnp.concatenate(lhs, axis=1), words[...], preferred_element_type=jnp.float32)


def given_back(found, words_back, sides):
    given = {}
    for side in sides:
        for shift in (0, 1):
            at = 256 * shift + 128 * side
            given[shift, side] = at
    columns = {}
    if len(sides) == 2:
        full = jnp.dot(found, words_back[...], preferred_element_type=jnp.float32)
        for key, at in given.items():
            columns[key] = full[:, at : at + 128].reshape(6, 64, 128)
    else:
        picked = jnp.concatenate([words_back[:, at : at + 128] for at in given.values()], axis=1)
        full = jnp.dot(found, picked, preferred_element_type=jnp.float32)
        for number, key in enumerate(given):
            columns[key] = full[:, 128 * number : 128 * number + 128].reshape(6, 64, 128)
    return [columns[0, side][1:6] + columns[1, side][0:5] for side in sides]


def rebuilt_half(given, odd):
    moved = pltpu.roll(given, 64, 1)
    return moved + time_rolled(given, 1) if odd else given + time_rolled(moved, 1)


def widened_half(block, odd):
    left = lax.broadcasted_iota(jnp.int32, block.shape, 1) < 64
    later = time_rolled(block, -1)
    if odd:
        return jnp.where(left, pltpu.roll(block, 64, 1), later).astype(jnp.bfloat16)
    return jnp.where(left, block, pltpu.roll(later, 64, 1)).astype(jnp.bfloat16)


def first_codes(near, far, words, not_top):
    found = shrink_codes(correlated(near, far, words, 0, 6))
    return found[64:320], jnp.concatenate([found[:64] * not_top, found[64:]], axis=0)


def last_codes(before, near, far, words):
    return shrink_codes(before + correlated(near, far, words, 0, 4)).reshape(4, 64, 512)


def inner_kernel(whole, own_even, own_odd, words, words_back, field, first, recon, rests, later, made_codes):
    inline_at = lax.axis_index("inline")
    not_top = jnp.where(inline_at == 0, 0.0, 1.0)
    not_bottom = jnp.where(inline_at == lax.axis_size("inline") - 1, 0.0, 1.0)
    odd_device = lax.rem(lax.axis_index("xline"), 2) == 1

    def loaded(pair, block_row):
        if_even, if_odd = ((own_odd, own_even), (own_even, own_odd))[pair]
        return jnp.where(odd_device, if_odd[block_row], if_even[block_row]).astype(jnp.float32)

    for pair in range(2):
        for block_row in range(7):
            even, odd = widened(loaded(pair, block_row))
            field[2 * pair, block_row] = even
            field[2 * pair + 1, block_row] = odd
    kept, found = zip(
        *(first_codes(field.at[at], field.at[at + 1], words, not_top) for at in range(3))
    )
    given = [given_back(part.astype(jnp.bfloat16), words_back, (0, 1)) for part in found]
    recon[0] = given[0][0]
    recon[1] = given[2][1]
    for column in (1, 2):
        pair, odd = column // 2, column % 2
        for block_row in range(5):
            rebuilt = rebuilt_half(given[column][0][block_row] + given[column - 1][1][block_row], odd)
            if block_row < 4:
                rest = whole[block_row, pair] - rebuilt
                rests[column - 1, block_row] = rest
            else:
                rest = (loaded(pair, 5) - rebuilt) * not_bottom
            later[column - 1, block_row] = widened_half(rest, odd)
    first[0] = kept[0]
    first[1] = kept[2]
    made_codes[...] = last_codes(kept[1], later.at[0], later.at[1], words)


def sparse_kernel(
    whole, own_even, own_odd, from_even, from_odd, inner, first_inner, recon_inner, rests, later_inner,
    codes_inner, words, words_back, codes, residual, outer, later, turned, binned, made_codes, flat_rest, leave
):
    stores = [pltpu.make_async_copy(codes_inner, codes.at[:, 1], leave.at[0])]
    stores[0].start()
    inline_at, xline_at = lax.axis_index("inline"), lax.axis_index("xline")
    inline_last = inline_at == lax.axis_size("inline") - 1
    xline_last = xline_at == lax.axis_size("xline") - 1
    not_top = jnp.where(inline_at == 0, 0.0, 1.0)
    not_left = jnp.where(xline_at == 0, 0.0, 1.0)
    not_bottom = jnp.where(inline_last, 0.0, 1.0)
    not_right = jnp.where(xline_last, 0.0, 1.0)

    odd_device = lax.rem(xline_at, 2) == 1
    sources = ((from_odd, from_even), (own_odd, own_even), (own_even, own_odd), (from_even, from_odd))
    edges = (not_left, None, None, not_right)

    def loaded(pair, block_row):
        if_even, if_odd = sources[pair]
        both = jnp.where(odd_device, if_odd[block_row], if_even[block_row]).astype(jnp.float32)
        return both if edges[pair] is None else both * edges[pair]

    def leaving(column, made):
        made_codes[len(stores) - 1] = made
        for part in range(2 if column == 3 else 1):
            rows = pl.ds(2 * part, 2) if column == 3 else pl.ds(0, 4)
            stores.append(
                pltpu.make_async_copy(
                    made_codes.at[len(stores) - 1 - part, rows],
                    codes.at[rows, column],
                    leave.at[len(stores)],
                )
            )
            stores[-1].start()

    def rest_of(column, given, spot):
        pair, odd = column // 2, column % 2
        for block_row in range(5):
            rebuilt = rebuilt_half(given[block_row], odd)
            if column == 4:
                rest = (loaded(3, block_row + 1) - rebuilt) * not_right
            elif block_row < 4:
                rest = whole[block_row, pair] - rebuilt
                binned[pair, block_row] = rest
            else:
                rest = loaded(pair + 1, 5) - rebuilt
            if block_row == 4:
                rest = rest * not_bottom
            later[spot, block_row] = widened_half(rest, odd)

    for block_row in range(7):
        outer[0, block_row] = widened(loaded(0, block_row))[1]
        even, odd = widened(loaded(3, block_row))
        outer[1, block_row] = even
        outer[2, block_row] = odd
    unused, left_found = first_codes(outer.at[0], inner.at[0], words, not_top)
    kept, middle = first_codes(inner.at[3], outer.at[1], words, not_top)
    unused, right_found = first_codes(outer.at[1], outer.at[2], words, not_top)
    (left_far,) = given_back((left_found * not_left).astype(jnp.bfloat16), words_back, (1,))
    near, far = given_back(middle.astype(jnp.bfloat16), words_back, (0, 1))
    (right_near,) = given_back(right_found.astype(jnp.bfloat16), words_back, (0,))
    rest_of(0, recon_inner[0] + left_far, 0)
    rest_of(3, recon_inner[1] + near, 1)
    rest_of(4, far + right_near, 2)
    leaving(0, last_codes(first_inner[0], later.at[0], later_inner.at[0], words))
    leaving(2, last_codes(first_inner[1], later_inner.at[1], later.at[1], words))
    leaving(3, last_codes(kept, later.at[1], later.at[2], words))
    left = lax.broadcasted_iota(jnp.int32, (64, 128), 1) < 64
    for block_row in range(4):
        binned[0, block_row] = jnp.where(left, binned[0, block_row], rests[0, block_row])
        binned[1, block_row] = jnp.where(left, rests[1, block_row], binned[1, block_row])
    for tile in range(2):
        blocks = [binned[pair, 2 * tile + part] for part in range(2) for pair in range(2)]
        for phase, made in enumerate(exchanged(blocks)):
            turned[tile, pl.ds(phase, 64, stride=4), :] = made
    for tile in range(2):
        flat = jnp.transpose(turned[tile])
        for number in range(8):
            odd, part, pair = number // 4, (number // 2) % 2, number % 2
            for row in range(4):
                at = number * 16 + row * 4
                to = (2 * tile + part) * 64 + row * 16 + (2 * pair + odd) * 4
                flat_rest[to : to + 4, :] = flat[at : at + 4, :]
    stores.append(pltpu.make_async_copy(flat_rest, residual, leave.at[5]))
    stores[-1].start()
    for store in stores:
        store.wait()


def body(
    base_volume, vintage_traces, dest_device, dest_slot, vintage_id, vintage_gains, dictionary
):
    trace_count, time_len = vintage_traces.shape
    device_count = lax.axis_size("inline") * lax.axis_size("xline")
    send_rows = device_count * 17
    sent = call_kernel(
        pack_kernel,
        jax.ShapeDtypeStruct((send_rows, 128), jnp.int32),
        pltpu.HBM,
        [
            pltpu.SMEM(vintage_gains.shape, jnp.float32),
            pltpu.VMEM(vintage_traces.shape, jnp.float32),
            pltpu.VMEM((1, trace_count), jnp.int32),
            pltpu.VMEM((1, trace_count), jnp.int32),
            pltpu.VMEM((1, trace_count), jnp.int32),
            pltpu.VMEM((send_rows, 128), jnp.int32),
            pltpu.VMEM((trace_count, 128), jnp.int32),
            pltpu.VMEM((1, trace_count), jnp.int32),
            pltpu.SMEM((1, trace_count), jnp.int32),
            pltpu.SemaphoreType.DMA((6,)),
            pltpu.SemaphoreType.DMA,
        ],
        pltpu.HBM,
        [
            vintage_gains,
            vintage_traces,
            dest_device.reshape(1, trace_count),
            dest_slot.reshape(1, trace_count),
            vintage_id.reshape(1, trace_count),
        ],
        all_vmem_bytes,
    )
    got = lax.all_to_all(
        sent.reshape(send_rows, 1, 128), ("inline", "xline"), split_axis=0, concat_axis=0, tiled=True
    ).reshape(send_rows, 128)
    words = dictionary.reshape(2, 4, 2, 4, 2, 4, 512).transpose(0, 2, 4, 5, 1, 3, 6).reshape(512, 512)
    words_back = words.T
    words = words * jnp.bfloat16(step_size)
    base = (
        base_volume.reshape(2, 2, 4, 2, 2, 4, time_len)
        .transpose(0, 4, 1, 3, 2, 5, 6)
        .reshape(256, time_len)
    )
    got, base, words, words_back = lax.optimization_barrier((got, base, words, words_back))
    pair_shape = lambda *lead: jax.ShapeDtypeStruct(lead + (64, 128), jnp.bfloat16)
    whole, half, to_even, to_odd = call_kernel(
        merge_kernel,
        (
            jax.ShapeDtypeStruct((4, 2, 64, 128), jnp.float32),
            pair_shape(2, 4),
            pair_shape(2, 2),
            pair_shape(2, 2),
        ),
        (pltpu.VMEM,) * 4,
        [
            pltpu.VMEM((2, 256, 128), jnp.float32),
        ],
        pltpu.VMEM,
        [got, base],
    )

    rows, columns = lax.axis_size("inline"), lax.axis_size("xline")

    def swapped(block, along_rows, odd_pairs):
        route = []
        for row in range(rows):
            for column in range(columns):
                at, count = (row, rows) if along_rows else (column, columns)
                to = at + 1 if at % 2 == odd_pairs else at - 1
                if not 0 <= to < count:
                    partner = (row, column ^ 1) if along_rows else (row ^ 1, column)
                else:
                    partner = (to, column) if along_rows else (row, to)
                route.append((row * columns + column, partner[0] * columns + partner[1]))
        return lax.ppermute(block, ("inline", "xline"), route)

    from_odd = swapped(to_odd, True, 1)
    from_even = swapped(to_even, True, 0)
    own_even, own_odd = call_kernel(
        assemble_kernel,
        (pair_shape(7), pair_shape(7)),
        (pltpu.VMEM,) * 2,
        [],
        pltpu.VMEM,
        [half, from_even, from_odd],
    )
    from_odd = swapped(own_odd, False, 1)
    from_even = swapped(own_even, False, 0)
    full_shape = lambda *shape: jax.ShapeDtypeStruct(shape, jnp.float32)
    inner, first, recon, rests, later, codes_inner = call_kernel(
        inner_kernel,
        (
            pair_shape(4, 7),
            full_shape(2, 256, 512),
            full_shape(2, 5, 64, 128),
            full_shape(2, 4, 64, 128),
            pair_shape(2, 5),
            full_shape(4, 64, 512),
        ),
        (pltpu.VMEM,) * 6,
        [],
        pltpu.VMEM,
        [whole, own_even, own_odd, words, words_back],
        cost=pl.CostEstimate(flops=1_400_000_000, bytes_accessed=4_000_000, transcendentals=0),
    )
    codes, residual = call_kernel(
        sparse_kernel,
        (full_shape(4, 4, 64, 512), full_shape(256, time_len)),
        (pltpu.HBM, pltpu.HBM),
        [
            pltpu.VMEM((3, 7, 64, 128), jnp.bfloat16),
            pltpu.VMEM((3, 5, 64, 128), jnp.bfloat16),
            pltpu.VMEM((2, 256, 128), jnp.float32),
            pltpu.VMEM((2, 4, 64, 128), jnp.float32),
            pltpu.VMEM((3, 4, 64, 512), jnp.float32),
            pltpu.VMEM((256, time_len), jnp.float32),
            pltpu.SemaphoreType.DMA((6,)),
        ],
        pltpu.VMEM,
        [
            whole, own_even, own_odd, from_even, from_odd, inner, first, recon, rests, later,
            codes_inner, words, words_back,
        ],
    )
    return codes, residual.reshape(16, 16, time_len)


def solution(mesh):
    in_specs = (
        P("inline", "xline", None),
        P(("inline", "xline"), None),
        P(("inline", "xline"), None),
        P(("inline", "xline")),
        P(("inline", "xline")),
        P(),
        P(),
    )
    out_specs = (P("inline", "xline", None, None), P("inline", "xline", None))
    return jax.shard_map(body, mesh=mesh, in_specs=in_specs, out_specs=out_specs, check_vma=False)
```

```python
import math

import jax
import jax.numpy as jnp
from jax import lax
from jax.experimental import pallas as pl
from jax.experimental.pallas import tpu as pltpu
from jax.sharding import PartitionSpec as P

step_size = 0.25
threshold = 0.02
octaves = 40.0
code_top = 32767.0
log_top = math.log2(12.0)
vmem_bytes = 48 * 1024 * 1024
all_vmem_bytes = 64 * 1024 * 1024


def shrink_codes(values):
    return values - jnp.clip(values, -threshold, threshold)


def call_kernel(kernel, out_shape, out_spaces, scratch, in_space, inputs, vmem_limit=vmem_bytes, cost=None):
    return pl.pallas_call(
        kernel,
        out_shape=out_shape,
        in_specs=[pl.BlockSpec(memory_space=in_space)] * len(inputs),
        out_specs=jax.tree.map(lambda space: pl.BlockSpec(memory_space=space), out_spaces),
        scratch_shapes=scratch,
        cost_estimate=cost,
        compiler_params=pltpu.CompilerParams(vmem_limit_bytes=vmem_limit),
    )(*inputs)


def encode(values):
    size = jnp.log2(jnp.maximum(jnp.abs(values), 1e-30))
    code = (size + (octaves - log_top)) * (code_top / octaves)
    code = jnp.clip(jnp.round(code), 0.0, code_top).astype(jnp.int32)
    return jnp.where(values < 0, -code, code)


def decode(code):
    code = code.astype(jnp.float32)
    size = jnp.exp2(jnp.abs(code) * (octaves / code_top) + (log_top - octaves))
    return size * jnp.clip(code, -1.0, 1.0)


def pack_kernel(gains_in, traces_in, dest_in, slot_in, vid_in, out, gains, traces, dest, slot, vid, built, words, place, place_at, arrive, leave):
    loads = [
        pltpu.make_async_copy(source, target, arrive.at[number])
        for number, (source, target) in enumerate(
            ((dest_in, dest), (slot_in, slot), (gains_in, gains), (vid_in, vid), (traces_in, traces))
        )
    ]
    for load in loads:
        load.start()
    trace_count = traces.shape[0]
    device_count = out.shape[0] // 17
    built[...] = jnp.zeros_like(built)
    chunks = trace_count // 128
    me = lax.axis_index("inline") * lax.axis_size("xline") + lax.axis_index("xline")
    loads[0].wait()
    loads[1].wait()
    row = lax.broadcasted_iota(jnp.int32, (128, 128), 0)
    lane = lax.broadcasted_iota(jnp.int32, (128, 128), 1)
    before = jnp.where(row < lane, 1.0, 0.0).astype(jnp.bfloat16)
    carry = jnp.zeros((device_count, 1), jnp.float32)
    places, owners, listed = [], [], []
    for chunk in range(chunks):
        target = dest[:, chunk * 128 : chunk * 128 + 128]
        hit = jnp.where(row == target, 1.0, 0.0)
        hit_half = hit.astype(jnp.bfloat16)
        earlier = jnp.dot(hit_half, before, preferred_element_type=jnp.float32)
        rank = jnp.sum(hit * (earlier + carry), axis=0, keepdims=True)
        carry = carry + jnp.sum(hit, axis=1, keepdims=True)
        rank = rank.astype(jnp.int32)
        places.append(target * 17 + rank)
        owners.append(hit_half)
        wanted = (slot[:, chunk * 128 : chunk * 128 + 128] + 1).astype(jnp.float32)
        spot = lax.rem(17 * me + rank, 128)
        listed.append(jnp.where(row == spot, wanted, 0.0).astype(jnp.bfloat16))
    place[...] = jnp.concatenate(places, axis=1)
    put = pltpu.make_async_copy(place, place_at, arrive.at[5])
    put.start()
    owner = jnp.concatenate(owners, axis=1)
    listing = jnp.concatenate(listed, axis=1)
    slots = lax.dot_general(
        owner, listing, (((1,), (1,)), ((), ())), preferred_element_type=jnp.float32
    ).astype(jnp.int32)

    loads[2].wait()
    loads[3].wait()
    survey = vid[...]
    gain = jnp.zeros(survey.shape, jnp.float32)
    for number in range(gains.shape[0]):
        gain = jnp.where(survey == number, gains[number], gain)
    gain = jnp.transpose(jnp.broadcast_to(gain, (128, trace_count)))
    loads[4].wait()
    code = [encode(traces[:, half * 128 : half * 128 + 128] * gain) for half in range(2)]
    words[...] = (code[0] << 16) | (code[1] & 65535)
    built[pl.ds(16, device_count, stride=17), :] = slots
    put.wait()
    for trace in range(trace_count):
        built[pl.ds(place_at[0, trace], 1), :] = words[trace : trace + 1, :]
    send = pltpu.make_async_copy(built, out, leave)
    send.start()
    send.wait()


def exchanged(four):
    lane = lax.broadcasted_iota(jnp.int32, four[0].shape, 1)

    def crossed(lower, upper, distance):
        keep = (lane // distance) % 2 == 0
        return (
            jnp.where(keep, lower, pltpu.roll(upper, distance, 1)),
            jnp.where(keep, pltpu.roll(lower, 128 - distance, 1), upper),
        )

    (zero, two), (one, three) = crossed(four[0], four[2], 32), crossed(four[1], four[3], 32)
    (zero, one), (two, three) = crossed(zero, one, 16), crossed(two, three, 16)
    return zero, one, two, three


def merge_kernel(got, base, to_odd, to_even, half, whole, turned):
    tiles = got.shape[0] // 128
    bin_row = lax.broadcasted_iota(jnp.int32, (256, 128), 0)
    tile, part, pair, odd = bin_row // 128, (bin_row // 32) % 2, (bin_row // 16) % 2, (bin_row // 64) % 2
    block_row, block_col = 2 * tile + part, 2 * pair + odd
    bin_slot = block_row * 64 + ((bin_row // 4) % 4) * 16 + block_col * 4 + bin_row % 4
    wanted = bin_slot + 1
    listed = got[pl.ds(16, 128, stride=17), :]
    begin = 17 * lax.broadcasted_iota(jnp.int32, (128, 128), 0)
    lane = lax.broadcasted_iota(jnp.int32, (128, 128), 1)
    tile_of = begin // 128 + jnp.where(lane < begin % 128, 1, 0)
    tiles_each = 4
    fold = jnp.zeros((256, 128), jnp.float32)
    stack = jnp.zeros((256, 512), jnp.float32)
    for at in range(0, tiles, tiles_each):
        hits, rows = [], []
        for tile in range(at, min(at + tiles_each, tiles)):
            low_group, high_group = (128 * tile) // 136, min((128 * tile + 127) // 136, 15)
            spot = slice(8 * low_group, 8 * high_group + 8)
            slots = jnp.sum(jnp.where(tile_of[spot] == tile, listed[spot], 0), axis=0, keepdims=True)
            hit = jnp.where(wanted == slots, 1.0, 0.0)
            fold = fold + hit
            hits.append(hit.astype(jnp.bfloat16))
            word = got[128 * tile : 128 * tile + 128, :]
            values = [decode(code) for code in (word >> 16, (word << 16) >> 16)]
            high = [value.astype(jnp.bfloat16) for value in values]
            low = [
                (value - part.astype(jnp.float32)).astype(jnp.bfloat16)
                for value, part in zip(values, high)
            ]
            rows.append(jnp.concatenate(high + low, axis=1))
        stack = stack + jnp.dot(
            jnp.concatenate(hits, axis=1),
            jnp.concatenate(rows, axis=0),
            preferred_element_type=jnp.float32,
        )
    fold = jnp.sum(fold, axis=1, keepdims=True)
    merged = (base[...] + (stack[:, :256] + stack[:, 256:])) / (1.0 + fold)
    turned[0] = jnp.transpose(merged[:128])
    turned[1] = jnp.transpose(merged[128:])
    for tile in range(2):
        slabs = [turned[tile, pl.ds(phase, 64, stride=4), :] for phase in range(4)]
        for number, made in enumerate(exchanged(slabs)):
            part, pair = number // 2, number % 2
            whole[2 * tile + part, pair] = made
            half[pair, 2 * tile + part] = made.astype(jnp.bfloat16)
    odd_device = lax.rem(lax.axis_index("inline"), 2)
    to_even[...] = half[:, pl.ds(2 - 2 * odd_device, 2)]
    to_odd[...] = half[:, pl.ds(2 * odd_device, 2)]


def assemble_kernel(from_odd, from_even, half, to_odd, to_even):
    inline_at = lax.axis_index("inline")
    odd_row = lax.rem(inline_at, 2) == 1
    odd_col = lax.rem(lax.axis_index("xline"), 2)
    for target, pair in ((to_even, 1 - odd_col), (to_odd, odd_col)):
        above = jnp.where(odd_row, from_even[pair, 1], from_odd[pair, 1])
        target[0] = jnp.where(inline_at == 0, jnp.zeros_like(above), above)
        target[1:5] = half[pair]
        below = jnp.where(odd_row, from_odd[pair], from_even[pair])
        last = inline_at == lax.axis_size("inline") - 1
        target[5:7] = jnp.where(last, jnp.zeros_like(below), below)


def time_rolled(values, distance):
    row = lax.broadcasted_iota(jnp.int32, values.shape, 0)
    if distance < 0:
        return jnp.where(row == values.shape[0] - 1, 0.0, pltpu.roll(values, values.shape[0] - 1, 0))
    return jnp.where(row == 0, 0.0, pltpu.roll(values, 1, 0))


def widened(both):
    left = lax.broadcasted_iota(jnp.int32, both.shape, 1) < 64
    later = time_rolled(both, -1)
    even = jnp.where(left, both, pltpu.roll(later, 64, 1))
    odd = jnp.where(left, pltpu.roll(both, 64, 1), later)
    return even.astype(jnp.bfloat16), odd.astype(jnp.bfloat16)


def correlated(near, far, words, first_row, count):
    lhs = [
        source[first_row + shift : first_row + shift + count].reshape(count * 64, 128)
        for shift in (0, 1)
        for source in (near, far)
    ]
    return jnp.dot(jnp.concatenate(lhs, axis=1), words[...], preferred_element_type=jnp.float32)


def given_back(found, words_back, sides):
    given = {}
    for side in sides:
        for shift in (0, 1):
            at = 256 * shift + 128 * side
            given[shift, side] = at
    columns = {}
    if len(sides) == 2:
        full = jnp.dot(found, words_back[...], preferred_element_type=jnp.float32)
        for key, at in given.items():
            columns[key] = full[:, at : at + 128].reshape(6, 64, 128)
    else:
        picked = jnp.concatenate([words_back[:, at : at + 128] for at in given.values()], axis=1)
        full = jnp.dot(found, picked, preferred_element_type=jnp.float32)
        for number, key in enumerate(given):
            columns[key] = full[:, 128 * number : 128 * number + 128].reshape(6, 64, 128)
    return [columns[0, side][1:6] + columns[1, side][0:5] for side in sides]


def rebuilt_half(given, odd):
    moved = pltpu.roll(given, 64, 1)
    return moved + time_rolled(given, 1) if odd else given + time_rolled(moved, 1)


def widened_half(block, odd):
    left = lax.broadcasted_iota(jnp.int32, block.shape, 1) < 64
    later = time_rolled(block, -1)
    if odd:
        return jnp.where(left, pltpu.roll(block, 64, 1), later).astype(jnp.bfloat16)
    return jnp.where(left, block, pltpu.roll(later, 64, 1)).astype(jnp.bfloat16)


def first_codes(near, far, words, not_top):
    found = shrink_codes(correlated(near, far, words, 0, 6))
    return found[64:320], jnp.concatenate([found[:64] * not_top, found[64:]], axis=0)


def last_codes(before, near, far, words):
    return shrink_codes(before + correlated(near, far, words, 0, 4)).reshape(4, 64, 512)


def inner_kernel(whole, own_even, own_odd, words, words_back, field, first, recon, rests, later, made_codes):
    inline_at = lax.axis_index("inline")
    not_top = jnp.where(inline_at == 0, 0.0, 1.0)
    not_bottom = jnp.where(inline_at == lax.axis_size("inline") - 1, 0.0, 1.0)
    odd_device = lax.rem(lax.axis_index("xline"), 2) == 1

    def loaded(pair, block_row):
        if_even, if_odd = ((own_odd, own_even), (own_even, own_odd))[pair]
        return jnp.where(odd_device, if_odd[block_row], if_even[block_row]).astype(jnp.float32)

    for pair in range(2):
        for block_row in range(7):
            even, odd = widened(loaded(pair, block_row))
            field[2 * pair, block_row] = even
            field[2 * pair + 1, block_row] = odd
    kept, found = zip(
        *(first_codes(field.at[at], field.at[at + 1], words, not_top) for at in range(3))
    )
    given = [given_back(part.astype(jnp.bfloat16), words_back, (0, 1)) for part in found]
    recon[0] = given[0][0]
    recon[1] = given[2][1]
    for column in (1, 2):
        pair, odd = column // 2, column % 2
        for block_row in range(5):
            rebuilt = rebuilt_half(given[column][0][block_row] + given[column - 1][1][block_row], odd)
            if block_row < 4:
                rest = whole[block_row, pair] - rebuilt
                rests[column - 1, block_row] = rest
            else:
                rest = (loaded(pair, 5) - rebuilt) * not_bottom
            later[column - 1, block_row] = widened_half(rest, odd)
    first[0] = kept[0]
    first[1] = kept[2]
    made_codes[...] = last_codes(kept[1], later.at[0], later.at[1], words)


def sparse_kernel(
    from_odd, from_even, whole, own_even, own_odd, inner, first_inner, recon_inner, rests, later_inner,
    codes_inner, words, words_back, codes, residual, outer, later, turned, binned, made_codes, flat_rest, leave
):
    stores = [pltpu.make_async_copy(codes_inner, codes.at[:, 1], leave.at[0])]
    stores[0].start()
    inline_at, xline_at = lax.axis_index("inline"), lax.axis_index("xline")
    inline_last = inline_at == lax.axis_size("inline") - 1
    xline_last = xline_at == lax.axis_size("xline") - 1
    not_top = jnp.where(inline_at == 0, 0.0, 1.0)
    not_left = jnp.where(xline_at == 0, 0.0, 1.0)
    not_bottom = jnp.where(inline_last, 0.0, 1.0)
    not_right = jnp.where(xline_last, 0.0, 1.0)

    odd_device = lax.rem(xline_at, 2) == 1
    sources = ((from_odd, from_even), (own_odd, own_even), (own_even, own_odd), (from_even, from_odd))
    edges = (not_left, None, None, not_right)

    def loaded(pair, block_row):
        if_even, if_odd = sources[pair]
        both = jnp.where(odd_device, if_odd[block_row], if_even[block_row]).astype(jnp.float32)
        return both if edges[pair] is None else both * edges[pair]

    def leaving(column, made):
        made_codes[len(stores) - 1] = made
        for part in range(2 if column == 3 else 1):
            rows = pl.ds(2 * part, 2) if column == 3 else pl.ds(0, 4)
            stores.append(
                pltpu.make_async_copy(
                    made_codes.at[len(stores) - 1 - part, rows],
                    codes.at[rows, column],
                    leave.at[len(stores)],
                )
            )
            stores[-1].start()

    def rest_of(column, given, spot):
        pair, odd = column // 2, column % 2
        for block_row in range(5):
            rebuilt = rebuilt_half(given[block_row], odd)
            if column == 4:
                rest = (loaded(3, block_row + 1) - rebuilt) * not_right
            elif block_row < 4:
                rest = whole[block_row, pair] - rebuilt
                binned[pair, block_row] = rest
            else:
                rest = loaded(pair + 1, 5) - rebuilt
            if block_row == 4:
                rest = rest * not_bottom
            later[spot, block_row] = widened_half(rest, odd)

    for block_row in range(7):
        outer[0, block_row] = widened(loaded(0, block_row))[1]
        even, odd = widened(loaded(3, block_row))
        outer[1, block_row] = even
        outer[2, block_row] = odd
    unused, left_found = first_codes(outer.at[0], inner.at[0], words, not_top)
    kept, middle = first_codes(inner.at[3], outer.at[1], words, not_top)
    unused, right_found = first_codes(outer.at[1], outer.at[2], words, not_top)
    (left_far,) = given_back((left_found * not_left).astype(jnp.bfloat16), words_back, (1,))
    near, far = given_back(middle.astype(jnp.bfloat16), words_back, (0, 1))
    (right_near,) = given_back(right_found.astype(jnp.bfloat16), words_back, (0,))
    rest_of(0, recon_inner[0] + left_far, 0)
    rest_of(3, recon_inner[1] + near, 1)
    rest_of(4, far + right_near, 2)
    leaving(0, last_codes(first_inner[0], later.at[0], later_inner.at[0], words))
    leaving(2, last_codes(first_inner[1], later_inner.at[1], later.at[1], words))
    leaving(3, last_codes(kept, later.at[1], later.at[2], words))
    left = lax.broadcasted_iota(jnp.int32, (64, 128), 1) < 64
    for block_row in range(4):
        binned[0, block_row] = jnp.where(left, binned[0, block_row], rests[0, block_row])
        binned[1, block_row] = jnp.where(left, rests[1, block_row], binned[1, block_row])
    for tile in range(2):
        blocks = [binned[pair, 2 * tile + part] for part in range(2) for pair in range(2)]
        for phase, made in enumerate(exchanged(blocks)):
            turned[tile, pl.ds(phase, 64, stride=4), :] = made
    for tile in range(2):
        flat = jnp.transpose(turned[tile])
        for number in range(8):
            odd, part, pair = number // 4, (number // 2) % 2, number % 2
            for row in range(4):
                at = number * 16 + row * 4
                to = (2 * tile + part) * 64 + row * 16 + (2 * pair + odd) * 4
                flat_rest[to : to + 4, :] = flat[at : at + 4, :]
    stores.append(pltpu.make_async_copy(flat_rest, residual, leave.at[5]))
    stores[-1].start()
    for store in stores:
        store.wait()


def body(
    base_volume, vintage_traces, dest_device, dest_slot, vintage_id, vintage_gains, dictionary
):
    trace_count, time_len = vintage_traces.shape
    device_count = lax.axis_size("inline") * lax.axis_size("xline")
    send_rows = device_count * 17
    sent = call_kernel(
        pack_kernel,
        jax.ShapeDtypeStruct((send_rows, 128), jnp.int32),
        pltpu.HBM,
        [
            pltpu.SMEM(vintage_gains.shape, jnp.float32),
            pltpu.VMEM(vintage_traces.shape, jnp.float32),
            pltpu.VMEM((1, trace_count), jnp.int32),
            pltpu.VMEM((1, trace_count), jnp.int32),
            pltpu.VMEM((1, trace_count), jnp.int32),
            pltpu.VMEM((send_rows, 128), jnp.int32),
            pltpu.VMEM((trace_count, 128), jnp.int32),
            pltpu.VMEM((1, trace_count), jnp.int32),
            pltpu.SMEM((1, trace_count), jnp.int32),
            pltpu.SemaphoreType.DMA((6,)),
            pltpu.SemaphoreType.DMA,
        ],
        pltpu.HBM,
        [
            vintage_gains,
            vintage_traces,
            dest_device.reshape(1, trace_count),
            dest_slot.reshape(1, trace_count),
            vintage_id.reshape(1, trace_count),
        ],
        all_vmem_bytes,
    )
    got = lax.all_to_all(
        sent.reshape(send_rows, 1, 128), ("inline", "xline"), split_axis=0, concat_axis=0, tiled=True
    ).reshape(send_rows, 128)
    words = dictionary.reshape(2, 4, 2, 4, 2, 4, 512).transpose(0, 2, 4, 5, 1, 3, 6).reshape(512, 512)
    words_back = words.T
    words = words * jnp.bfloat16(step_size)
    base = (
        base_volume.reshape(2, 2, 4, 2, 2, 4, time_len)
        .transpose(0, 4, 1, 3, 2, 5, 6)
        .reshape(256, time_len)
    )
    got, base, words, words_back = lax.optimization_barrier((got, base, words, words_back))
    pair_shape = lambda *lead: jax.ShapeDtypeStruct(lead + (64, 128), jnp.bfloat16)
    to_odd, to_even, half, whole = call_kernel(
        merge_kernel,
        (
            pair_shape(2, 2),
            pair_shape(2, 2),
            pair_shape(2, 4),
            jax.ShapeDtypeStruct((4, 2, 64, 128), jnp.float32),
        ),
        (pltpu.VMEM,) * 4,
        [
            pltpu.VMEM((2, 256, 128), jnp.float32),
        ],
        pltpu.VMEM,
        [got, base],
    )

    rows, columns = lax.axis_size("inline"), lax.axis_size("xline")

    def swapped(block, along_rows, odd_pairs):
        route = []
        for row in range(rows):
            for column in range(columns):
                at, count = (row, rows) if along_rows else (column, columns)
                to = at + 1 if at % 2 == odd_pairs else at - 1
                if not 0 <= to < count:
                    partner = (row, column ^ 1) if along_rows else (row ^ 1, column)
                else:
                    partner = (to, column) if along_rows else (row, to)
                route.append((row * columns + column, partner[0] * columns + partner[1]))
        return lax.ppermute(block, ("inline", "xline"), route)

    from_odd = swapped(to_odd, True, 1)
    from_even = swapped(to_even, True, 0)
    own_odd, own_even = call_kernel(
        assemble_kernel,
        (pair_shape(7), pair_shape(7)),
        (pltpu.VMEM,) * 2,
        [],
        pltpu.VMEM,
        [from_odd, from_even, half],
    )
    from_odd = swapped(own_odd, False, 1)
    from_even = swapped(own_even, False, 0)
    full_shape = lambda *shape: jax.ShapeDtypeStruct(shape, jnp.float32)
    inner, first, recon, rests, later, codes_inner = call_kernel(
        inner_kernel,
        (
            pair_shape(4, 7),
            full_shape(2, 256, 512),
            full_shape(2, 5, 64, 128),
            full_shape(2, 4, 64, 128),
            pair_shape(2, 5),
            full_shape(4, 64, 512),
        ),
        (pltpu.VMEM,) * 6,
        [],
        pltpu.VMEM,
        [whole, own_even, own_odd, words, words_back],
        cost=pl.CostEstimate(flops=1_400_000_000, bytes_accessed=4_000_000, transcendentals=0),
    )
    codes, residual = call_kernel(
        sparse_kernel,
        (full_shape(4, 4, 64, 512), full_shape(256, time_len)),
        (pltpu.HBM, pltpu.HBM),
        [
            pltpu.VMEM((3, 7, 64, 128), jnp.bfloat16),
            pltpu.VMEM((3, 5, 64, 128), jnp.bfloat16),
            pltpu.VMEM((2, 256, 128), jnp.float32),
            pltpu.VMEM((2, 4, 64, 128), jnp.float32),
            pltpu.VMEM((3, 4, 64, 512), jnp.float32),
            pltpu.VMEM((256, time_len), jnp.float32),
            pltpu.SemaphoreType.DMA((6,)),
        ],
        pltpu.VMEM,
        [
            from_odd, from_even, whole, own_even, own_odd, inner, first, recon, rests, later,
            codes_inner, words, words_back,
        ],
    )
    return codes, residual.reshape(16, 16, time_len)


def solution(mesh):
    in_specs = (
        P("inline", "xline", None),
        P(("inline", "xline"), None),
        P(("inline", "xline"), None),
        P(("inline", "xline")),
        P(("inline", "xline")),
        P(),
        P(),
    )
    out_specs = (P("inline", "xline", None, None), P("inline", "xline", None))
    return jax.shard_map(body, mesh=mesh, in_specs=in_specs, out_specs=out_specs, check_vma=False)
```

```python
import math

import jax
import jax.numpy as jnp
from jax import lax
from jax.experimental import pallas as pl
from jax.experimental.pallas import tpu as pltpu
from jax.sharding import PartitionSpec as P

step_size = 0.25
threshold = 0.02
octaves = 40.0
code_top = 32767.0
log_top = math.log2(12.0)
vmem_bytes = 48 * 1024 * 1024
all_vmem_bytes = 64 * 1024 * 1024


def shrink_codes(values):
    return values - jnp.clip(values, -threshold, threshold)


def call_kernel(kernel, out_shape, out_spaces, scratch, in_space, inputs, vmem_limit=vmem_bytes, cost=None):
    return pl.pallas_call(
        kernel,
        out_shape=out_shape,
        in_specs=[pl.BlockSpec(memory_space=in_space)] * len(inputs),
        out_specs=jax.tree.map(lambda space: pl.BlockSpec(memory_space=space), out_spaces),
        scratch_shapes=scratch,
        cost_estimate=cost,
        compiler_params=pltpu.CompilerParams(vmem_limit_bytes=vmem_limit),
    )(*inputs)


def encode(values):
    size = jnp.log2(jnp.maximum(jnp.abs(values), 1e-30))
    code = (size + (octaves - log_top)) * (code_top / octaves)
    code = jnp.clip(jnp.round(code), 0.0, code_top).astype(jnp.int32)
    return jnp.where(values < 0, -code, code)


def decode(code):
    code = code.astype(jnp.float32)
    size = jnp.exp2(jnp.abs(code) * (octaves / code_top) + (log_top - octaves))
    return size * jnp.clip(code, -1.0, 1.0)


def pack_kernel(gains_in, traces_in, dest_in, slot_in, vid_in, out, gains, traces, dest, slot, vid, built, words, place, place_at, arrive, leave):
    loads = [
        pltpu.make_async_copy(source, target, arrive.at[number])
        for number, (source, target) in enumerate(
            ((dest_in, dest), (slot_in, slot), (gains_in, gains), (vid_in, vid), (traces_in, traces))
        )
    ]
    for load in loads:
        load.start()
    trace_count = traces.shape[0]
    device_count = out.shape[0] // 17
    built[...] = jnp.zeros_like(built)
    chunks = trace_count // 128
    me = lax.axis_index("inline") * lax.axis_size("xline") + lax.axis_index("xline")
    loads[0].wait()
    loads[1].wait()
    row = lax.broadcasted_iota(jnp.int32, (128, 128), 0)
    lane = lax.broadcasted_iota(jnp.int32, (128, 128), 1)
    before = jnp.where(row < lane, 1.0, 0.0).astype(jnp.bfloat16)
    carry = jnp.zeros((device_count, 1), jnp.float32)
    places, owners, listed = [], [], []
    for chunk in range(chunks):
        target = dest[:, chunk * 128 : chunk * 128 + 128]
        hit = jnp.where(row == target, 1.0, 0.0)
        hit_half = hit.astype(jnp.bfloat16)
        earlier = jnp.dot(hit_half, before, preferred_element_type=jnp.float32)
        rank = jnp.sum(hit * (earlier + carry), axis=0, keepdims=True)
        carry = carry + jnp.sum(hit, axis=1, keepdims=True)
        rank = rank.astype(jnp.int32)
        places.append(target * 17 + rank)
        owners.append(hit_half)
        wanted = (slot[:, chunk * 128 : chunk * 128 + 128] + 1).astype(jnp.float32)
        spot = lax.rem(17 * me + rank, 128)
        listed.append(jnp.where(row == spot, wanted, 0.0).astype(jnp.bfloat16))
    place[...] = jnp.concatenate(places, axis=1)
    put = pltpu.make_async_copy(place, place_at, arrive.at[5])
    put.start()
    owner = jnp.concatenate(owners, axis=1)
    listing = jnp.concatenate(listed, axis=1)
    slots = lax.dot_general(
        owner, listing, (((1,), (1,)), ((), ())), preferred_element_type=jnp.float32
    ).astype(jnp.int32)

    loads[2].wait()
    loads[3].wait()
    survey = vid[...]
    gain = jnp.zeros(survey.shape, jnp.float32)
    for number in range(gains.shape[0]):
        gain = jnp.where(survey == number, gains[number], gain)
    gain = jnp.transpose(jnp.broadcast_to(gain, (128, trace_count)))
    loads[4].wait()
    code = [encode(traces[:, half * 128 : half * 128 + 128] * gain) for half in range(2)]
    words[...] = (code[0] << 16) | (code[1] & 65535)
    built[pl.ds(16, device_count, stride=17), :] = slots
    put.wait()
    for trace in range(trace_count):
        built[pl.ds(place_at[0, trace], 1), :] = words[trace : trace + 1, :]
    send = pltpu.make_async_copy(built, out, leave)
    send.start()
    send.wait()


def exchanged(four):
    lane = lax.broadcasted_iota(jnp.int32, four[0].shape, 1)

    def crossed(lower, upper, distance):
        keep = (lane // distance) % 2 == 0
        return (
            jnp.where(keep, lower, pltpu.roll(upper, distance, 1)),
            jnp.where(keep, pltpu.roll(lower, 128 - distance, 1), upper),
        )

    (zero, two), (one, three) = crossed(four[0], four[2], 32), crossed(four[1], four[3], 32)
    (zero, one), (two, three) = crossed(zero, one, 16), crossed(two, three, 16)
    return zero, one, two, three


def merge_kernel(got, base, to_odd, to_even, side_odd, side_even, half, whole, turned):
    tiles = got.shape[0] // 128
    bin_row = lax.broadcasted_iota(jnp.int32, (256, 128), 0)
    tile, part, pair, odd = bin_row // 128, (bin_row // 32) % 2, (bin_row // 16) % 2, (bin_row // 64) % 2
    block_row, block_col = 2 * tile + part, 2 * pair + odd
    bin_slot = block_row * 64 + ((bin_row // 4) % 4) * 16 + block_col * 4 + bin_row % 4
    wanted = bin_slot + 1
    listed = got[pl.ds(16, 128, stride=17), :]
    begin = 17 * lax.broadcasted_iota(jnp.int32, (128, 128), 0)
    lane = lax.broadcasted_iota(jnp.int32, (128, 128), 1)
    tile_of = begin // 128 + jnp.where(lane < begin % 128, 1, 0)
    tiles_each = 4
    fold = jnp.zeros((256, 128), jnp.float32)
    stack = jnp.zeros((256, 512), jnp.float32)
    for at in range(0, tiles, tiles_each):
        hits, rows = [], []
        for tile in range(at, min(at + tiles_each, tiles)):
            low_group, high_group = (128 * tile) // 136, min((128 * tile + 127) // 136, 15)
            spot = slice(8 * low_group, 8 * high_group + 8)
            slots = jnp.sum(jnp.where(tile_of[spot] == tile, listed[spot], 0), axis=0, keepdims=True)
            hit = jnp.where(wanted == slots, 1.0, 0.0)
            fold = fold + hit
            hits.append(hit.astype(jnp.bfloat16))
            word = got[128 * tile : 128 * tile + 128, :]
            values = [decode(code) for code in (word >> 16, (word << 16) >> 16)]
            high = [value.astype(jnp.bfloat16) for value in values]
            low = [
                (value - part.astype(jnp.float32)).astype(jnp.bfloat16)
                for value, part in zip(values, high)
            ]
            rows.append(jnp.concatenate(high + low, axis=1))
        stack = stack + jnp.dot(
            jnp.concatenate(hits, axis=1),
            jnp.concatenate(rows, axis=0),
            preferred_element_type=jnp.float32,
        )
    fold = jnp.sum(fold, axis=1, keepdims=True)
    merged = (base[...] + (stack[:, :256] + stack[:, 256:])) / (1.0 + fold)
    turned[0] = jnp.transpose(merged[:128])
    turned[1] = jnp.transpose(merged[128:])
    for tile in range(2):
        slabs = [turned[tile, pl.ds(phase, 64, stride=4), :] for phase in range(4)]
        for number, made in enumerate(exchanged(slabs)):
            part, pair = number // 2, number % 2
            whole[2 * tile + part, pair] = made
            half[pair, 2 * tile + part] = made.astype(jnp.bfloat16)
    odd_device = lax.rem(lax.axis_index("inline"), 2)
    to_even[...] = half[:, pl.ds(2 - 2 * odd_device, 2)]
    to_odd[...] = half[:, pl.ds(2 * odd_device, 2)]
    odd_device = lax.rem(lax.axis_index("xline"), 2)
    side_even[...] = half[1 - odd_device]
    side_odd[...] = half[odd_device]


def assemble_kernel(from_odd, from_even, to_odd, to_even):
    inline_at = lax.axis_index("inline")
    odd_row = lax.rem(inline_at, 2) == 1
    odd_col = lax.rem(lax.axis_index("xline"), 2)
    last = inline_at == lax.axis_size("inline") - 1
    for target, pair in ((to_even, 1 - odd_col), (to_odd, odd_col)):
        above = jnp.where(odd_row, from_even[pair, 1], from_odd[pair, 1])
        target[0] = jnp.where(inline_at == 0, jnp.zeros_like(above), above)
        below = jnp.where(odd_row, from_odd[pair], from_even[pair])
        target[1:3] = jnp.where(last, jnp.zeros_like(below), below)


def time_rolled(values, distance):
    row = lax.broadcasted_iota(jnp.int32, values.shape, 0)
    if distance < 0:
        return jnp.where(row == values.shape[0] - 1, 0.0, pltpu.roll(values, values.shape[0] - 1, 0))
    return jnp.where(row == 0, 0.0, pltpu.roll(values, 1, 0))


def widened(both):
    left = lax.broadcasted_iota(jnp.int32, both.shape, 1) < 64
    later = time_rolled(both, -1)
    even = jnp.where(left, both, pltpu.roll(later, 64, 1))
    odd = jnp.where(left, pltpu.roll(both, 64, 1), later)
    return even.astype(jnp.bfloat16), odd.astype(jnp.bfloat16)


def correlated(patches, block, words):
    lhs = [
        jnp.concatenate(
            [block(row + down, col + right) for down in (0, 1) for right in (0, 1)], axis=1
        )
        for row, col in patches
    ]
    return jnp.dot(jnp.concatenate(lhs, axis=0), words[...], preferred_element_type=jnp.float32)


def first_codes(patches, block, words, words_back, sums, not_top=1.0, not_left=1.0):
    found = shrink_codes(correlated(patches, block, words))
    pieces = [found[64 * number : 64 * number + 64] for number in range(len(patches))]
    masked = []
    for (row, col), piece in zip(patches, pieces):
        piece = piece * not_top if row < 0 else piece
        masked.append((piece * not_left if col < 0 else piece).astype(jnp.bfloat16))
    given = jnp.dot(
        jnp.concatenate(masked, axis=0), words_back[...], preferred_element_type=jnp.float32
    )
    for number, (row, col) in enumerate(patches):
        for down in (0, 1):
            for right in (0, 1):
                spot = (row + down, col + right)
                if 0 <= spot[0] <= 4 and 0 <= spot[1] <= 4:
                    at = 128 * (2 * down + right)
                    part = given[64 * number : 64 * number + 64, at : at + 128]
                    sums[spot] = sums[spot] + part if spot in sums else part
    return dict(zip(patches, pieces))


def last_codes(before, column, block, words):
    patches = [(row, column) for row in range(4)]
    found = jnp.concatenate(before, axis=0) + correlated(patches, block, words)
    return shrink_codes(found).reshape(4, 64, 512)


outer_spot = {-1: 0, 4: 1, 5: 2}
late_first = ((3, 0), (3, 1), (3, 2), (0, 3), (1, 3), (2, 3))


def chosen(pair, odd_pairs, even_pairs):
    odd_device = lax.rem(lax.axis_index("xline"), 2) == 1
    if pair in (-1, 0):
        return lambda row: jnp.where(odd_device, even_pairs[row], odd_pairs[row]).astype(jnp.float32)
    return lambda row: jnp.where(odd_device, odd_pairs[row], even_pairs[row]).astype(jnp.float32)


def edge_masks():
    inline_at, xline_at = lax.axis_index("inline"), lax.axis_index("xline")
    at_edge = (
        inline_at == 0,
        inline_at == lax.axis_size("inline") - 1,
        xline_at == 0,
        xline_at == lax.axis_size("xline") - 1,
    )
    return [jnp.where(edge, 0.0, 1.0) for edge in at_edge]


def rebuilt_half(given, odd):
    moved = pltpu.roll(given, 64, 1)
    return moved + time_rolled(given, 1) if odd else given + time_rolled(moved, 1)


def widened_half(block, odd):
    left = lax.broadcasted_iota(jnp.int32, block.shape, 1) < 64
    later = time_rolled(block, -1)
    if odd:
        return jnp.where(left, pltpu.roll(block, 64, 1), later).astype(jnp.bfloat16)
    return jnp.where(left, block, pltpu.roll(later, 64, 1)).astype(jnp.bfloat16)


def inner_kernel(half, words, words_back, field, first, recon):
    for pair in range(2):
        for row in range(4):
            even, odd = widened(half[pair, row].astype(jnp.float32))
            field[2 * pair, row] = even
            field[2 * pair + 1, row] = odd
    sums = {}
    patches = [(row, col) for col in range(3) for row in range(3)]
    found = first_codes(patches, lambda row, col: field[col, row], words, words_back, sums)
    for (row, col), piece in found.items():
        first[col, row] = piece
    for (row, col), part in sums.items():
        recon[col, row] = part


def side_kernel(
    side_odd, side_even, edge_odd, edge_even, whole, inner, first_inner, recon_inner, words, words_back,
    field_edge, field_side, first, recon, rests, later, made_codes
):
    not_top, not_bottom, not_left, not_right = edge_masks()
    for pair in range(2):
        load = chosen(pair, edge_odd, edge_even)
        for number in range(3):
            even, odd = widened(load(number))
            field_edge[2 * pair, number] = even
            field_edge[2 * pair + 1, number] = odd
    left, right = chosen(-1, side_odd, side_even), chosen(2, side_odd, side_even)
    for row in range(4):
        field_side[0, row] = widened(left(row) * not_left)[1]
        even, odd = widened(right(row) * not_right)
        field_side[1, row] = even
        field_side[2, row] = odd

    def block(row, col):
        if 0 <= col <= 3:
            return inner[col, row] if 0 <= row <= 3 else field_edge[col, outer_spot[row]]
        return field_side[outer_spot[col], row]

    sums = {(row, col): recon_inner[col, row] for row in range(4) for col in range(4)}
    patches = [(row, col) for col in range(3) for row in (-1, 3, 4)]
    patches += [(row, col) for col in (-1, 3, 4) for row in range(3)]
    found = first_codes(patches, block, words, words_back, sums, not_top, not_left)
    for number, spot in enumerate(late_first):
        first[number] = found[spot]
    for number, col in enumerate((0, 3, 4)):
        for row in range(5):
            if (row, col) != (4, 4):
                recon[number, row] = sums[row, col]
    for col in (1, 2):
        pair, odd = col // 2, col % 2
        load = chosen(pair, edge_odd, edge_even)
        for row in range(5):
            rebuilt = rebuilt_half(sums[row, col], odd)
            if row < 4:
                rest = whole[row, pair] - rebuilt
                rests[col - 1, row] = rest
            else:
                rest = (load(1) - rebuilt) * not_bottom
            later[col - 1, row] = widened_half(rest, odd)
    before = [first_inner[1, row] for row in range(3)] + [found[3, 1]]
    made_codes[...] = last_codes(before, 1, lambda row, col: later[col - 1, row], words)


def sparse_kernel(
    corner_odd, corner_even, side_odd, side_even, edge_odd, edge_even, whole, inner, field_edge, field_side,
    first_inner, first_side, recon_side, rests, later_inner, codes_inner, words, words_back,
    codes, residual, field_corner, later, turned, binned, made_codes, flat_rest, leave
):
    stores = [pltpu.make_async_copy(codes_inner, codes.at[:, 1], leave.at[0])]
    stores[0].start()
    not_top, not_bottom, not_left, not_right = edge_masks()

    def leaving(column, made):
        number = len(stores)
        made_codes[number - 1] = made
        for part in range(2 if column == 3 else 1):
            rows = pl.ds(2 * part, 2) if column == 3 else pl.ds(0, 4)
            stores.append(
                pltpu.make_async_copy(
                    made_codes.at[number - 1, rows], codes.at[rows, column], leave.at[len(stores)]
                )
            )
            stores[-1].start()

    left, right = chosen(-1, corner_odd, corner_even), chosen(2, corner_odd, corner_even)
    for number in range(3):
        field_corner[0, number] = widened(left(number) * not_left)[1]
        even, odd = widened(right(number) * not_right)
        field_corner[1, number] = even
        field_corner[2, number] = odd

    def block(row, col):
        if 0 <= col <= 3:
            return inner[col, row] if 0 <= row <= 3 else field_edge[col, outer_spot[row]]
        if 0 <= row <= 3:
            return field_side[outer_spot[col], row]
        return field_corner[outer_spot[col], outer_spot[row]]

    sums = {
        (row, col): recon_side[number, row]
        for number, col in enumerate((0, 3, 4))
        for row in range(5)
        if (row, col) != (4, 4)
    }
    patches = [(row, col) for col in (-1, 3, 4) for row in (-1, 3, 4)]
    found = first_codes(patches, block, words, words_back, sums, not_top, not_left)

    late_spot = {0: 0, 3: 1, 4: 2}

    def rest_of(col):
        pair, odd = col // 2, col % 2
        for row in range(5):
            rebuilt = rebuilt_half(sums[row, col], odd)
            if col == 4:
                source = chosen(2, side_odd, side_even)(row) if row < 4 else right(1)
                rest = (source - rebuilt) * not_right
            elif row < 4:
                rest = whole[row, pair] - rebuilt
                binned[pair, row] = rest
            else:
                rest = chosen(pair, edge_odd, edge_even)(1) - rebuilt
            if row == 4:
                rest = rest * not_bottom
            later[late_spot[col], row] = widened_half(rest, odd)

    def rest_block(row, col):
        if col in (1, 2):
            return later_inner[col - 1, row]
        return later[late_spot[col], row]

    def before(col):
        if col == 3:
            return [first_side[3 + row] for row in range(3)] + [found[3, 3]]
        return [first_inner[col, row] for row in range(3)] + [first_side[col]]

    rest_of(0)
    rest_of(3)
    rest_of(4)
    for column in (0, 2, 3):
        leaving(column, last_codes(before(column), column, rest_block, words))

    left = lax.broadcasted_iota(jnp.int32, (64, 128), 1) < 64
    for block_row in range(4):
        binned[0, block_row] = jnp.where(left, binned[0, block_row], rests[0, block_row])
        binned[1, block_row] = jnp.where(left, rests[1, block_row], binned[1, block_row])
    for tile in range(2):
        blocks = [binned[pair, 2 * tile + part] for part in range(2) for pair in range(2)]
        for phase, made in enumerate(exchanged(blocks)):
            turned[tile, pl.ds(phase, 64, stride=4), :] = made
    for tile in range(2):
        flat = jnp.transpose(turned[tile])
        for number in range(8):
            odd, part, pair = number // 4, (number // 2) % 2, number % 2
            for row in range(4):
                at = number * 16 + row * 4
                to = (2 * tile + part) * 64 + row * 16 + (2 * pair + odd) * 4
                flat_rest[to : to + 4, :] = flat[at : at + 4, :]
    stores.append(pltpu.make_async_copy(flat_rest, residual, leave.at[5]))
    stores[-1].start()
    for store in stores:
        store.wait()


def body(
    base_volume, vintage_traces, dest_device, dest_slot, vintage_id, vintage_gains, dictionary
):
    trace_count, time_len = vintage_traces.shape
    device_count = lax.axis_size("inline") * lax.axis_size("xline")
    send_rows = device_count * 17
    sent = call_kernel(
        pack_kernel,
        jax.ShapeDtypeStruct((send_rows, 128), jnp.int32),
        pltpu.HBM,
        [
            pltpu.SMEM(vintage_gains.shape, jnp.float32),
            pltpu.VMEM(vintage_traces.shape, jnp.float32),
            pltpu.VMEM((1, trace_count), jnp.int32),
            pltpu.VMEM((1, trace_count), jnp.int32),
            pltpu.VMEM((1, trace_count), jnp.int32),
            pltpu.VMEM((send_rows, 128), jnp.int32),
            pltpu.VMEM((trace_count, 128), jnp.int32),
            pltpu.VMEM((1, trace_count), jnp.int32),
            pltpu.SMEM((1, trace_count), jnp.int32),
            pltpu.SemaphoreType.DMA((6,)),
            pltpu.SemaphoreType.DMA,
        ],
        pltpu.HBM,
        [
            vintage_gains,
            vintage_traces,
            dest_device.reshape(1, trace_count),
            dest_slot.reshape(1, trace_count),
            vintage_id.reshape(1, trace_count),
        ],
        all_vmem_bytes,
    )
    got = lax.all_to_all(
        sent.reshape(send_rows, 1, 128), ("inline", "xline"), split_axis=0, concat_axis=0, tiled=True
    ).reshape(send_rows, 128)
    words = dictionary.reshape(2, 4, 2, 4, 2, 4, 512).transpose(0, 2, 4, 5, 1, 3, 6).reshape(512, 512)
    words_back = words.T
    words = words * jnp.bfloat16(step_size)
    base = (
        base_volume.reshape(2, 2, 4, 2, 2, 4, time_len)
        .transpose(0, 4, 1, 3, 2, 5, 6)
        .reshape(256, time_len)
    )
    got, base, words, words_back = lax.optimization_barrier((got, base, words, words_back))
    full_shape = lambda *shape: jax.ShapeDtypeStruct(shape, jnp.float32)
    pair_shape = lambda *lead: jax.ShapeDtypeStruct(lead + (64, 128), jnp.bfloat16)
    to_odd, to_even, side_odd, side_even, half, whole = call_kernel(
        merge_kernel,
        (
            pair_shape(2, 2),
            pair_shape(2, 2),
            pair_shape(4),
            pair_shape(4),
            pair_shape(2, 4),
            full_shape(4, 2, 64, 128),
        ),
        (pltpu.VMEM,) * 6,
        [pltpu.VMEM((2, 256, 128), jnp.float32)],
        pltpu.VMEM,
        [got, base],
    )

    rows, columns = lax.axis_size("inline"), lax.axis_size("xline")

    def swapped(block, along_rows, odd_pairs):
        route = []
        for row in range(rows):
            for column in range(columns):
                at, count = (row, rows) if along_rows else (column, columns)
                to = at + 1 if at % 2 == odd_pairs else at - 1
                if not 0 <= to < count:
                    partner = (row, column ^ 1) if along_rows else (row ^ 1, column)
                else:
                    partner = (to, column) if along_rows else (row, to)
                route.append((row * columns + column, partner[0] * columns + partner[1]))
        return lax.ppermute(block, ("inline", "xline"), route)

    from_odd = swapped(to_odd, True, 1)
    from_even = swapped(to_even, True, 0)
    side_odd = swapped(side_odd, False, 1)
    side_even = swapped(side_even, False, 0)
    inner, first_inner, recon_inner = call_kernel(
        inner_kernel,
        (pair_shape(4, 4), full_shape(3, 3, 64, 512), full_shape(4, 4, 64, 128)),
        (pltpu.VMEM,) * 3,
        [],
        pltpu.VMEM,
        [half, words, words_back],
        cost=pl.CostEstimate(flops=600_000_000, bytes_accessed=2_000_000, transcendentals=0),
    )
    edge_odd, edge_even = call_kernel(
        assemble_kernel,
        (pair_shape(3), pair_shape(3)),
        (pltpu.VMEM,) * 2,
        [],
        pltpu.VMEM,
        [from_odd, from_even],
    )
    corner_odd = swapped(edge_odd, False, 1)
    corner_even = swapped(edge_even, False, 0)
    field_edge, field_side, first_side, recon_side, rests, later, codes_inner = call_kernel(
        side_kernel,
        (
            pair_shape(4, 3),
            pair_shape(3, 4),
            full_shape(6, 64, 512),
            full_shape(3, 5, 64, 128),
            full_shape(2, 4, 64, 128),
            pair_shape(2, 5),
            full_shape(4, 64, 512),
        ),
        (pltpu.VMEM,) * 7,
        [],
        pltpu.VMEM,
        [
            side_odd, side_even, edge_odd, edge_even, whole, inner, first_inner, recon_inner, words,
            words_back,
        ],
        cost=pl.CostEstimate(flops=1_400_000_000, bytes_accessed=4_000_000, transcendentals=0),
    )
    codes, residual = call_kernel(
        sparse_kernel,
        (full_shape(4, 4, 64, 512), full_shape(256, time_len)),
        (pltpu.HBM, pltpu.HBM),
        [
            pltpu.VMEM((3, 3, 64, 128), jnp.bfloat16),
            pltpu.VMEM((3, 5, 64, 128), jnp.bfloat16),
            pltpu.VMEM((2, 256, 128), jnp.float32),
            pltpu.VMEM((2, 4, 64, 128), jnp.float32),
            pltpu.VMEM((3, 4, 64, 512), jnp.float32),
            pltpu.VMEM((256, time_len), jnp.float32),
            pltpu.SemaphoreType.DMA((6,)),
        ],
        pltpu.VMEM,
        [
            corner_odd, corner_even, side_odd, side_even, edge_odd, edge_even, whole, inner, field_edge,
            field_side, first_inner, first_side, recon_side, rests, later, codes_inner, words, words_back,
        ],
    )
    return codes, residual.reshape(16, 16, time_len)


def solution(mesh):
    in_specs = (
        P("inline", "xline", None),
        P(("inline", "xline"), None),
        P(("inline", "xline"), None),
        P(("inline", "xline")),
        P(("inline", "xline")),
        P(),
        P(),
    )
    out_specs = (P("inline", "xline", None, None), P("inline", "xline", None))
    return jax.shard_map(body, mesh=mesh, in_specs=in_specs, out_specs=out_specs, check_vma=False)
```

```python
import math

import jax
import jax.numpy as jnp
from jax import lax
from jax.experimental import pallas as pl
from jax.experimental.pallas import tpu as pltpu
from jax.sharding import PartitionSpec as P

step_size = 0.25
threshold = 0.02
octaves = 40.0
code_top = 32767.0
log_top = math.log2(12.0)
vmem_bytes = 48 * 1024 * 1024
all_vmem_bytes = 64 * 1024 * 1024


def shrink_codes(values):
    return values - jnp.clip(values, -threshold, threshold)


def call_kernel(kernel, out_shape, out_spaces, scratch, in_space, inputs, vmem_limit=vmem_bytes, cost=None):
    return pl.pallas_call(
        kernel,
        out_shape=out_shape,
        in_specs=[pl.BlockSpec(memory_space=in_space)] * len(inputs),
        out_specs=jax.tree.map(lambda space: pl.BlockSpec(memory_space=space), out_spaces),
        scratch_shapes=scratch,
        cost_estimate=cost,
        compiler_params=pltpu.CompilerParams(vmem_limit_bytes=vmem_limit),
    )(*inputs)


def encode(values):
    size = jnp.log2(jnp.maximum(jnp.abs(values), 1e-30))
    code = (size + (octaves - log_top)) * (code_top / octaves)
    code = jnp.clip(jnp.round(code), 0.0, code_top).astype(jnp.int32)
    return jnp.where(values < 0, -code, code)


def decode(code):
    code = code.astype(jnp.float32)
    size = jnp.exp2(jnp.abs(code) * (octaves / code_top) + (log_top - octaves))
    return size * jnp.clip(code, -1.0, 1.0)


def pack_kernel(gains_in, traces_in, dest_in, slot_in, vid_in, out, gains, traces, dest, slot, vid, built, words, place, place_at, arrive, leave):
    loads = [
        pltpu.make_async_copy(source, target, arrive.at[number])
        for number, (source, target) in enumerate(
            ((dest_in, dest), (slot_in, slot), (gains_in, gains), (vid_in, vid), (traces_in, traces))
        )
    ]
    for load in loads:
        load.start()
    trace_count = traces.shape[0]
    device_count = out.shape[0] // 17
    built[...] = jnp.zeros_like(built)
    chunks = trace_count // 128
    me = lax.axis_index("inline") * lax.axis_size("xline") + lax.axis_index("xline")
    loads[0].wait()
    loads[1].wait()
    row = lax.broadcasted_iota(jnp.int32, (128, 128), 0)
    lane = lax.broadcasted_iota(jnp.int32, (128, 128), 1)
    before = jnp.where(row < lane, 1.0, 0.0).astype(jnp.bfloat16)
    carry = jnp.zeros((device_count, 1), jnp.float32)
    places, owners, listed = [], [], []
    for chunk in range(chunks):
        target = dest[:, chunk * 128 : chunk * 128 + 128]
        hit = jnp.where(row == target, 1.0, 0.0)
        hit_half = hit.astype(jnp.bfloat16)
        earlier = jnp.dot(hit_half, before, preferred_element_type=jnp.float32)
        rank = jnp.sum(hit * (earlier + carry), axis=0, keepdims=True)
        carry = carry + jnp.sum(hit, axis=1, keepdims=True)
        rank = rank.astype(jnp.int32)
        places.append(target * 17 + rank)
        owners.append(hit_half)
        wanted = (slot[:, chunk * 128 : chunk * 128 + 128] + 1).astype(jnp.float32)
        spot = lax.rem(17 * me + rank, 128)
        listed.append(jnp.where(row == spot, wanted, 0.0).astype(jnp.bfloat16))
    place[...] = jnp.concatenate(places, axis=1)
    put = pltpu.make_async_copy(place, place_at, arrive.at[5])
    put.start()
    owner = jnp.concatenate(owners, axis=1)
    listing = jnp.concatenate(listed, axis=1)
    slots = lax.dot_general(
        owner, listing, (((1,), (1,)), ((), ())), preferred_element_type=jnp.float32
    ).astype(jnp.int32)

    loads[2].wait()
    loads[3].wait()
    survey = vid[...]
    gain = jnp.zeros(survey.shape, jnp.float32)
    for number in range(gains.shape[0]):
        gain = jnp.where(survey == number, gains[number], gain)
    gain = jnp.transpose(jnp.broadcast_to(gain, (128, trace_count)))
    loads[4].wait()
    code = [encode(traces[:, half * 128 : half * 128 + 128] * gain) for half in range(2)]
    words[...] = (code[0] << 16) | (code[1] & 65535)
    built[pl.ds(16, device_count, stride=17), :] = slots
    put.wait()
    for trace in range(trace_count):
        built[pl.ds(place_at[0, trace], 1), :] = words[trace : trace + 1, :]
    send = pltpu.make_async_copy(built, out, leave)
    send.start()
    send.wait()


def exchanged(four):
    lane = lax.broadcasted_iota(jnp.int32, four[0].shape, 1)

    def crossed(lower, upper, distance):
        keep = (lane // distance) % 2 == 0
        return (
            jnp.where(keep, lower, pltpu.roll(upper, distance, 1)),
            jnp.where(keep, pltpu.roll(lower, 128 - distance, 1), upper),
        )

    (zero, two), (one, three) = crossed(four[0], four[2], 32), crossed(four[1], four[3], 32)
    (zero, one), (two, three) = crossed(zero, one, 16), crossed(two, three, 16)
    return zero, one, two, three


def merge_kernel(got, base, to_odd, to_even, side_odd, side_even, half, whole, turned):
    tiles = got.shape[0] // 128
    bin_row = lax.broadcasted_iota(jnp.int32, (256, 128), 0)
    tile, part, pair, odd = bin_row // 128, (bin_row // 32) % 2, (bin_row // 16) % 2, (bin_row // 64) % 2
    block_row, block_col = 2 * tile + part, 2 * pair + odd
    bin_slot = block_row * 64 + ((bin_row // 4) % 4) * 16 + block_col * 4 + bin_row % 4
    wanted = bin_slot + 1
    listed = got[pl.ds(16, 128, stride=17), :]
    begin = 17 * lax.broadcasted_iota(jnp.int32, (128, 128), 0)
    lane = lax.broadcasted_iota(jnp.int32, (128, 128), 1)
    tile_of = begin // 128 + jnp.where(lane < begin % 128, 1, 0)
    tiles_each = 4
    fold = jnp.zeros((256, 128), jnp.float32)
    stack = jnp.zeros((256, 512), jnp.float32)
    for at in range(0, tiles, tiles_each):
        hits, rows = [], []
        for tile in range(at, min(at + tiles_each, tiles)):
            low_group, high_group = (128 * tile) // 136, min((128 * tile + 127) // 136, 15)
            spot = slice(8 * low_group, 8 * high_group + 8)
            slots = jnp.sum(jnp.where(tile_of[spot] == tile, listed[spot], 0), axis=0, keepdims=True)
            hit = jnp.where(wanted == slots, 1.0, 0.0)
            fold = fold + hit
            hits.append(hit.astype(jnp.bfloat16))
            word = got[128 * tile : 128 * tile + 128, :]
            values = [decode(code) for code in (word >> 16, (word << 16) >> 16)]
            high = [value.astype(jnp.bfloat16) for value in values]
            low = [
                (value - part.astype(jnp.float32)).astype(jnp.bfloat16)
                for value, part in zip(values, high)
            ]
            rows.append(jnp.concatenate(high + low, axis=1))
        stack = stack + jnp.dot(
            jnp.concatenate(hits, axis=1),
            jnp.concatenate(rows, axis=0),
            preferred_element_type=jnp.float32,
        )
    fold = jnp.sum(fold, axis=1, keepdims=True)
    merged = (base[...] + (stack[:, :256] + stack[:, 256:])) / (1.0 + fold)
    turned[0] = jnp.transpose(merged[:128])
    turned[1] = jnp.transpose(merged[128:])
    for tile in range(2):
        slabs = [turned[tile, pl.ds(phase, 64, stride=4), :] for phase in range(4)]
        for number, made in enumerate(exchanged(slabs)):
            part, pair = number // 2, number % 2
            whole[2 * tile + part, pair] = made
            half[pair, 2 * tile + part] = made.astype(jnp.bfloat16)
    odd_device = lax.rem(lax.axis_index("inline"), 2)
    to_even[...] = half[:, pl.ds(2 - 2 * odd_device, 2)]
    to_odd[...] = half[:, pl.ds(2 * odd_device, 2)]
    odd_device = lax.rem(lax.axis_index("xline"), 2)
    side_even[...] = half[1 - odd_device]
    side_odd[...] = half[odd_device]


def assemble_kernel(from_odd, from_even, to_odd, to_even):
    inline_at = lax.axis_index("inline")
    odd_row = lax.rem(inline_at, 2) == 1
    odd_col = lax.rem(lax.axis_index("xline"), 2)
    last = inline_at == lax.axis_size("inline") - 1
    for target, pair in ((to_even, 1 - odd_col), (to_odd, odd_col)):
        above = jnp.where(odd_row, from_even[pair, 1], from_odd[pair, 1])
        target[0] = jnp.where(inline_at == 0, jnp.zeros_like(above), above)
        below = jnp.where(odd_row, from_odd[pair], from_even[pair])
        target[1:3] = jnp.where(last, jnp.zeros_like(below), below)


def time_rolled(values, distance):
    row = lax.broadcasted_iota(jnp.int32, values.shape, 0)
    if distance < 0:
        return jnp.where(row == values.shape[0] - 1, 0.0, pltpu.roll(values, values.shape[0] - 1, 0))
    return jnp.where(row == 0, 0.0, pltpu.roll(values, 1, 0))


def widened(both):
    left = lax.broadcasted_iota(jnp.int32, both.shape, 1) < 64
    later = time_rolled(both, -1)
    even = jnp.where(left, both, pltpu.roll(later, 64, 1))
    odd = jnp.where(left, pltpu.roll(both, 64, 1), later)
    return even.astype(jnp.bfloat16), odd.astype(jnp.bfloat16)


def correlated(patches, block, words):
    lhs = [
        jnp.concatenate(
            [block(row + down, col + right) for down in (0, 1) for right in (0, 1)], axis=1
        )
        for row, col in patches
    ]
    return jnp.dot(jnp.concatenate(lhs, axis=0), words[...], preferred_element_type=jnp.float32)


def group_codes(patches, block, words, words_back, sums, not_top, not_left):
    found = shrink_codes(correlated(patches, block, words))
    pieces = [found[64 * number : 64 * number + 64] for number in range(len(patches))]
    masked = []
    for (row, col), piece in zip(patches, pieces):
        piece = piece * not_top if row < 0 else piece
        masked.append((piece * not_left if col < 0 else piece).astype(jnp.bfloat16))
    given = jnp.dot(
        jnp.concatenate(masked, axis=0), words_back[...], preferred_element_type=jnp.float32
    )
    for number, (row, col) in enumerate(patches):
        for down in (0, 1):
            for right in (0, 1):
                spot = (row + down, col + right)
                if 0 <= spot[0] <= 4 and 0 <= spot[1] <= 4:
                    at = 128 * (2 * down + right)
                    part = given[64 * number : 64 * number + 64, at : at + 128]
                    sums[spot] = sums[spot] + part if spot in sums else part
    return dict(zip(patches, pieces))


def first_codes(each, patches, block, words, words_back, sums, not_top=1.0, not_left=1.0):
    found = {}
    for at in range(0, len(patches), each):
        group = patches[at : at + each]
        found.update(group_codes(group, block, words, words_back, sums, not_top, not_left))
    return found


def last_codes(before, column, block, words):
    patches = [(row, column) for row in range(4)]
    found = jnp.concatenate(before, axis=0) + correlated(patches, block, words)
    return shrink_codes(found).reshape(4, 64, 512)


outer_spot = {-1: 0, 4: 1, 5: 2}
late_first = ((3, 0), (3, 1), (3, 2), (0, 3), (1, 3), (2, 3))


def chosen(pair, odd_pairs, even_pairs):
    odd_device = lax.rem(lax.axis_index("xline"), 2) == 1
    if pair in (-1, 0):
        return lambda row: jnp.where(odd_device, even_pairs[row], odd_pairs[row]).astype(jnp.float32)
    return lambda row: jnp.where(odd_device, odd_pairs[row], even_pairs[row]).astype(jnp.float32)


def edge_masks():
    inline_at, xline_at = lax.axis_index("inline"), lax.axis_index("xline")
    at_edge = (
        inline_at == 0,
        inline_at == lax.axis_size("inline") - 1,
        xline_at == 0,
        xline_at == lax.axis_size("xline") - 1,
    )
    return [jnp.where(edge, 0.0, 1.0) for edge in at_edge]


def rebuilt_half(given, odd):
    moved = pltpu.roll(given, 64, 1)
    return moved + time_rolled(given, 1) if odd else given + time_rolled(moved, 1)


def widened_half(block, odd):
    left = lax.broadcasted_iota(jnp.int32, block.shape, 1) < 64
    later = time_rolled(block, -1)
    if odd:
        return jnp.where(left, pltpu.roll(block, 64, 1), later).astype(jnp.bfloat16)
    return jnp.where(left, block, pltpu.roll(later, 64, 1)).astype(jnp.bfloat16)


def inner_kernel(half, words, words_back, field, first, recon):
    for pair in range(2):
        for row in range(4):
            even, odd = widened(half[pair, row].astype(jnp.float32))
            field[2 * pair, row] = even
            field[2 * pair + 1, row] = odd
    sums = {}
    patches = [(row, col) for col in range(3) for row in range(3)]
    found = first_codes(6, patches, lambda row, col: field[col, row], words, words_back, sums)
    for (row, col), piece in found.items():
        first[col, row] = piece
    for (row, col), part in sums.items():
        recon[col, row] = part


def side_kernel(
    side_odd, side_even, edge_odd, edge_even, whole, inner, first_inner, recon_inner, words, words_back,
    field_edge, field_side, first, recon, rests, later, made_codes
):
    not_top, not_bottom, not_left, not_right = edge_masks()
    for pair in range(2):
        load = chosen(pair, edge_odd, edge_even)
        for number in range(3):
            even, odd = widened(load(number))
            field_edge[2 * pair, number] = even
            field_edge[2 * pair + 1, number] = odd
    left, right = chosen(-1, side_odd, side_even), chosen(2, side_odd, side_even)
    for row in range(4):
        field_side[0, row] = widened(left(row) * not_left)[1]
        even, odd = widened(right(row) * not_right)
        field_side[1, row] = even
        field_side[2, row] = odd

    def block(row, col):
        if 0 <= col <= 3:
            return inner[col, row] if 0 <= row <= 3 else field_edge[col, outer_spot[row]]
        return field_side[outer_spot[col], row]

    sums = {(row, col): recon_inner[col, row] for row in range(4) for col in range(4)}
    patches = [(row, col) for col in range(3) for row in (-1, 3, 4)]
    patches += [(row, col) for col in (-1, 3, 4) for row in range(3)]
    found = first_codes(6, patches, block, words, words_back, sums, not_top, not_left)
    for number, spot in enumerate(late_first):
        first[number] = found[spot]
    for number, col in enumerate((0, 3, 4)):
        for row in range(5):
            if (row, col) != (4, 4):
                recon[number, row] = sums[row, col]
    for col in (1, 2):
        pair, odd = col // 2, col % 2
        load = chosen(pair, edge_odd, edge_even)
        for row in range(5):
            rebuilt = rebuilt_half(sums[row, col], odd)
            if row < 4:
                rest = whole[row, pair] - rebuilt
                rests[col - 1, row] = rest
            else:
                rest = (load(1) - rebuilt) * not_bottom
            later[col - 1, row] = widened_half(rest, odd)
    before = [first_inner[1, row] for row in range(3)] + [found[3, 1]]
    made_codes[...] = last_codes(before, 1, lambda row, col: later[col - 1, row], words)


def sparse_kernel(
    corner_odd, corner_even, side_odd, side_even, edge_odd, edge_even, whole, inner, field_edge, field_side,
    first_inner, first_side, recon_side, rests, later_inner, codes_inner, words, words_back,
    codes, residual, field_corner, later, turned, binned, made_codes, flat_rest, leave
):
    stores = [pltpu.make_async_copy(codes_inner, codes.at[:, 1], leave.at[0])]
    stores[0].start()
    not_top, not_bottom, not_left, not_right = edge_masks()

    def leaving(column, made):
        number = len(stores)
        made_codes[number - 1] = made
        for part in range(2 if column == 3 else 1):
            rows = pl.ds(2 * part, 2) if column == 3 else pl.ds(0, 4)
            stores.append(
                pltpu.make_async_copy(
                    made_codes.at[number - 1, rows], codes.at[rows, column], leave.at[len(stores)]
                )
            )
            stores[-1].start()

    left, right = chosen(-1, corner_odd, corner_even), chosen(2, corner_odd, corner_even)
    for number in range(3):
        field_corner[0, number] = widened(left(number) * not_left)[1]
        even, odd = widened(right(number) * not_right)
        field_corner[1, number] = even
        field_corner[2, number] = odd

    def block(row, col):
        if 0 <= col <= 3:
            return inner[col, row] if 0 <= row <= 3 else field_edge[col, outer_spot[row]]
        if 0 <= row <= 3:
            return field_side[outer_spot[col], row]
        return field_corner[outer_spot[col], outer_spot[row]]

    sums = {
        (row, col): recon_side[number, row]
        for number, col in enumerate((0, 3, 4))
        for row in range(5)
        if (row, col) != (4, 4)
    }
    patches = [(row, col) for col in (-1, 3, 4) for row in (-1, 3, 4)]
    found = first_codes(3, patches, block, words, words_back, sums, not_top, not_left)

    late_spot = {0: 0, 3: 1, 4: 2}

    def rest_of(col):
        pair, odd = col // 2, col % 2
        for row in range(5):
            rebuilt = rebuilt_half(sums[row, col], odd)
            if col == 4:
                source = chosen(2, side_odd, side_even)(row) if row < 4 else right(1)
                rest = (source - rebuilt) * not_right
            elif row < 4:
                rest = whole[row, pair] - rebuilt
                binned[pair, row] = rest
            else:
                rest = chosen(pair, edge_odd, edge_even)(1) - rebuilt
            if row == 4:
                rest = rest * not_bottom
            later[late_spot[col], row] = widened_half(rest, odd)

    def rest_block(row, col):
        if col in (1, 2):
            return later_inner[col - 1, row]
        return later[late_spot[col], row]

    def before(col):
        if col == 3:
            return [first_side[3 + row] for row in range(3)] + [found[3, 3]]
        return [first_inner[col, row] for row in range(3)] + [first_side[col]]

    rest_of(0)
    rest_of(3)
    rest_of(4)
    for column in (0, 2, 3):
        leaving(column, last_codes(before(column), column, rest_block, words))

    left = lax.broadcasted_iota(jnp.int32, (64, 128), 1) < 64
    for block_row in range(4):
        binned[0, block_row] = jnp.where(left, binned[0, block_row], rests[0, block_row])
        binned[1, block_row] = jnp.where(left, rests[1, block_row], binned[1, block_row])
    for tile in range(2):
        blocks = [binned[pair, 2 * tile + part] for part in range(2) for pair in range(2)]
        for phase, made in enumerate(exchanged(blocks)):
            turned[tile, pl.ds(phase, 64, stride=4), :] = made
    for tile in range(2):
        flat = jnp.transpose(turned[tile])
        for number in range(8):
            odd, part, pair = number // 4, (number // 2) % 2, number % 2
            for row in range(4):
                at = number * 16 + row * 4
                to = (2 * tile + part) * 64 + row * 16 + (2 * pair + odd) * 4
                flat_rest[to : to + 4, :] = flat[at : at + 4, :]
    stores.append(pltpu.make_async_copy(flat_rest, residual, leave.at[5]))
    stores[-1].start()
    for store in stores:
        store.wait()


def body(
    base_volume, vintage_traces, dest_device, dest_slot, vintage_id, vintage_gains, dictionary
):
    trace_count, time_len = vintage_traces.shape
    device_count = lax.axis_size("inline") * lax.axis_size("xline")
    send_rows = device_count * 17
    sent = call_kernel(
        pack_kernel,
        jax.ShapeDtypeStruct((send_rows, 128), jnp.int32),
        pltpu.HBM,
        [
            pltpu.SMEM(vintage_gains.shape, jnp.float32),
            pltpu.VMEM(vintage_traces.shape, jnp.float32),
            pltpu.VMEM((1, trace_count), jnp.int32),
            pltpu.VMEM((1, trace_count), jnp.int32),
            pltpu.VMEM((1, trace_count), jnp.int32),
            pltpu.VMEM((send_rows, 128), jnp.int32),
            pltpu.VMEM((trace_count, 128), jnp.int32),
            pltpu.VMEM((1, trace_count), jnp.int32),
            pltpu.SMEM((1, trace_count), jnp.int32),
            pltpu.SemaphoreType.DMA((6,)),
            pltpu.SemaphoreType.DMA,
        ],
        pltpu.HBM,
        [
            vintage_gains,
            vintage_traces,
            dest_device.reshape(1, trace_count),
            dest_slot.reshape(1, trace_count),
            vintage_id.reshape(1, trace_count),
        ],
        all_vmem_bytes,
    )
    got = lax.all_to_all(
        sent.reshape(send_rows, 1, 128), ("inline", "xline"), split_axis=0, concat_axis=0, tiled=True
    ).reshape(send_rows, 128)
    words = dictionary.reshape(2, 4, 2, 4, 2, 4, 512).transpose(0, 2, 4, 5, 1, 3, 6).reshape(512, 512)
    words_back = words.T
    words = words * jnp.bfloat16(step_size)
    base = (
        base_volume.reshape(2, 2, 4, 2, 2, 4, time_len)
        .transpose(0, 4, 1, 3, 2, 5, 6)
        .reshape(256, time_len)
    )
    got, base, words, words_back = lax.optimization_barrier((got, base, words, words_back))
    full_shape = lambda *shape: jax.ShapeDtypeStruct(shape, jnp.float32)
    pair_shape = lambda *lead: jax.ShapeDtypeStruct(lead + (64, 128), jnp.bfloat16)
    to_odd, to_even, side_odd, side_even, half, whole = call_kernel(
        merge_kernel,
        (
            pair_shape(2, 2),
            pair_shape(2, 2),
            pair_shape(4),
            pair_shape(4),
            pair_shape(2, 4),
            full_shape(4, 2, 64, 128),
        ),
        (pltpu.VMEM,) * 6,
        [pltpu.VMEM((2, 256, 128), jnp.float32)],
        pltpu.VMEM,
        [got, base],
    )

    rows, columns = lax.axis_size("inline"), lax.axis_size("xline")

    def swapped(block, along_rows, odd_pairs):
        route = []
        for row in range(rows):
            for column in range(columns):
                at, count = (row, rows) if along_rows else (column, columns)
                to = at + 1 if at % 2 == odd_pairs else at - 1
                if not 0 <= to < count:
                    partner = (row, column ^ 1) if along_rows else (row ^ 1, column)
                else:
                    partner = (to, column) if along_rows else (row, to)
                route.append((row * columns + column, partner[0] * columns + partner[1]))
        return lax.ppermute(block, ("inline", "xline"), route)

    from_odd = swapped(to_odd, True, 1)
    from_even = swapped(to_even, True, 0)
    side_odd = swapped(side_odd, False, 1)
    side_even = swapped(side_even, False, 0)
    inner, first_inner, recon_inner = call_kernel(
        inner_kernel,
        (pair_shape(4, 4), full_shape(3, 3, 64, 512), full_shape(4, 4, 64, 128)),
        (pltpu.VMEM,) * 3,
        [],
        pltpu.VMEM,
        [half, words, words_back],
        cost=pl.CostEstimate(flops=600_000_000, bytes_accessed=2_000_000, transcendentals=0),
    )
    edge_odd, edge_even = call_kernel(
        assemble_kernel,
        (pair_shape(3), pair_shape(3)),
        (pltpu.VMEM,) * 2,
        [],
        pltpu.VMEM,
        [from_odd, from_even],
    )
    corner_odd = swapped(edge_odd, False, 1)
    corner_even = swapped(edge_even, False, 0)
    field_edge, field_side, first_side, recon_side, rests, later, codes_inner = call_kernel(
        side_kernel,
        (
            pair_shape(4, 3),
            pair_shape(3, 4),
            full_shape(6, 64, 512),
            full_shape(3, 5, 64, 128),
            full_shape(2, 4, 64, 128),
            pair_shape(2, 5),
            full_shape(4, 64, 512),
        ),
        (pltpu.VMEM,) * 7,
        [],
        pltpu.VMEM,
        [
            side_odd, side_even, edge_odd, edge_even, whole, inner, first_inner, recon_inner, words,
            words_back,
        ],
        cost=pl.CostEstimate(flops=1_400_000_000, bytes_accessed=4_000_000, transcendentals=0),
    )
    codes, residual = call_kernel(
        sparse_kernel,
        (full_shape(4, 4, 64, 512), full_shape(256, time_len)),
        (pltpu.HBM, pltpu.HBM),
        [
            pltpu.VMEM((3, 3, 64, 128), jnp.bfloat16),
            pltpu.VMEM((3, 5, 64, 128), jnp.bfloat16),
            pltpu.VMEM((2, 256, 128), jnp.float32),
            pltpu.VMEM((2, 4, 64, 128), jnp.float32),
            pltpu.VMEM((3, 4, 64, 512), jnp.float32),
            pltpu.VMEM((256, time_len), jnp.float32),
            pltpu.SemaphoreType.DMA((6,)),
        ],
        pltpu.VMEM,
        [
            corner_odd, corner_even, side_odd, side_even, edge_odd, edge_even, whole, inner, field_edge,
            field_side, first_inner, first_side, recon_side, rests, later, codes_inner, words, words_back,
        ],
    )
    return codes, residual.reshape(16, 16, time_len)


def solution(mesh):
    in_specs = (
        P("inline", "xline", None),
        P(("inline", "xline"), None),
        P(("inline", "xline"), None),
        P(("inline", "xline")),
        P(("inline", "xline")),
        P(),
        P(),
    )
    out_specs = (P("inline", "xline", None, None), P("inline", "xline", None))
    return jax.shard_map(body, mesh=mesh, in_specs=in_specs, out_specs=out_specs, check_vma=False)
```

```python
import math

import jax
import jax.numpy as jnp
from jax import lax
from jax.experimental import pallas as pl
from jax.experimental.pallas import tpu as pltpu
from jax.sharding import PartitionSpec as P

step_size = 0.25
threshold = 0.02
octaves = 40.0
code_top = 32767.0
log_top = math.log2(12.0)
vmem_bytes = 48 * 1024 * 1024


def shrink_codes(values):
    return values - jnp.clip(values, -threshold, threshold)


def call_kernel(kernel, out_shape, out_spaces, scratch, in_space, inputs, vmem_limit=vmem_bytes, cost=None):
    return pl.pallas_call(
        kernel,
        out_shape=out_shape,
        in_specs=[pl.BlockSpec(memory_space=in_space)] * len(inputs),
        out_specs=jax.tree.map(lambda space: pl.BlockSpec(memory_space=space), out_spaces),
        scratch_shapes=scratch,
        cost_estimate=cost,
        compiler_params=pltpu.CompilerParams(vmem_limit_bytes=vmem_limit),
    )(*inputs)


def encode(values):
    size = jnp.log2(jnp.maximum(jnp.abs(values), 1e-30))
    code = (size + (octaves - log_top)) * (code_top / octaves)
    code = jnp.clip(jnp.round(code), 0.0, code_top).astype(jnp.int32)
    return jnp.where(values < 0, -code, code)


def decode(code):
    code = code.astype(jnp.float32)
    size = jnp.exp2(jnp.abs(code) * (octaves / code_top) + (log_top - octaves))
    return size * jnp.clip(code, -1.0, 1.0)


def pack_kernel(gains_in, traces_in, dest_in, slot_in, vid_in, out, gains, traces, dest, slot, vid, built, words, place, place_at, arrive, leave):
    loads = [
        pltpu.make_async_copy(source, target, arrive.at[number])
        for number, (source, target) in enumerate(
            ((dest_in, dest), (slot_in, slot), (gains_in, gains), (vid_in, vid), (traces_in, traces))
        )
    ]
    for load in loads:
        load.start()
    trace_count = traces.shape[0]
    device_count = out.shape[0] // 17
    built[...] = jnp.zeros_like(built)
    chunks = trace_count // 128
    me = lax.axis_index("inline") * lax.axis_size("xline") + lax.axis_index("xline")
    loads[0].wait()
    loads[1].wait()
    row = lax.broadcasted_iota(jnp.int32, (128, 128), 0)
    lane = lax.broadcasted_iota(jnp.int32, (128, 128), 1)
    before = jnp.where(row < lane, 1.0, 0.0).astype(jnp.bfloat16)
    carry = jnp.zeros((device_count, 1), jnp.float32)
    places, owners, listed = [], [], []
    for chunk in range(chunks):
        target = dest[:, chunk * 128 : chunk * 128 + 128]
        hit = jnp.where(row == target, 1.0, 0.0)
        hit_half = hit.astype(jnp.bfloat16)
        earlier = jnp.dot(hit_half, before, preferred_element_type=jnp.float32)
        rank = jnp.sum(hit * (earlier + carry), axis=0, keepdims=True)
        carry = carry + jnp.sum(hit, axis=1, keepdims=True)
        rank = rank.astype(jnp.int32)
        places.append(target * 17 + rank)
        owners.append(hit_half)
        wanted = (slot[:, chunk * 128 : chunk * 128 + 128] + 1).astype(jnp.float32)
        spot = lax.rem(17 * me + rank, 128)
        listed.append(jnp.where(row == spot, wanted, 0.0).astype(jnp.bfloat16))
    place[...] = jnp.concatenate(places, axis=1)
    put = pltpu.make_async_copy(place, place_at, arrive.at[5])
    put.start()
    owner = jnp.concatenate(owners, axis=1)
    listing = jnp.concatenate(listed, axis=1)
    slots = lax.dot_general(
        owner, listing, (((1,), (1,)), ((), ())), preferred_element_type=jnp.float32
    ).astype(jnp.int32)

    loads[2].wait()
    loads[3].wait()
    survey = vid[...]
    gain = jnp.zeros(survey.shape, jnp.float32)
    for number in range(gains.shape[0]):
        gain = jnp.where(survey == number, gains[number], gain)
    gain = jnp.transpose(jnp.broadcast_to(gain, (128, trace_count)))
    loads[4].wait()
    code = [encode(traces[:, half * 128 : half * 128 + 128] * gain) for half in range(2)]
    words[...] = (code[0] << 16) | (code[1] & 65535)
    built[pl.ds(16, device_count, stride=17), :] = slots
    put.wait()
    for trace in range(trace_count):
        built[pl.ds(place_at[0, trace], 1), :] = words[trace : trace + 1, :]
    send = pltpu.make_async_copy(built, out, leave)
    send.start()
    send.wait()


def exchanged(four):
    lane = lax.broadcasted_iota(jnp.int32, four[0].shape, 1)

    def crossed(lower, upper, distance):
        keep = (lane // distance) % 2 == 0
        return (
            jnp.where(keep, lower, pltpu.roll(upper, distance, 1)),
            jnp.where(keep, pltpu.roll(lower, 128 - distance, 1), upper),
        )

    (zero, two), (one, three) = crossed(four[0], four[2], 32), crossed(four[1], four[3], 32)
    (zero, one), (two, three) = crossed(zero, one, 16), crossed(two, three, 16)
    return zero, one, two, three


def merge_kernel(got, base, to_odd, to_even, side_odd, side_even, half, whole, turned, ordered):
    tiles = got.shape[0] // 128
    for number in range(64):
        tile, odd, part, pair = number // 32, number // 16 % 2, number // 8 % 2, number // 4 % 2
        at = (4 * (2 * tile + part) + number % 4) * 16 + 4 * (2 * pair + odd)
        ordered[4 * number : 4 * number + 4, :] = base[at : at + 4, :]
    bin_row = lax.broadcasted_iota(jnp.int32, (256, 128), 0)
    tile, part, pair, odd = bin_row // 128, (bin_row // 32) % 2, (bin_row // 16) % 2, (bin_row // 64) % 2
    block_row, block_col = 2 * tile + part, 2 * pair + odd
    bin_slot = block_row * 64 + ((bin_row // 4) % 4) * 16 + block_col * 4 + bin_row % 4
    wanted = bin_slot + 1
    listed = got[pl.ds(16, 128, stride=17), :]
    begin = 17 * lax.broadcasted_iota(jnp.int32, (128, 128), 0)
    lane = lax.broadcasted_iota(jnp.int32, (128, 128), 1)
    tile_of = begin // 128 + jnp.where(lane < begin % 128, 1, 0)
    tiles_each = 2
    fold = jnp.zeros((256, 128), jnp.float32)
    stack = jnp.zeros((256, 256), jnp.float32)
    for at in range(0, tiles, tiles_each):
        hits, rows, rests = [], [], []
        for tile in range(at, min(at + tiles_each, tiles)):
            low_group, high_group = (128 * tile) // 136, min((128 * tile + 127) // 136, 15)
            spot = slice(8 * low_group, 8 * high_group + 8)
            slots = jnp.sum(jnp.where(tile_of[spot] == tile, listed[spot], 0), axis=0, keepdims=True)
            hit = jnp.where(wanted == slots, 1.0, 0.0)
            fold = fold + hit
            hits.append(hit.astype(jnp.bfloat16))
            word = got[128 * tile : 128 * tile + 128, :]
            values = [decode(code) for code in (word >> 16, (word << 16) >> 16)]
            high = [value.astype(jnp.bfloat16) for value in values]
            low = [
                (value - part.astype(jnp.float32)).astype(jnp.bfloat16)
                for value, part in zip(values, high)
            ]
            rows.append(jnp.concatenate(high, axis=1))
            rests.append(jnp.concatenate(low, axis=1))
        stack = stack + jnp.dot(
            jnp.concatenate(hits + hits, axis=1),
            jnp.concatenate(rows + rests, axis=0),
            preferred_element_type=jnp.float32,
        )
    fold = jnp.sum(fold, axis=1, keepdims=True)
    merged = (ordered[...] + stack) / (1.0 + fold)
    turned[0] = jnp.transpose(merged[:128])
    turned[1] = jnp.transpose(merged[128:])
    for tile in range(2):
        slabs = [turned[tile, pl.ds(phase, 64, stride=4), :] for phase in range(4)]
        for number, made in enumerate(exchanged(slabs)):
            part, pair = number // 2, number % 2
            whole[2 * tile + part, pair] = made
            half[pair, 2 * tile + part] = made.astype(jnp.bfloat16)
    odd_device = lax.rem(lax.axis_index("inline"), 2)
    to_even[...] = half[:, pl.ds(2 - 2 * odd_device, 2)]
    to_odd[...] = half[:, pl.ds(2 * odd_device, 2)]
    odd_device = lax.rem(lax.axis_index("xline"), 2)
    side_even[...] = half[1 - odd_device]
    side_odd[...] = half[odd_device]


def assemble_kernel(from_odd, from_even, to_odd, to_even):
    inline_at = lax.axis_index("inline")
    odd_row = lax.rem(inline_at, 2) == 1
    odd_col = lax.rem(lax.axis_index("xline"), 2)
    last = inline_at == lax.axis_size("inline") - 1
    for target, pair in ((to_even, 1 - odd_col), (to_odd, odd_col)):
        above = jnp.where(odd_row, from_even[pair, 1], from_odd[pair, 1])
        target[0] = jnp.where(inline_at == 0, jnp.zeros_like(above), above)
        below = jnp.where(odd_row, from_odd[pair], from_even[pair])
        target[1:3] = jnp.where(last, jnp.zeros_like(below), below)


def time_rolled(values, distance):
    row = lax.broadcasted_iota(jnp.int32, values.shape, 0)
    if distance < 0:
        return jnp.where(row == values.shape[0] - 1, 0.0, pltpu.roll(values, values.shape[0] - 1, 0))
    return jnp.where(row == 0, 0.0, pltpu.roll(values, 1, 0))


def widened(both):
    left = lax.broadcasted_iota(jnp.int32, both.shape, 1) < 64
    later = time_rolled(both, -1)
    even = jnp.where(left, both, pltpu.roll(later, 64, 1))
    odd = jnp.where(left, pltpu.roll(both, 64, 1), later)
    return even.astype(jnp.bfloat16), odd.astype(jnp.bfloat16)


def correlated(patches, block, words):
    lhs = [
        jnp.concatenate(
            [block(row + down, col + right) for down in (0, 1) for right in (0, 1)], axis=1
        )
        for row, col in patches
    ]
    return jnp.dot(jnp.concatenate(lhs, axis=0), words[...], preferred_element_type=jnp.float32)


def group_codes(patches, block, words, words_back, sums, not_top, not_left):
    found = shrink_codes(correlated(patches, block, words))
    pieces = [found[64 * number : 64 * number + 64] for number in range(len(patches))]
    masked = []
    for (row, col), piece in zip(patches, pieces):
        piece = piece * not_top if row < 0 else piece
        masked.append((piece * not_left if col < 0 else piece).astype(jnp.bfloat16))
    given = jnp.dot(
        jnp.concatenate(masked, axis=0), words_back[...], preferred_element_type=jnp.float32
    )
    for number, (row, col) in enumerate(patches):
        for down in (0, 1):
            for right in (0, 1):
                spot = (row + down, col + right)
                if 0 <= spot[0] <= 4 and 0 <= spot[1] <= 4:
                    at = 128 * (2 * down + right)
                    part = given[64 * number : 64 * number + 64, at : at + 128]
                    sums[spot] = sums[spot] + part if spot in sums else part
    return dict(zip(patches, pieces))


def first_codes(each, patches, block, words, words_back, sums, not_top=1.0, not_left=1.0):
    found = {}
    for at in range(0, len(patches), each):
        group = patches[at : at + each]
        found.update(group_codes(group, block, words, words_back, sums, not_top, not_left))
    return found


def last_codes(before, column, block, words):
    patches = [(row, column) for row in range(4)]
    found = jnp.concatenate(before, axis=0) + correlated(patches, block, words)
    return shrink_codes(found).reshape(4, 64, 512)


outer_spot = {-1: 0, 4: 1, 5: 2}
late_first = ((3, 0), (3, 1), (3, 2), (0, 3), (1, 3), (2, 3))


def chosen(pair, odd_pairs, even_pairs):
    odd_device = lax.rem(lax.axis_index("xline"), 2) == 1
    if pair in (-1, 0):
        return lambda row: jnp.where(odd_device, even_pairs[row], odd_pairs[row]).astype(jnp.float32)
    return lambda row: jnp.where(odd_device, odd_pairs[row], even_pairs[row]).astype(jnp.float32)


def edge_masks():
    inline_at, xline_at = lax.axis_index("inline"), lax.axis_index("xline")
    at_edge = (
        inline_at == 0,
        inline_at == lax.axis_size("inline") - 1,
        xline_at == 0,
        xline_at == lax.axis_size("xline") - 1,
    )
    return [jnp.where(edge, 0.0, 1.0) for edge in at_edge]


def rebuilt_half(given, odd):
    moved = pltpu.roll(given, 64, 1)
    return moved + time_rolled(given, 1) if odd else given + time_rolled(moved, 1)


def widened_half(block, odd):
    left = lax.broadcasted_iota(jnp.int32, block.shape, 1) < 64
    later = time_rolled(block, -1)
    if odd:
        return jnp.where(left, pltpu.roll(block, 64, 1), later).astype(jnp.bfloat16)
    return jnp.where(left, block, pltpu.roll(later, 64, 1)).astype(jnp.bfloat16)


def inner_kernel(half, words, words_back, field, first, recon):
    for pair in range(2):
        for row in range(4):
            even, odd = widened(half[pair, row].astype(jnp.float32))
            field[2 * pair, row] = even
            field[2 * pair + 1, row] = odd
    sums = {}
    patches = [(row, col) for col in range(3) for row in range(3)]
    found = first_codes(6, patches, lambda row, col: field[col, row], words, words_back, sums)
    for (row, col), piece in found.items():
        first[col, row] = piece
    for (row, col), part in sums.items():
        recon[col, row] = part


def side_kernel(
    side_odd, side_even, edge_odd, edge_even, whole, inner, first_inner, recon_inner, words, words_back,
    field_edge, field_side, first, recon, rests, later, made_codes
):
    not_top, not_bottom, not_left, not_right = edge_masks()
    for pair in range(2):
        load = chosen(pair, edge_odd, edge_even)
        for number in range(3):
            even, odd = widened(load(number))
            field_edge[2 * pair, number] = even
            field_edge[2 * pair + 1, number] = odd
    left, right = chosen(-1, side_odd, side_even), chosen(2, side_odd, side_even)
    for row in range(4):
        field_side[0, row] = widened(left(row) * not_left)[1]
        even, odd = widened(right(row) * not_right)
        field_side[1, row] = even
        field_side[2, row] = odd

    def block(row, col):
        if 0 <= col <= 3:
            return inner[col, row] if 0 <= row <= 3 else field_edge[col, outer_spot[row]]
        return field_side[outer_spot[col], row]

    sums = {(row, col): recon_inner[col, row] for row in range(4) for col in range(4)}
    patches = [(row, col) for col in range(3) for row in (-1, 3, 4)]
    patches += [(row, col) for col in (-1, 3, 4) for row in range(3)]
    found = first_codes(6, patches, block, words, words_back, sums, not_top, not_left)
    for number, spot in enumerate(late_first):
        first[number] = found[spot]
    for number, col in enumerate((0, 3, 4)):
        for row in range(5):
            if (row, col) != (4, 4):
                recon[number, row] = sums[row, col]
    for col in (1, 2):
        pair, odd = col // 2, col % 2
        load = chosen(pair, edge_odd, edge_even)
        for row in range(5):
            rebuilt = rebuilt_half(sums[row, col], odd)
            if row < 4:
                rest = whole[row, pair] - rebuilt
                rests[col - 1, row] = rest
            else:
                rest = (load(1) - rebuilt) * not_bottom
            later[col - 1, row] = widened_half(rest, odd)
    before = [first_inner[1, row] for row in range(3)] + [found[3, 1]]
    made_codes[...] = last_codes(before, 1, lambda row, col: later[col - 1, row], words)


def sparse_kernel(
    corner_odd, corner_even, side_odd, side_even, edge_odd, edge_even, whole, inner, field_edge, field_side,
    first_inner, first_side, recon_side, rests, later_inner, codes_inner, words, words_back,
    codes, residual, field_corner, later, turned, binned, made_codes, flat_rest, leave
):
    stores = [pltpu.make_async_copy(codes_inner, codes.at[:, 1], leave.at[0])]
    stores[0].start()
    not_top, not_bottom, not_left, not_right = edge_masks()

    def leaving(column, made):
        number = len(stores)
        made_codes[number - 1] = made
        for part in range(2 if column == 3 else 1):
            rows = pl.ds(2 * part, 2) if column == 3 else pl.ds(0, 4)
            stores.append(
                pltpu.make_async_copy(
                    made_codes.at[number - 1, rows], codes.at[rows, column], leave.at[len(stores)]
                )
            )
            stores[-1].start()

    left, right = chosen(-1, corner_odd, corner_even), chosen(2, corner_odd, corner_even)
    for number in range(3):
        field_corner[0, number] = widened(left(number) * not_left)[1]
        even, odd = widened(right(number) * not_right)
        field_corner[1, number] = even
        field_corner[2, number] = odd

    def block(row, col):
        if 0 <= col <= 3:
            return inner[col, row] if 0 <= row <= 3 else field_edge[col, outer_spot[row]]
        if 0 <= row <= 3:
            return field_side[outer_spot[col], row]
        return field_corner[outer_spot[col], outer_spot[row]]

    sums = {
        (row, col): recon_side[number, row]
        for number, col in enumerate((0, 3, 4))
        for row in range(5)
        if (row, col) != (4, 4)
    }
    patches = [(row, col) for col in (-1, 3, 4) for row in (-1, 3, 4)]
    found = first_codes(3, patches, block, words, words_back, sums, not_top, not_left)

    late_spot = {0: 0, 3: 1, 4: 2}

    def rest_of(col):
        pair, odd = col // 2, col % 2
        for row in range(5):
            rebuilt = rebuilt_half(sums[row, col], odd)
            if col == 4:
                source = chosen(2, side_odd, side_even)(row) if row < 4 else right(1)
                rest = (source - rebuilt) * not_right
            elif row < 4:
                rest = whole[row, pair] - rebuilt
                binned[pair, row] = rest
            else:
                rest = chosen(pair, edge_odd, edge_even)(1) - rebuilt
            if row == 4:
                rest = rest * not_bottom
            later[late_spot[col], row] = widened_half(rest, odd)

    def rest_block(row, col):
        if col in (1, 2):
            return later_inner[col - 1, row]
        return later[late_spot[col], row]

    def before(col):
        if col == 3:
            return [first_side[3 + row] for row in range(3)] + [found[3, 3]]
        return [first_inner[col, row] for row in range(3)] + [first_side[col]]

    rest_of(0)
    rest_of(3)
    rest_of(4)
    for column in (0, 2, 3):
        leaving(column, last_codes(before(column), column, rest_block, words))

    left = lax.broadcasted_iota(jnp.int32, (64, 128), 1) < 64
    for block_row in range(4):
        binned[0, block_row] = jnp.where(left, binned[0, block_row], rests[0, block_row])
        binned[1, block_row] = jnp.where(left, rests[1, block_row], binned[1, block_row])
    for tile in range(2):
        blocks = [binned[pair, 2 * tile + part] for part in range(2) for pair in range(2)]
        for phase, made in enumerate(exchanged(blocks)):
            turned[tile, pl.ds(phase, 64, stride=4), :] = made
    for tile in range(2):
        flat = jnp.transpose(turned[tile])
        for number in range(8):
            odd, part, pair = number // 4, (number // 2) % 2, number % 2
            for row in range(4):
                at = number * 16 + row * 4
                to = (2 * tile + part) * 64 + row * 16 + (2 * pair + odd) * 4
                flat_rest[to : to + 4, :] = flat[at : at + 4, :]
    stores.append(pltpu.make_async_copy(flat_rest, residual, leave.at[5]))
    stores[-1].start()
    for store in stores:
        store.wait()


def body(
    base_volume, vintage_traces, dest_device, dest_slot, vintage_id, vintage_gains, dictionary
):
    trace_count, time_len = vintage_traces.shape
    device_count = lax.axis_size("inline") * lax.axis_size("xline")
    send_rows = device_count * 17
    sent = call_kernel(
        pack_kernel,
        jax.ShapeDtypeStruct((send_rows, 128), jnp.int32),
        pltpu.HBM,
        [
            pltpu.SMEM(vintage_gains.shape, jnp.float32),
            pltpu.VMEM(vintage_traces.shape, jnp.float32),
            pltpu.VMEM((1, trace_count), jnp.int32),
            pltpu.VMEM((1, trace_count), jnp.int32),
            pltpu.VMEM((1, trace_count), jnp.int32),
            pltpu.VMEM((send_rows, 128), jnp.int32),
            pltpu.VMEM((trace_count, 128), jnp.int32),
            pltpu.VMEM((1, trace_count), jnp.int32),
            pltpu.SMEM((1, trace_count), jnp.int32),
            pltpu.SemaphoreType.DMA((6,)),
            pltpu.SemaphoreType.DMA,
        ],
        pltpu.HBM,
        [
            pltpu.with_memory_space_constraint(array, pltpu.HBM)
            for array in (
                vintage_gains,
                vintage_traces,
                dest_device.reshape(1, trace_count),
                dest_slot.reshape(1, trace_count),
                vintage_id.reshape(1, trace_count),
            )
        ],
    )
    got = lax.all_to_all(
        sent.reshape(send_rows, 1, 128), ("inline", "xline"), split_axis=0, concat_axis=0, tiled=True
    ).reshape(send_rows, 128)
    full_shape = lambda *shape: jax.ShapeDtypeStruct(shape, jnp.float32)
    pair_shape = lambda *lead: jax.ShapeDtypeStruct(lead + (64, 128), jnp.bfloat16)
    to_odd, to_even, side_odd, side_even, half, whole = call_kernel(
        merge_kernel,
        (
            pair_shape(2, 2),
            pair_shape(2, 2),
            pair_shape(4),
            pair_shape(4),
            pair_shape(2, 4),
            full_shape(4, 2, 64, 128),
        ),
        (pltpu.VMEM,) * 6,
        [pltpu.VMEM((2, 256, 128), jnp.float32), pltpu.VMEM((256, time_len), jnp.float32)],
        pltpu.VMEM,
        [got, base_volume.reshape(256, time_len)],
    )
    half, dictionary = lax.optimization_barrier((half, dictionary))
    words = dictionary.reshape(2, 4, 2, 4, 2, 4, 512).transpose(0, 2, 4, 5, 1, 3, 6).reshape(512, 512)
    words_back = words.T
    words = words * jnp.bfloat16(step_size)

    rows, columns = lax.axis_size("inline"), lax.axis_size("xline")

    def swapped(block, along_rows, odd_pairs):
        route = []
        for row in range(rows):
            for column in range(columns):
                at, count = (row, rows) if along_rows else (column, columns)
                to = at + 1 if at % 2 == odd_pairs else at - 1
                if not 0 <= to < count:
                    partner = (row, column ^ 1) if along_rows else (row ^ 1, column)
                else:
                    partner = (to, column) if along_rows else (row, to)
                route.append((row * columns + column, partner[0] * columns + partner[1]))
        return lax.ppermute(block, ("inline", "xline"), route)

    from_odd = swapped(to_odd, True, 1)
    from_even = swapped(to_even, True, 0)
    side_odd = swapped(side_odd, False, 1)
    side_even = swapped(side_even, False, 0)
    inner, first_inner, recon_inner = call_kernel(
        inner_kernel,
        (pair_shape(4, 4), full_shape(3, 3, 64, 512), full_shape(4, 4, 64, 128)),
        (pltpu.VMEM,) * 3,
        [],
        pltpu.VMEM,
        [half, words, words_back],
        cost=pl.CostEstimate(flops=600_000_000, bytes_accessed=2_000_000, transcendentals=0),
    )
    edge_odd, edge_even = call_kernel(
        assemble_kernel,
        (pair_shape(3), pair_shape(3)),
        (pltpu.VMEM,) * 2,
        [],
        pltpu.VMEM,
        [from_odd, from_even],
    )
    corner_odd = swapped(edge_odd, False, 1)
    corner_even = swapped(edge_even, False, 0)
    field_edge, field_side, first_side, recon_side, rests, later, codes_inner = call_kernel(
        side_kernel,
        (
            pair_shape(4, 3),
            pair_shape(3, 4),
            full_shape(6, 64, 512),
            full_shape(3, 5, 64, 128),
            full_shape(2, 4, 64, 128),
            pair_shape(2, 5),
            full_shape(4, 64, 512),
        ),
        (pltpu.VMEM,) * 7,
        [],
        pltpu.VMEM,
        [
            side_odd, side_even, edge_odd, edge_even, whole, inner, first_inner, recon_inner, words,
            words_back,
        ],
        cost=pl.CostEstimate(flops=1_400_000_000, bytes_accessed=4_000_000, transcendentals=0),
    )
    codes, residual = call_kernel(
        sparse_kernel,
        (full_shape(4, 4, 64, 512), full_shape(256, time_len)),
        (pltpu.HBM, pltpu.HBM),
        [
            pltpu.VMEM((3, 3, 64, 128), jnp.bfloat16),
            pltpu.VMEM((3, 5, 64, 128), jnp.bfloat16),
            pltpu.VMEM((2, 256, 128), jnp.float32),
            pltpu.VMEM((2, 4, 64, 128), jnp.float32),
            pltpu.VMEM((3, 4, 64, 512), jnp.float32),
            pltpu.VMEM((256, time_len), jnp.float32),
            pltpu.SemaphoreType.DMA((6,)),
        ],
        pltpu.VMEM,
        [
            corner_odd, corner_even, side_odd, side_even, edge_odd, edge_even, whole, inner, field_edge,
            field_side, first_inner, first_side, recon_side, rests, later, codes_inner, words, words_back,
        ],
    )
    return codes, residual.reshape(16, 16, time_len)


def solution(mesh):
    in_specs = (
        P("inline", "xline", None),
        P(("inline", "xline"), None),
        P(("inline", "xline"), None),
        P(("inline", "xline")),
        P(("inline", "xline")),
        P(),
        P(),
    )
    out_specs = (P("inline", "xline", None, None), P("inline", "xline", None))
    return jax.shard_map(body, mesh=mesh, in_specs=in_specs, out_specs=out_specs, check_vma=False)
```

```python
import math

import jax
import jax.numpy as jnp
from jax import lax
from jax.experimental import pallas as pl
from jax.experimental.pallas import tpu as pltpu
from jax.sharding import PartitionSpec as P

step_size = 0.25
threshold = 0.02
octaves = 40.0
code_top = 32767.0
log_top = math.log2(12.0)
vmem_bytes = 48 * 1024 * 1024


def shrink_codes(values):
    return values - jnp.clip(values, -threshold, threshold)


def call_kernel(kernel, out_shape, out_spaces, scratch, in_space, inputs, vmem_limit=vmem_bytes, cost=None):
    return pl.pallas_call(
        kernel,
        out_shape=out_shape,
        in_specs=[pl.BlockSpec(memory_space=in_space)] * len(inputs),
        out_specs=jax.tree.map(lambda space: pl.BlockSpec(memory_space=space), out_spaces),
        scratch_shapes=scratch,
        cost_estimate=cost,
        compiler_params=pltpu.CompilerParams(vmem_limit_bytes=vmem_limit),
    )(*inputs)


def encode(values):
    size = jnp.log2(jnp.maximum(jnp.abs(values), 1e-30))
    code = (size + (octaves - log_top)) * (code_top / octaves)
    code = jnp.clip(jnp.round(code), 0.0, code_top).astype(jnp.int32)
    return jnp.where(values < 0, -code, code)


def decode(code):
    code = code.astype(jnp.float32)
    size = jnp.exp2(jnp.abs(code) * (octaves / code_top) + (log_top - octaves))
    return size * jnp.clip(code, -1.0, 1.0)


def pack_kernel(gains_in, traces_in, dest_in, slot_in, vid_in, built, gains, traces, dest, slot, vid, words, place, place_at, arrive):
    loads = [
        pltpu.make_async_copy(source, target, arrive.at[number])
        for number, (source, target) in enumerate(
            ((dest_in, dest), (slot_in, slot), (gains_in, gains), (vid_in, vid), (traces_in, traces))
        )
    ]
    for load in loads:
        load.start()
    trace_count = traces.shape[0]
    device_count = built.shape[0] // 17
    built[...] = jnp.zeros_like(built)
    chunks = trace_count // 128
    me = lax.axis_index("inline") * lax.axis_size("xline") + lax.axis_index("xline")
    loads[0].wait()
    loads[1].wait()
    row = lax.broadcasted_iota(jnp.int32, (128, 128), 0)
    lane = lax.broadcasted_iota(jnp.int32, (128, 128), 1)
    before = jnp.where(row < lane, 1.0, 0.0).astype(jnp.bfloat16)
    carry = jnp.zeros((device_count, 1), jnp.float32)
    places, owners, listed = [], [], []
    for chunk in range(chunks):
        target = dest[:, chunk * 128 : chunk * 128 + 128]
        hit = jnp.where(row == target, 1.0, 0.0)
        hit_half = hit.astype(jnp.bfloat16)
        earlier = jnp.dot(hit_half, before, preferred_element_type=jnp.float32)
        rank = jnp.sum(hit * (earlier + carry), axis=0, keepdims=True)
        carry = carry + jnp.sum(hit, axis=1, keepdims=True)
        rank = rank.astype(jnp.int32)
        places.append(target * 17 + rank)
        owners.append(hit_half)
        wanted = (slot[:, chunk * 128 : chunk * 128 + 128] + 1).astype(jnp.float32)
        spot = lax.rem(17 * me + rank, 128)
        listed.append(jnp.where(row == spot, wanted, 0.0).astype(jnp.bfloat16))
    place[...] = jnp.concatenate(places, axis=1)
    put = pltpu.make_async_copy(place, place_at, arrive.at[5])
    put.start()
    owner = jnp.concatenate(owners, axis=1)
    listing = jnp.concatenate(listed, axis=1)
    slots = lax.dot_general(
        owner, listing, (((1,), (1,)), ((), ())), preferred_element_type=jnp.float32
    ).astype(jnp.int32)

    loads[2].wait()
    loads[3].wait()
    survey = vid[...]
    gain = jnp.zeros(survey.shape, jnp.float32)
    for number in range(gains.shape[0]):
        gain = jnp.where(survey == number, gains[number], gain)
    gain = jnp.transpose(jnp.broadcast_to(gain, (128, trace_count)))
    loads[4].wait()
    code = [encode(traces[:, half * 128 : half * 128 + 128] * gain) for half in range(2)]
    words[...] = (code[0] << 16) | (code[1] & 65535)
    built[pl.ds(16, device_count, stride=17), :] = slots
    put.wait()
    for trace in range(trace_count):
        built[pl.ds(place_at[0, trace], 1), :] = words[trace : trace + 1, :]


def exchanged(four):
    lane = lax.broadcasted_iota(jnp.int32, four[0].shape, 1)

    def crossed(lower, upper, distance):
        keep = (lane // distance) % 2 == 0
        return (
            jnp.where(keep, lower, pltpu.roll(upper, distance, 1)),
            jnp.where(keep, pltpu.roll(lower, 128 - distance, 1), upper),
        )

    (zero, two), (one, three) = crossed(four[0], four[2], 32), crossed(four[1], four[3], 32)
    (zero, one), (two, three) = crossed(zero, one, 16), crossed(two, three, 16)
    return zero, one, two, three


def merge_kernel(got, base, to_odd, to_even, side_odd, side_even, half, whole, turned, ordered):
    tiles = got.shape[0] // 128
    for number in range(64):
        tile, odd, part, pair = number // 32, number // 16 % 2, number // 8 % 2, number // 4 % 2
        at = (4 * (2 * tile + part) + number % 4) * 16 + 4 * (2 * pair + odd)
        ordered[4 * number : 4 * number + 4, :] = base[at : at + 4, :]
    bin_row = lax.broadcasted_iota(jnp.int32, (256, 128), 0)
    tile, part, pair, odd = bin_row // 128, (bin_row // 32) % 2, (bin_row // 16) % 2, (bin_row // 64) % 2
    block_row, block_col = 2 * tile + part, 2 * pair + odd
    bin_slot = block_row * 64 + ((bin_row // 4) % 4) * 16 + block_col * 4 + bin_row % 4
    wanted = bin_slot + 1
    listed = got[pl.ds(16, 128, stride=17), :]
    begin = 17 * lax.broadcasted_iota(jnp.int32, (128, 128), 0)
    lane = lax.broadcasted_iota(jnp.int32, (128, 128), 1)
    tile_of = begin // 128 + jnp.where(lane < begin % 128, 1, 0)
    tiles_each = 2
    fold = jnp.zeros((256, 128), jnp.float32)
    stack = jnp.zeros((256, 256), jnp.float32)
    for at in range(0, tiles, tiles_each):
        hits, rows, rests = [], [], []
        for tile in range(at, min(at + tiles_each, tiles)):
            low_group, high_group = (128 * tile) // 136, min((128 * tile + 127) // 136, 15)
            spot = slice(8 * low_group, 8 * high_group + 8)
            slots = jnp.sum(jnp.where(tile_of[spot] == tile, listed[spot], 0), axis=0, keepdims=True)
            hit = jnp.where(wanted == slots, 1.0, 0.0)
            fold = fold + hit
            hits.append(hit.astype(jnp.bfloat16))
            word = got[128 * tile : 128 * tile + 128, :]
            values = [decode(code) for code in (word >> 16, (word << 16) >> 16)]
            high = [value.astype(jnp.bfloat16) for value in values]
            low = [
                (value - part.astype(jnp.float32)).astype(jnp.bfloat16)
                for value, part in zip(values, high)
            ]
            rows.append(jnp.concatenate(high, axis=1))
            rests.append(jnp.concatenate(low, axis=1))
        stack = stack + jnp.dot(
            jnp.concatenate(hits + hits, axis=1),
            jnp.concatenate(rows + rests, axis=0),
            preferred_element_type=jnp.float32,
        )
    fold = jnp.sum(fold, axis=1, keepdims=True)
    merged = (ordered[...] + stack) / (1.0 + fold)
    turned[0] = jnp.transpose(merged[:128])
    turned[1] = jnp.transpose(merged[128:])
    for tile in range(2):
        slabs = [turned[tile, pl.ds(phase, 64, stride=4), :] for phase in range(4)]
        for number, made in enumerate(exchanged(slabs)):
            part, pair = number // 2, number % 2
            whole[2 * tile + part, pair] = made
            half[pair, 2 * tile + part] = made.astype(jnp.bfloat16)
    odd_device = lax.rem(lax.axis_index("inline"), 2)
    to_even[...] = half[:, pl.ds(2 - 2 * odd_device, 2)]
    to_odd[...] = half[:, pl.ds(2 * odd_device, 2)]
    odd_device = lax.rem(lax.axis_index("xline"), 2)
    side_even[...] = half[1 - odd_device]
    side_odd[...] = half[odd_device]


def assemble_kernel(from_odd, from_even, to_odd, to_even):
    inline_at = lax.axis_index("inline")
    odd_row = lax.rem(inline_at, 2) == 1
    odd_col = lax.rem(lax.axis_index("xline"), 2)
    last = inline_at == lax.axis_size("inline") - 1
    for target, pair in ((to_even, 1 - odd_col), (to_odd, odd_col)):
        above = jnp.where(odd_row, from_even[pair, 1], from_odd[pair, 1])
        target[0] = jnp.where(inline_at == 0, jnp.zeros_like(above), above)
        below = jnp.where(odd_row, from_odd[pair], from_even[pair])
        target[1:3] = jnp.where(last, jnp.zeros_like(below), below)


def time_rolled(values, distance):
    row = lax.broadcasted_iota(jnp.int32, values.shape, 0)
    if distance < 0:
        return jnp.where(row == values.shape[0] - 1, 0.0, pltpu.roll(values, values.shape[0] - 1, 0))
    return jnp.where(row == 0, 0.0, pltpu.roll(values, 1, 0))


def widened(both):
    left = lax.broadcasted_iota(jnp.int32, both.shape, 1) < 64
    later = time_rolled(both, -1)
    even = jnp.where(left, both, pltpu.roll(later, 64, 1))
    odd = jnp.where(left, pltpu.roll(both, 64, 1), later)
    return even.astype(jnp.bfloat16), odd.astype(jnp.bfloat16)


def correlated(patches, block, words):
    lhs = [
        jnp.concatenate(
            [block(row + down, col + right) for down in (0, 1) for right in (0, 1)], axis=1
        )
        for row, col in patches
    ]
    return jnp.dot(jnp.concatenate(lhs, axis=0), words[...], preferred_element_type=jnp.float32)


def group_codes(patches, block, words, words_back, sums, not_top, not_left):
    found = shrink_codes(correlated(patches, block, words))
    pieces = [found[64 * number : 64 * number + 64] for number in range(len(patches))]
    masked = []
    for (row, col), piece in zip(patches, pieces):
        piece = piece * not_top if row < 0 else piece
        masked.append((piece * not_left if col < 0 else piece).astype(jnp.bfloat16))
    given = jnp.dot(
        jnp.concatenate(masked, axis=0), words_back[...], preferred_element_type=jnp.float32
    )
    for number, (row, col) in enumerate(patches):
        for down in (0, 1):
            for right in (0, 1):
                spot = (row + down, col + right)
                if 0 <= spot[0] <= 4 and 0 <= spot[1] <= 4:
                    at = 128 * (2 * down + right)
                    part = given[64 * number : 64 * number + 64, at : at + 128]
                    sums[spot] = sums[spot] + part if spot in sums else part
    return dict(zip(patches, pieces))


def first_codes(each, patches, block, words, words_back, sums, not_top=1.0, not_left=1.0):
    found = {}
    for at in range(0, len(patches), each):
        group = patches[at : at + each]
        found.update(group_codes(group, block, words, words_back, sums, not_top, not_left))
    return found


def last_codes(before, column, block, words):
    patches = [(row, column) for row in range(4)]
    found = jnp.concatenate(before, axis=0) + correlated(patches, block, words)
    return shrink_codes(found).reshape(4, 64, 512)


outer_spot = {-1: 0, 4: 1, 5: 2}
late_first = ((3, 0), (3, 1), (3, 2), (0, 3), (1, 3), (2, 3))


def chosen(pair, odd_pairs, even_pairs):
    odd_device = lax.rem(lax.axis_index("xline"), 2) == 1
    if pair in (-1, 0):
        return lambda row: jnp.where(odd_device, even_pairs[row], odd_pairs[row]).astype(jnp.float32)
    return lambda row: jnp.where(odd_device, odd_pairs[row], even_pairs[row]).astype(jnp.float32)


def edge_masks():
    inline_at, xline_at = lax.axis_index("inline"), lax.axis_index("xline")
    at_edge = (
        inline_at == 0,
        inline_at == lax.axis_size("inline") - 1,
        xline_at == 0,
        xline_at == lax.axis_size("xline") - 1,
    )
    return [jnp.where(edge, 0.0, 1.0) for edge in at_edge]


def rebuilt_half(given, odd):
    moved = pltpu.roll(given, 64, 1)
    return moved + time_rolled(given, 1) if odd else given + time_rolled(moved, 1)


def widened_half(block, odd):
    left = lax.broadcasted_iota(jnp.int32, block.shape, 1) < 64
    later = time_rolled(block, -1)
    if odd:
        return jnp.where(left, pltpu.roll(block, 64, 1), later).astype(jnp.bfloat16)
    return jnp.where(left, block, pltpu.roll(later, 64, 1)).astype(jnp.bfloat16)


def inner_kernel(half, words, words_back, field, first, recon):
    for pair in range(2):
        for row in range(4):
            even, odd = widened(half[pair, row].astype(jnp.float32))
            field[2 * pair, row] = even
            field[2 * pair + 1, row] = odd
    sums = {}
    patches = [(row, col) for col in range(3) for row in range(3)]
    found = first_codes(6, patches, lambda row, col: field[col, row], words, words_back, sums)
    for (row, col), piece in found.items():
        first[col, row] = piece
    for (row, col), part in sums.items():
        recon[col, row] = part


def side_kernel(
    side_odd, side_even, edge_odd, edge_even, whole, inner, first_inner, recon_inner, words, words_back,
    field_edge, field_side, first, recon, rests, later, made_codes
):
    not_top, not_bottom, not_left, not_right = edge_masks()
    for pair in range(2):
        load = chosen(pair, edge_odd, edge_even)
        for number in range(3):
            even, odd = widened(load(number))
            field_edge[2 * pair, number] = even
            field_edge[2 * pair + 1, number] = odd
    left, right = chosen(-1, side_odd, side_even), chosen(2, side_odd, side_even)
    for row in range(4):
        field_side[0, row] = widened(left(row) * not_left)[1]
        even, odd = widened(right(row) * not_right)
        field_side[1, row] = even
        field_side[2, row] = odd

    def block(row, col):
        if 0 <= col <= 3:
            return inner[col, row] if 0 <= row <= 3 else field_edge[col, outer_spot[row]]
        return field_side[outer_spot[col], row]

    sums = {(row, col): recon_inner[col, row] for row in range(4) for col in range(4)}
    patches = [(row, col) for col in range(3) for row in (-1, 3, 4)]
    patches += [(row, col) for col in (-1, 3, 4) for row in range(3)]
    found = first_codes(6, patches, block, words, words_back, sums, not_top, not_left)
    for number, spot in enumerate(late_first):
        first[number] = found[spot]
    for number, col in enumerate((0, 3, 4)):
        for row in range(5):
            if (row, col) != (4, 4):
                recon[number, row] = sums[row, col]
    for col in (1, 2):
        pair, odd = col // 2, col % 2
        load = chosen(pair, edge_odd, edge_even)
        for row in range(5):
            rebuilt = rebuilt_half(sums[row, col], odd)
            if row < 4:
                rest = whole[row, pair] - rebuilt
                rests[col - 1, row] = rest
            else:
                rest = (load(1) - rebuilt) * not_bottom
            later[col - 1, row] = widened_half(rest, odd)
    before = [first_inner[1, row] for row in range(3)] + [found[3, 1]]
    made_codes[...] = last_codes(before, 1, lambda row, col: later[col - 1, row], words)


def sparse_kernel(
    corner_odd, corner_even, side_odd, side_even, edge_odd, edge_even, whole, inner, field_edge, field_side,
    first_inner, first_side, recon_side, rests, later_inner, codes_inner, words, words_back,
    codes, residual, field_corner, later, turned, binned, made_codes, flat_rest, leave
):
    stores = [pltpu.make_async_copy(codes_inner, codes.at[:, 1], leave.at[0])]
    stores[0].start()
    not_top, not_bottom, not_left, not_right = edge_masks()

    def leaving(column, made):
        number = len(stores)
        made_codes[number - 1] = made
        for part in range(2 if column == 3 else 1):
            rows = pl.ds(2 * part, 2) if column == 3 else pl.ds(0, 4)
            stores.append(
                pltpu.make_async_copy(
                    made_codes.at[number - 1, rows], codes.at[rows, column], leave.at[len(stores)]
                )
            )
            stores[-1].start()

    left, right = chosen(-1, corner_odd, corner_even), chosen(2, corner_odd, corner_even)
    for number in range(3):
        field_corner[0, number] = widened(left(number) * not_left)[1]
        even, odd = widened(right(number) * not_right)
        field_corner[1, number] = even
        field_corner[2, number] = odd

    def block(row, col):
        if 0 <= col <= 3:
            return inner[col, row] if 0 <= row <= 3 else field_edge[col, outer_spot[row]]
        if 0 <= row <= 3:
            return field_side[outer_spot[col], row]
        return field_corner[outer_spot[col], outer_spot[row]]

    sums = {
        (row, col): recon_side[number, row]
        for number, col in enumerate((0, 3, 4))
        for row in range(5)
        if (row, col) != (4, 4)
    }
    patches = [(row, col) for col in (-1, 3, 4) for row in (-1, 3, 4)]
    found = first_codes(3, patches, block, words, words_back, sums, not_top, not_left)

    late_spot = {0: 0, 3: 1, 4: 2}

    def rest_of(col):
        pair, odd = col // 2, col % 2
        for row in range(5):
            rebuilt = rebuilt_half(sums[row, col], odd)
            if col == 4:
                source = chosen(2, side_odd, side_even)(row) if row < 4 else right(1)
                rest = (source - rebuilt) * not_right
            elif row < 4:
                rest = whole[row, pair] - rebuilt
                binned[pair, row] = rest
            else:
                rest = chosen(pair, edge_odd, edge_even)(1) - rebuilt
            if row == 4:
                rest = rest * not_bottom
            later[late_spot[col], row] = widened_half(rest, odd)

    def rest_block(row, col):
        if col in (1, 2):
            return later_inner[col - 1, row]
        return later[late_spot[col], row]

    def before(col):
        if col == 3:
            return [first_side[3 + row] for row in range(3)] + [found[3, 3]]
        return [first_inner[col, row] for row in range(3)] + [first_side[col]]

    rest_of(0)
    rest_of(3)
    rest_of(4)
    for column in (0, 2, 3):
        leaving(column, last_codes(before(column), column, rest_block, words))

    left = lax.broadcasted_iota(jnp.int32, (64, 128), 1) < 64
    for block_row in range(4):
        binned[0, block_row] = jnp.where(left, binned[0, block_row], rests[0, block_row])
        binned[1, block_row] = jnp.where(left, rests[1, block_row], binned[1, block_row])
    for tile in range(2):
        blocks = [binned[pair, 2 * tile + part] for part in range(2) for pair in range(2)]
        for phase, made in enumerate(exchanged(blocks)):
            turned[tile, pl.ds(phase, 64, stride=4), :] = made
    for tile in range(2):
        flat = jnp.transpose(turned[tile])
        for number in range(8):
            odd, part, pair = number // 4, (number // 2) % 2, number % 2
            for row in range(4):
                at = number * 16 + row * 4
                to = (2 * tile + part) * 64 + row * 16 + (2 * pair + odd) * 4
                flat_rest[to : to + 4, :] = flat[at : at + 4, :]
    stores.append(pltpu.make_async_copy(flat_rest, residual, leave.at[5]))
    stores[-1].start()
    for store in stores:
        store.wait()


def body(
    base_volume, vintage_traces, dest_device, dest_slot, vintage_id, vintage_gains, dictionary
):
    trace_count, time_len = vintage_traces.shape
    device_count = lax.axis_size("inline") * lax.axis_size("xline")
    send_rows = device_count * 17
    sent = call_kernel(
        pack_kernel,
        jax.ShapeDtypeStruct((send_rows, 128), jnp.int32),
        pltpu.VMEM,
        [
            pltpu.SMEM(vintage_gains.shape, jnp.float32),
            pltpu.VMEM(vintage_traces.shape, jnp.float32),
            pltpu.VMEM((1, trace_count), jnp.int32),
            pltpu.VMEM((1, trace_count), jnp.int32),
            pltpu.VMEM((1, trace_count), jnp.int32),
            pltpu.VMEM((trace_count, 128), jnp.int32),
            pltpu.VMEM((1, trace_count), jnp.int32),
            pltpu.SMEM((1, trace_count), jnp.int32),
            pltpu.SemaphoreType.DMA((6,)),
        ],
        pltpu.HBM,
        [
            pltpu.with_memory_space_constraint(array, pltpu.HBM)
            for array in (
                vintage_gains,
                vintage_traces,
                dest_device.reshape(1, trace_count),
                dest_slot.reshape(1, trace_count),
                vintage_id.reshape(1, trace_count),
            )
        ],
    )
    got = lax.all_to_all(
        sent.reshape(send_rows, 1, 128), ("inline", "xline"), split_axis=0, concat_axis=0, tiled=True
    ).reshape(send_rows, 128)
    full_shape = lambda *shape: jax.ShapeDtypeStruct(shape, jnp.float32)
    pair_shape = lambda *lead: jax.ShapeDtypeStruct(lead + (64, 128), jnp.bfloat16)
    to_odd, to_even, side_odd, side_even, half, whole = call_kernel(
        merge_kernel,
        (
            pair_shape(2, 2),
            pair_shape(2, 2),
            pair_shape(4),
            pair_shape(4),
            pair_shape(2, 4),
            full_shape(4, 2, 64, 128),
        ),
        (pltpu.VMEM,) * 6,
        [pltpu.VMEM((2, 256, 128), jnp.float32), pltpu.VMEM((256, time_len), jnp.float32)],
        pltpu.VMEM,
        [got, base_volume.reshape(256, time_len)],
    )
    half, dictionary = lax.optimization_barrier((half, dictionary))
    words = dictionary.reshape(2, 4, 2, 4, 2, 4, 512).transpose(0, 2, 4, 5, 1, 3, 6).reshape(512, 512)
    words_back = words.T
    words = words * jnp.bfloat16(step_size)

    rows, columns = lax.axis_size("inline"), lax.axis_size("xline")

    def swapped(block, along_rows, odd_pairs):
        route = []
        for row in range(rows):
            for column in range(columns):
                at, count = (row, rows) if along_rows else (column, columns)
                to = at + 1 if at % 2 == odd_pairs else at - 1
                if not 0 <= to < count:
                    partner = (row, column ^ 1) if along_rows else (row ^ 1, column)
                else:
                    partner = (to, column) if along_rows else (row, to)
                route.append((row * columns + column, partner[0] * columns + partner[1]))
        return lax.ppermute(block, ("inline", "xline"), route)

    from_odd = swapped(to_odd, True, 1)
    from_even = swapped(to_even, True, 0)
    side_odd = swapped(side_odd, False, 1)
    side_even = swapped(side_even, False, 0)
    inner, first_inner, recon_inner = call_kernel(
        inner_kernel,
        (pair_shape(4, 4), full_shape(3, 3, 64, 512), full_shape(4, 4, 64, 128)),
        (pltpu.VMEM,) * 3,
        [],
        pltpu.VMEM,
        [half, words, words_back],
        cost=pl.CostEstimate(flops=600_000_000, bytes_accessed=2_000_000, transcendentals=0),
    )
    edge_odd, edge_even = call_kernel(
        assemble_kernel,
        (pair_shape(3), pair_shape(3)),
        (pltpu.VMEM,) * 2,
        [],
        pltpu.VMEM,
        [from_odd, from_even],
    )
    corner_odd = swapped(edge_odd, False, 1)
    corner_even = swapped(edge_even, False, 0)
    field_edge, field_side, first_side, recon_side, rests, later, codes_inner = call_kernel(
        side_kernel,
        (
            pair_shape(4, 3),
            pair_shape(3, 4),
            full_shape(6, 64, 512),
            full_shape(3, 5, 64, 128),
            full_shape(2, 4, 64, 128),
            pair_shape(2, 5),
            full_shape(4, 64, 512),
        ),
        (pltpu.VMEM,) * 7,
        [],
        pltpu.VMEM,
        [
            side_odd, side_even, edge_odd, edge_even, whole, inner, first_inner, recon_inner, words,
            words_back,
        ],
        cost=pl.CostEstimate(flops=1_400_000_000, bytes_accessed=4_000_000, transcendentals=0),
    )
    codes, residual = call_kernel(
        sparse_kernel,
        (full_shape(4, 4, 64, 512), full_shape(256, time_len)),
        (pltpu.HBM, pltpu.HBM),
        [
            pltpu.VMEM((3, 3, 64, 128), jnp.bfloat16),
            pltpu.VMEM((3, 5, 64, 128), jnp.bfloat16),
            pltpu.VMEM((2, 256, 128), jnp.float32),
            pltpu.VMEM((2, 4, 64, 128), jnp.float32),
            pltpu.VMEM((3, 4, 64, 512), jnp.float32),
            pltpu.VMEM((256, time_len), jnp.float32),
            pltpu.SemaphoreType.DMA((6,)),
        ],
        pltpu.VMEM,
        [
            corner_odd, corner_even, side_odd, side_even, edge_odd, edge_even, whole, inner, field_edge,
            field_side, first_inner, first_side, recon_side, rests, later, codes_inner, words, words_back,
        ],
    )
    return codes, residual.reshape(16, 16, time_len)


def solution(mesh):
    in_specs = (
        P("inline", "xline", None),
        P(("inline", "xline"), None),
        P(("inline", "xline"), None),
        P(("inline", "xline")),
        P(("inline", "xline")),
        P(),
        P(),
    )
    out_specs = (P("inline", "xline", None, None), P("inline", "xline", None))
    return jax.shard_map(body, mesh=mesh, in_specs=in_specs, out_specs=out_specs, check_vma=False)
```
